32 devices in a mesh: section: 2 (over core), seq: 4 (over z), mp: 4 (over y, x).
Axes of the slice: x: 2, y: 2, z: 4, core: 2. Of those that a mesh axis runs over, the one named last changes fastest.
Arguments:
- enc_rows: bfloat16 [2, 768, 1536], P('section', 'seq'), may hold values from -6 to 6
- vis_index: int32 [2, 768], P('section', 'seq'), may hold values from 0 to 8639, as said below
- owner_of: int32 [8640], replicated, may hold values from 0 to 3, as said below
- enc_gain: bfloat16 [1536], replicated, may hold values from 0.5 to 1.5
- embed_weight: bfloat16 [1536, 768], P('section'), may hold values from -0.15625 to 0.15625
- mask_token: bfloat16 [768], replicated, may hold values from -4 to 4
- attn_gain: bfloat16 [768], replicated, may hold values from 0.5 to 1.5
- qkv_weight: bfloat16 [768, 3, 768], P('section', None, 'mp')
- out_weight: bfloat16 [768, 768], P('mp', 'section'), may hold values from -0.21875 to 0.21875
- mlp_gain: bfloat16 [768], replicated, may hold values from 0.5 to 1.5
- up_weight: bfloat16 [768, 3072], P('section', 'mp'), may hold values from -0.21875 to 0.21875
- down_weight: bfloat16 [3072, 768], P('mp', 'section'), may hold values from -0.109375 to 0.109375
Outputs:
- decoded: float32 [2, 8640, 768], P('section', 'seq')
The draws below stay inside these ranges and needn't reach their ends.
Inputs may be any that keep to these rules, and one draw needn't show every extreme that they name: `vis_index`: each volume's row names 768 different patches. `owner_of`: each owner owns exactly 2160 patches.
All inputs are finite; a program needn't handle non-finite values.
Results may differ from the reference program's by a relative error of at most 0.012.
Values may be sent and summed in bfloat16 or wider, within the bound.
No kernel may reach another device: no remote copies, remote signals or barrier semaphores. Data moves between devices by JAX's collectives and lax.ppermute only.
A program may use at most 320 MiB of HBM per device.

```python
import jax
import jax.numpy as jnp
from jax import lax

GX = 6
P_SIZE = 8640
PAT_DEV = 2160
VIS = 768
VOLS = 2
E = 1536
DD = 768
HEADS = 12
HD = 64
DFF = 3072


def draw_vis_index(key, part):
    volume_keys = jax.random.split(key, VOLS)

    def shuffled(single_key):
        return jax.random.permutation(single_key, P_SIZE)
    return jax.vmap(shuffled)(volume_keys)[:, :VIS].astype(jnp.int32)


def draw_owner_of(key, part):
    return (jax.random.permutation(key, P_SIZE) // PAT_DEV).astype(jnp.int32)


def draw_qkv_weight(key, part):
    weights_drawn = jax.random.normal(key, (DD, 3, DD), jnp.float32) * DD ** (-0.5)
    query_part = weights_drawn[:, 0, :] * 4.0
    key_part = weights_drawn[:, 1, :]
    weights_drawn = jnp.stack([query_part, key_part, weights_drawn[:, 2, :]], axis=1)
    return weights_drawn.astype(jnp.bfloat16)


def shard_levels(rng, extent, cuts, smallest, top_value):
    def one(axis_at, shards_of):
        heights = jax.random.uniform(jax.random.fold_in(jax.random.fold_in(rng, 6), axis_at), (shards_of,), jnp.float32, smallest / len(cuts), top_value / len(cuts))
        return jnp.repeat(jnp.exp(heights), extent[axis_at] // shards_of).reshape((-1,) + (1,) * (len(extent) - axis_at - 1))

    loudness = one(*cuts[0])
    for cut in cuts[1:]:
        loudness = loudness * one(*cut)
    return loudness


def normal_values(stream_key, dims, width, limit, cuts=(), kind=jnp.bfloat16):
    values = width * jax.random.normal(stream_key, dims, jnp.float32)
    if cuts:
        values = values * shard_levels(stream_key, dims, cuts, -0.22, 0.18)
    return jnp.clip(values, -limit, limit).astype(kind)


def setup_inputs(seed: int = 0) -> dict:
    splits = jax.random.split(jax.random.key(seed), 13)
    return {
        "enc_rows": normal_values(splits[0], (VOLS, VIS, E), 1.0, 6.0, ((0, 2), (1, 4))),
        "vis_index": draw_vis_index(jax.random.fold_in(splits[12], 71), 0),
        "owner_of": draw_owner_of(jax.random.fold_in(splits[12], 71), 0),
        "enc_gain": jnp.clip(1.0 + 0.1 * jax.random.normal(splits[3], (E,), jnp.float32), 0.5, 1.5).astype(jnp.bfloat16),
        "embed_weight": normal_values(splits[4], (E, DD), E ** -0.5, 0.15625, ((0, 2),)),
        "mask_token": normal_values(splits[5], (DD,), 1.0, 4.0),
        "attn_gain": jnp.clip(1.0 + 0.1 * jax.random.normal(splits[6], (DD,), jnp.float32), 0.5, 1.5).astype(jnp.bfloat16),
        "qkv_weight": draw_qkv_weight(jax.random.fold_in(splits[12], 71), 0),
        "out_weight": normal_values(splits[8], (DD, DD), DD ** -0.5, 0.21875, ((0, 4), (1, 2))),
        "mlp_gain": jnp.clip(1.0 + 0.1 * jax.random.normal(splits[9], (DD,), jnp.float32), 0.5, 1.5).astype(jnp.bfloat16),
        "up_weight": normal_values(splits[10], (DD, DFF), DD ** -0.5, 0.21875, ((0, 2), (1, 4))),
        "down_weight": normal_values(splits[11], (DFF, DD), DFF ** -0.5, 0.109375, ((0, 4), (1, 2))),
    }


def place_codes(patches, features):
    half_width = features // 8
    coordinates = jnp.stack([patches % GX, patches // GX % GX, patches // (GX * GX) % GX, patches // (GX * GX * GX)], axis=1).astype(jnp.float32)
    frequency = 1.0 / 10000.0 ** (jnp.arange(half_width, dtype=jnp.float32) / half_width)
    angles = coordinates[:, :, None] * frequency[None, None, :]
    return jnp.concatenate([jnp.sin(angles), jnp.cos(angles)], axis=2).reshape(patches.shape[0], features)

def layer_norm(values, scales):
    centred = values - lax.optimization_barrier(jnp.mean(values, axis=-1, keepdims=True))
    spread = lax.optimization_barrier(jnp.mean(centred * centred, axis=-1, keepdims=True))
    return centred * lax.rsqrt(spread + 1e-06) * scales.astype(jnp.float32)

def reference(enc_rows, vis_index, owner_of, enc_gain, embed_weight, mask_token, attn_gain, qkv_weight, out_weight, mlp_gain, up_weight, down_weight):
    owner_order = jnp.argsort(owner_of, stable=True).astype(jnp.int32)
    slot_of = jnp.zeros((P_SIZE,), jnp.int32).at[owner_order].set(jnp.arange(P_SIZE, dtype=jnp.int32))
    place_rows = place_codes(owner_order, DD)
    mask_row = mask_token.astype(jnp.float32)
    query_rows = GX * GX * GX
    outputs = []
    for volume in range(VOLS):
        normed_enc = layer_norm(enc_rows[volume].astype(jnp.float32), enc_gain).astype(jnp.bfloat16)
        embedded = jnp.dot(normed_enc, embed_weight, preferred_element_type=jnp.float32).astype(jnp.bfloat16)
        embedded = lax.optimization_barrier(embedded)
        visible_slots = slot_of[vis_index[volume]]
        start_rows = jnp.broadcast_to(mask_row[None, :], (P_SIZE, DD)).at[visible_slots].set(embedded.astype(jnp.float32))
        stream = start_rows + place_rows
        attn_in = layer_norm(stream, attn_gain).astype(jnp.bfloat16)
        projected = jnp.dot(attn_in, qkv_weight.reshape(DD, 3 * DD), preferred_element_type=jnp.float32).astype(jnp.bfloat16)
        projected = lax.optimization_barrier(projected).reshape(P_SIZE, 3, HEADS, HD)
        key_heads = projected[:, 1].astype(jnp.float32)
        value_heads = projected[:, 2].astype(jnp.float32)
        query_blocks = projected[:, 0].reshape(P_SIZE // query_rows, query_rows, HEADS, HD)

        def attend_block(query_block):
            scores = jnp.einsum('qhd,khd->hqk', query_block.astype(jnp.float32), key_heads) * HD ** (-0.5)
            row_peak = lax.optimization_barrier(jnp.max(scores, axis=-1, keepdims=True))
            exponent = jnp.exp(scores - row_peak)
            totals = lax.optimization_barrier(jnp.sum(exponent, axis=-1))
            weights = lax.optimization_barrier(exponent.astype(jnp.bfloat16))
            context = jnp.einsum('hqk,khd->hqd', weights.astype(jnp.float32), value_heads) / totals[:, :, None]
            return jnp.transpose(context, (1, 0, 2)).reshape(query_rows, DD).astype(jnp.bfloat16)
        context = lax.map(attend_block, query_blocks).reshape(P_SIZE, DD)
        middle = stream + jnp.dot(context, out_weight, preferred_element_type=jnp.float32)
        mlp_in = layer_norm(middle, mlp_gain).astype(jnp.bfloat16)
        hidden = jax.nn.gelu(jnp.dot(mlp_in, up_weight, preferred_element_type=jnp.float32), approximate=False).astype(jnp.bfloat16)
        outputs.append(middle + jnp.dot(hidden, down_weight, preferred_element_type=jnp.float32))
    return jnp.stack(outputs, axis=0)
```

```python
import functools
import math

import jax
import jax.numpy as jnp
import numpy as np
from jax import lax
from jax.experimental import pallas as pl
from jax.experimental.pallas import tpu as pltpu
from jax.sharding import PartitionSpec as P

GX = 6
HD = 64
LANES = 128
KEY_BLOCK = 1024
KEY_PAD = 256
OFF_BIAS = -1e30
HEADROOM = 88.0
WINDOW = 180.0
CUBE = GX * GX * GX
HIGH = lax.Precision.HIGHEST
BF = jnp.bfloat16
F32 = jnp.float32
I32 = jnp.int32
VMEM_LIMIT = 56 * 1024 * 1024
LOG_SCALE = math.log2(math.e) * HD ** (-0.5)
NT = (((1,), (1,)), ((), ()))
PARAMS = pltpu.CompilerParams(vmem_limit_bytes=VMEM_LIMIT)


def layer_norm(values, scales):
    centred = values - jnp.mean(values, axis=-1, keepdims=True)
    spread = jnp.mean(centred * centred, axis=-1, keepdims=True)
    return centred * lax.rsqrt(spread + 1e-06) * scales


def dot32(a, b):
    return jnp.dot(a, b, preferred_element_type=F32)


def split3(values):
    high = values.astype(BF)
    rest = values - high.astype(F32)
    mid = rest.astype(BF)
    return high, mid, (rest - mid.astype(F32)).astype(BF)


def split2(values):
    high = values.astype(BF)
    return high, (values - high.astype(F32)).astype(BF)


def shifted(values, axis, step):
    size = lax.axis_size(axis)
    return lax.ppermute(values, axis, [(i, (i + step) % size) for i in range(size)])


def shift_pieces(values, axis):
    return [values] + [shifted(values, axis, step) for step in range(1, lax.axis_size(axis))]


def gather_rows(values, axis):
    if lax.axis_size(axis) > 4:
        return lax.all_gather(values, axis, axis=0, tiled=True)
    return jnp.concatenate(shift_pieces(values, axis), axis=0)


def whole(array):
    return pl.BlockSpec(array.shape, lambda *_: (0,) * array.ndim)


SMEM = pl.BlockSpec(memory_space=pltpu.SMEM)


def place_table(slabs, features):
    quarter = features // 4
    frequency = (1.0 / 10000.0 ** (np.arange(quarter // 2, dtype=np.float32) / (quarter // 2))).astype(np.float32)
    angles = np.arange(max(slabs, GX), dtype=np.float32)[:, None] * frequency[None, :]
    codes = np.concatenate([np.sin(angles), np.cos(angles)], axis=1).astype(np.float32)
    place = np.arange(CUBE)
    cube = np.concatenate(
        [codes[place % GX], codes[place // GX % GX], codes[place // (GX * GX)], np.zeros((CUBE, quarter), np.float32)],
        axis=1,
    )
    slab = np.concatenate([np.zeros((slabs, 3 * quarter), np.float32), codes[:slabs]], axis=1)
    return np.concatenate([cube, slab], axis=0)


def embed_kernel(section_ref, rows_ref, gain_ref, mine_ref, other_ref, out_ref):
    normed = layer_norm(rows_ref[...].astype(F32), gain_ref[...].astype(F32)).astype(BF)
    half = normed.shape[1] // 2
    low, high = normed[:, :half], normed[:, half:]
    first = section_ref[0] == 0

    @pl.when(first)
    def _():
        out_ref[...] = (dot32(low, mine_ref[...]) + dot32(high, other_ref[...])).astype(BF)

    @pl.when(jnp.logical_not(first))
    def _():
        out_ref[...] = (dot32(low, other_ref[...]) + dot32(high, mine_ref[...])).astype(BF)


def table_kernel(
    groups, section_ref, table_ref, mask_ref, gain_ref, mine_ref, other_ref, weight_ref, proj_ref, sum_ref, square_ref
):
    features = table_ref.shape[1]
    places = table_ref.shape[0]
    first = section_ref[0] == 0
    mine, other = mine_ref[...], other_ref[...]
    full = jnp.concatenate([jnp.where(first, mine, other), jnp.where(first, other, mine)], axis=0)
    gain = gain_ref[...].astype(F32)
    mask = mask_ref[...].astype(F32)
    mask = mask - jnp.mean(mask, axis=1, keepdims=True)
    table = table_ref[...]
    row = lax.broadcasted_iota(I32, table.shape, 0)
    lane = lax.broadcasted_iota(I32, table.shape, 1)
    rows = table + jnp.where(row < CUBE, mask, 0.0)
    gained = jnp.concatenate([rows * gain, jnp.broadcast_to(gain, (16, features))], axis=0)
    proj = sum(dot32(part, full) for part in split3(gained))
    last = lane >= features - features // 4
    squared = jnp.where(row < CUBE, jnp.where(last, 0.0, rows), jnp.where(last, rows + mask, 0.0))
    total = jnp.sum(rows, axis=1, keepdims=True)
    square = jnp.sum(squared * squared, axis=1, keepdims=True)
    column = lax.broadcasted_iota(I32, (1, groups * HD), 1)
    scale = jnp.where(column < groups * HD // 3, LOG_SCALE, 1.0)
    proj = (proj[:places, :] - (total / features) * proj[places : places + 1, :]) * scale
    for group in range(groups):
        span = slice(group * HD, (group + 1) * HD)
        wide = slice(group * LANES, (group + 1) * LANES)
        weight_ref[:, wide] = jnp.concatenate([full[:, span], jnp.zeros((features, HD), BF)], axis=1)
        proj_ref[:, wide] = jnp.concatenate([proj[:, span], jnp.zeros((places, HD), F32)], axis=1)
    sum_ref[...] = jnp.broadcast_to(total / features, sum_ref.shape)
    square_ref[...] = jnp.broadcast_to(square / features, square_ref.shape)


def top_rows(values):
    return jnp.max(values.reshape(values.shape[0] // 8, 8, LANES), axis=0)


def square_sums(values):
    return dot32((values * values).astype(BF), jnp.ones((LANES, LANES), BF))


def masked_kernel(heads, patch_total, proj_ref, sum_ref, square_ref, ids_ref, km_ref, vm_ref, top_ref, shown):
    step = pl.program_id(0)
    parts = km_ref.shape[1] // CUBE
    slabs = patch_total // CUBE
    lane = lax.broadcasted_iota(I32, (1, LANES), 1)

    @pl.when(step == 0)
    def _():
        ids = ids_ref[...]
        slab = ids // CUBE
        inner = ids - slab * CUBE
        rows = lax.broadcasted_iota(I32, (CUBE, ids.shape[1]), 0)
        columns = lax.broadcasted_iota(I32, (LANES, ids.shape[1]), 0)
        by_place = jnp.where(rows == inner, 1.0, 0.0).astype(BF)
        by_slab = jnp.where(columns == slab, 1.0, 0.0).astype(BF)
        shown[...] = lax.dot_general(by_place, by_slab, NT, preferred_element_type=F32).astype(BF)
        cross = lambda a, b: lax.dot_general(a, b, NT, precision=HIGH, preferred_element_type=F32)
        share = jnp.full((CUBE, LANES), 1.0 / LANES, F32)
        mean = sum_ref[:CUBE, 0:1] + cross(share, sum_ref[CUBE:, :])
        spread = square_ref[:CUBE, 0:1] + cross(share, square_ref[CUBE:, :]) - mean * mean
        scale = lax.rsqrt(spread + 1e-06)
        largest = lambda x: jnp.max(jnp.max(x, axis=0, keepdims=True), axis=1, keepdims=True)
        key_top = jnp.zeros((1, 1), F32)
        value_top = jnp.zeros((1, 1), F32)
        for head in range(heads):
            wide = slice((heads + head) * LANES, (heads + head + 1) * LANES)
            inner, outer = proj_ref[:CUBE, wide], proj_ref[CUBE:, wide]
            norm = jnp.sum(inner * inner, axis=1, keepdims=True) + cross(jnp.ones((CUBE, LANES), F32), outer * outer)
            norm = (norm + 2.0 * cross(inner, outer)) * scale * scale
            key_top = jnp.maximum(key_top, largest(norm))
            wide = slice((2 * heads + head) * LANES, (2 * heads + head + 1) * LANES)
            value_top = jnp.maximum(value_top, largest(jnp.abs(proj_ref[:CUBE, wide])) + largest(jnp.abs(proj_ref[CUBE:, wide])))
        top_ref[:8, :] = jnp.broadcast_to(key_top, (8, LANES))
        top_ref[8:, :] = jnp.broadcast_to(value_top * largest(scale), (8, LANES))

    value_extra = jnp.where(lane >= HD, 1.0, 0.0)
    scales = []
    extras = []
    slab_rows = []
    for part in range(parts):
        slab = step * parts + part
        row = CUBE + jnp.minimum(slab, slabs - 1)
        slab_rows.append(proj_ref[pl.ds(row, 1), :])
        mean = sum_ref[:CUBE, :] + sum_ref[pl.ds(row, 1), :]
        spread = square_ref[:CUBE, :] + square_ref[pl.ds(row, 1), :] - mean * mean
        scales.append(lax.rsqrt(spread + 1e-06))
        pick = (lax.broadcasted_iota(I32, (LANES, LANES), 0) == slab) & (
            lax.broadcasted_iota(I32, (LANES, LANES), 1) == HD
        )
        key_extra = dot32(shown[...], jnp.where(pick, OFF_BIAS, 0.0).astype(BF))
        constant = jnp.where((lane > HD) & (lane < HD + 4), 1.0, jnp.where((lane == HD) & (slab >= slabs), OFF_BIAS, 0.0))
        extras.append(key_extra + constant)
    scale = jnp.concatenate(scales, axis=0)
    key_extra = jnp.concatenate(extras, axis=0)
    for head in range(heads):
        for first, extra, target in ((heads, key_extra, km_ref), (2 * heads, value_extra, vm_ref)):
            wide = slice((first + head) * LANES, (first + head + 1) * LANES)
            block = jnp.concatenate([proj_ref[:CUBE, wide] + row[:, wide] for row in slab_rows], axis=0)
            target[head] = (block * scale + extra).astype(BF)


def owned_kernel(seq_ref, owner_ref, ids_ref):
    groups, size = owner_ref.shape
    rows = ids_ref.shape[0]
    flags = jnp.where(owner_ref[...] == seq_ref[0], 1.0, 0.0).astype(BF)

    def upper(count):
        shape = (count, count)
        return jnp.where(lax.broadcasted_iota(I32, shape, 0) <= lax.broadcasted_iota(I32, shape, 1), 1.0, 0.0).astype(BF)

    local = dot32(flags, upper(size))
    totals = lax.dot_general(jnp.ones((8, size), BF), flags, NT, preferred_element_type=F32)
    ends = dot32(totals.astype(BF), upper(groups))
    begins = (ends - totals)[0:1, :]
    ends = ends[0:1, :]
    slot = lax.broadcasted_iota(I32, (rows, 1), 0).astype(F32)
    group = jnp.sum(jnp.where(ends <= slot, 1.0, 0.0), axis=1, keepdims=True)
    lane = lax.broadcasted_iota(I32, (rows, groups), 1).astype(F32)
    hot = jnp.where(lane == group, 1.0, 0.0)
    begin = jnp.sum(hot * begins, axis=1, keepdims=True)
    counts = dot32(hot.astype(BF), local.astype(BF))
    within = jnp.sum(jnp.where(counts <= slot - begin, 1.0, 0.0), axis=1, keepdims=True)
    ids_ref[...] = (group * size + within).astype(I32)


def place_hot(ids, places):
    lane = lax.broadcasted_iota(I32, (ids.shape[0], places), 1)
    slab = ids // CUBE
    inner = ids - slab * CUBE
    return jnp.where((lane == inner) | (lane == slab + CUBE), 1.0, 0.0).astype(BF)


def queries_kernel(
    heads, rows_ref, idc_ref, idr_ref, own_ref, table_ref, gain_ref, weight_ref, proj_ref, sum_ref, square_ref, top_ref,
    kv_ref, vv_ref, q_ref, seen_q, bounds, tables,
):
    step = pl.program_id(0)
    wide = heads * LANES

    @pl.when(step == 0)
    def _():
        count = rows_ref.shape[0]
        hot = place_hot(idc_ref[...], table_ref.shape[0])
        place = sum(dot32(hot, part) for part in split2(table_ref[...]))
        seen = layer_norm(rows_ref[...].astype(F32) + place, gain_ref[...].astype(F32)).astype(BF)
        seen_q[...] = (dot32(seen, weight_ref[:, :wide]) * LOG_SCALE).astype(BF)
        lane = lax.broadcasted_iota(I32, (1, LANES), 1)
        extra = jnp.where((lane > HD) & (lane < HD + 4), 1.0, 0.0)
        ones = jnp.where(lane >= HD, 1.0, 0.0)
        top = top_ref[:8, :]
        high = top_ref[8:, :]
        spare = kv_ref.shape[1] - count
        for head in range(heads):
            first = (heads + head) * LANES
            keys = dot32(seen, weight_ref[:, first : first + LANES])
            top = jnp.maximum(top, top_rows(square_sums(keys)))
            middle = jnp.mean(keys, axis=0, keepdims=True)
            middle = jnp.sum(middle * middle, axis=1, keepdims=True)
            bounds[head : head + 1, :] = jnp.broadcast_to(jnp.sqrt(middle) * 1.03, (1, LANES))
            kv_ref[head, :count, :] = (keys + extra).astype(BF)
            first = (2 * heads + head) * LANES
            values = dot32(seen, weight_ref[:, first : first + LANES])
            high = jnp.maximum(high, top_rows(jnp.abs(values)))
            vv_ref[head, :count, :] = (values + ones).astype(BF)
            if spare:
                off = lax.broadcasted_iota(I32, (spare, LANES), 1) == HD
                kv_ref[head, count:, :] = jnp.where(off, OFF_BIAS, 0.0).astype(BF)
                vv_ref[head, count:, :] = jnp.ones((spare, LANES), BF)
        bounds[heads : heads + 1, :] = jnp.sqrt(jnp.max(top, axis=0, keepdims=True)) * 1.03
        largest = jnp.max(jnp.max(high, axis=0, keepdims=True), axis=1, keepdims=True)
        bounds[heads + 1 : heads + 2, :] = jnp.broadcast_to(largest, (1, LANES))
        joined = jnp.concatenate([proj_ref[:, :wide], sum_ref[...], square_ref[...]], axis=1)
        for i, part in enumerate(split2(joined)):
            tables[i] = part

    @pl.when(step > 0)
    def _():
        ids = own_ref[...]
        count = ids.shape[0]
        hot = place_hot(ids, table_ref.shape[0])
        mixed = dot32(hot, tables[0]) + dot32(hot, tables[1])
        mean = mixed[:, wide : wide + LANES]
        scale = lax.rsqrt(mixed[:, wide + LANES :] - mean * mean + 1e-06)
        match = jnp.where(ids == idr_ref[...], 1.0, 0.0)
        shown = jnp.max(match, axis=1, keepdims=True) > 0.5
        picked = dot32(match.astype(BF), seen_q[...])
        lane = lax.broadcasted_iota(I32, (count, LANES), 1)
        limit = bounds[heads : heads + 1, :]
        fine = bounds[heads + 1 : heads + 2, :] < 2.0**25
        for head in range(heads):
            span = slice(head * LANES, (head + 1) * LANES)
            part = jnp.where(shown, picked[:, span], scale * mixed[:, span])
            norm = jnp.sqrt(square_sums(part))
            ceiling = norm * limit
            slack = jnp.where(fine, ceiling + norm * bounds[head : head + 1, :], 1e30)
            extra = jnp.where(lane == HD, 1.0, jnp.where(lane == HD + 1, HEADROOM - ceiling, 0.0))
            extra = jnp.where(lane == HD + 4, slack, extra)
            q_ref[head] = jnp.where(lane < HD, part, extra).astype(BF)


def attend_kernel(offset, rows, q_ref, km_ref, vm_ref, kv_ref, vv_ref, out_ref, q_scr, acc, ctx, p_even, p_odd):
    head = pl.program_id(0)
    q_scr[...] = q_ref[0, offset : offset + rows, :]
    block = p_even.shape[1]
    steps = km_ref.shape[1] // block
    rest = km_ref.shape[1] - steps * block
    tails = [(km_ref, vm_ref, steps * block, rest)] if rest else []
    visible = kv_ref.shape[1]
    tails += [(kv_ref, vv_ref, i, min(block, visible - i)) for i in range(0, visible, block)]

    def keys_of(i):
        if isinstance(i, int) and i >= steps:
            keys, _, start, size = tails[i - steps]
            return keys[0, start : start + size, :]
        return km_ref[0, pl.ds(i * block, block), :]

    def values_of(i):
        if isinstance(i, int) and i >= steps:
            _, values, start, size = tails[i - steps]
            return values[0, start : start + size, :]
        return vm_ref[0, pl.ds(i * block, block), :]

    def scores(i):
        return lax.dot_general(q_scr[...], keys_of(i), NT, preferred_element_type=F32)

    total = steps + len(tails)
    lane = lax.broadcasted_iota(I32, (rows, LANES), 1)
    slack = jnp.max(jnp.where(lane == HD + 4, q_scr[...].astype(F32), -1e30))

    @pl.when(jnp.logical_not(slack <= WINDOW))
    def _():
        q_scr[...] = jnp.where(lane > HD, 0.0, q_scr[...].astype(F32)).astype(BF)

        def look(i, best):
            return jnp.maximum(best, jnp.max(scores(i), axis=1, keepdims=True))

        peak = lax.fori_loop(0, steps, look, jnp.full((rows, 1), -3e38, F32))
        for i in range(steps, total):
            peak = look(i, peak)
        high, mid, low = split3(peak)
        new = jnp.where(lane == HD + 1, -high.astype(F32), q_scr[...].astype(F32))
        new = jnp.where(lane == HD + 2, -mid.astype(F32), new)
        new = jnp.where(lane == HD + 3, -low.astype(F32), new)
        q_scr[...] = new.astype(BF)

    def width_of(i):
        return tails[i - steps][3] if isinstance(i, int) and i >= steps else block

    def weigh(i, target):
        target[:, : width_of(i)] = jnp.exp2(scores(i)).astype(BF)

    def add(weights, i):
        acc[...] += dot32(weights[:, : width_of(i)], values_of(i))

    acc[...] = jnp.zeros_like(acc)
    slots = (p_even, p_odd)
    weigh(0, p_even)

    def body(j, carry):
        i = 2 * j + 1
        weigh(i, p_odd)
        add(p_even, i - 1)
        weigh(i + 1, p_even)
        add(p_odd, i)
        return carry

    pairs = (steps - 1) // 2
    lax.fori_loop(0, pairs, body, 0)
    for i in range(1 + 2 * pairs, total + 1):
        if i < total:
            weigh(i, slots[i % 2])
        add(slots[1 - i % 2], i - 1)
    totals = acc[...]
    ctx[head] = totals[:, :HD] / totals[:, HD:]

    @pl.when(head == pl.num_programs(0) - 1)
    def _():
        out_ref[...] = jnp.concatenate([ctx[i] for i in range(ctx.shape[0])], axis=1).astype(BF)


def attend(q_all, km, vm, kv, vv, offset, rows):
    heads, total, _ = q_all.shape
    masked, visible = km.shape[1], kv.shape[1]
    per_head = lambda size: pl.BlockSpec((1, size, LANES), lambda h: (h, 0, 0))
    return pl.pallas_call(
        functools.partial(attend_kernel, offset, rows),
        grid=(heads,),
        in_specs=[per_head(total), per_head(masked), per_head(masked), per_head(visible), per_head(visible)],
        out_specs=pl.BlockSpec((rows, heads * HD), lambda h: (0, 0)),
        out_shape=jax.ShapeDtypeStruct((rows, heads * HD), BF),
        scratch_shapes=[
            pltpu.VMEM((rows, LANES), BF),
            pltpu.VMEM((rows, LANES), F32),
            pltpu.VMEM((heads, rows, HD), F32),
            pltpu.VMEM((rows, KEY_BLOCK), BF),
            pltpu.VMEM((rows, KEY_BLOCK), BF),
        ],
        compiler_params=PARAMS,
        cost_estimate=pl.CostEstimate(
            flops=8 * heads * rows * (masked + visible) * LANES,
            bytes_accessed=4 * heads * masked * LANES,
            transcendentals=heads * rows * masked,
        ),
        name="attend",
    )(q_all, km, vm, kv, vv)


def mlp_kernel(pieces, share, priors, scalars, *refs):
    ctx_refs, refs = refs[:pieces], refs[pieces:]
    own_ref, idr_ref, rows_ref, table_ref, mask_ref, gain_ref = refs[:6]
    earlier, refs = refs[6 : 6 + priors], refs[6 + priors :]
    weights, refs = refs[: 2 * pieces], refs[2 * pieces :]
    res_ref, ups, downs, outs, acc, mlp_in, sems = refs[:7]
    stages = refs[7:]
    step = pl.program_id(0)
    half = weights[0].shape[1]
    up = ups.shape[2]
    tail = up + downs.shape[1]
    first = scalars[0]
    swap = lambda a: jnp.where(first == 0, a, jnp.concatenate([a[:, half:], a[:, :half]], axis=1))

    def out_copy(i):
        side = slice(i % 2 * half, (i % 2 + 1) * half)
        return pltpu.make_async_copy(weights[i].at[tail:], outs.at[i // 2, :, side], sems.at[i, 0])

    def copies(i):
        side = slice(i % 2 * half, (i % 2 + 1) * half)
        moves = [
            pltpu.make_async_copy(
                weights[i].at[k * half : (k + 1) * half],
                ups.at[i // 2, side, k * half : (k + 1) * half],
                sems.at[i, 1 + k],
            )
            for k in range(up // half)
        ]
        last = sems.at[i, 1 + up // half]
        return moves + [pltpu.make_async_copy(weights[i].at[up:tail], downs.at[i // 2, :, side], last)]

    def stored(k):
        count = earlier[k].shape[0]
        place = pl.ds(pl.multiple_of(scalars[1 + k], 16), count)
        return pltpu.make_async_copy(stages[k], res_ref.at[place], sems.at[2 * pieces + 1 + k, 0])

    @pl.when(step == 0)
    def _():
        for i in range(2 * pieces):
            out_copy(i).start()
        for i in range(2 * pieces):
            for copy in copies(i):
                copy.start()
        ids = own_ref[...]
        hot = place_hot(ids, table_ref.shape[0])
        place = sum(dot32(hot, part) for part in split2(table_ref[...]))
        match = jnp.where(ids == idr_ref[...], 1.0, 0.0)
        shown = jnp.max(match, axis=1, keepdims=True) > 0.5
        stream = jnp.where(shown, dot32(match.astype(BF), rows_ref[...]), mask_ref[...].astype(F32)) + place
        acc[...] = swap(stream)
        for i in range(pieces):
            out_copy(2 * i).wait()
            out_copy(2 * i + 1).wait()
            acc[...] += dot32(ctx_refs[i][...], outs[i])
        mlp_in[...] = layer_norm(acc[...], swap(gain_ref[...].astype(F32))).astype(BF)

    for i in range(pieces):

        @pl.when(step == i)
        def _(i=i):
            for copy in copies(2 * i) + copies(2 * i + 1):
                copy.wait()
            for k in range(i, priors, pieces):
                stages[k][...] = earlier[k][...].astype(F32)
                stored(k).start()

    wide = 256 if up % 256 == 0 else up
    blocks = [slice(k, k + wide) for k in range(0, up, wide)]
    pres = [dot32(mlp_in[...], ups[step, :, span]) for span in blocks]
    added = 0.0
    for pre, span in zip(pres, blocks):
        hidden = (0.5 * pre * (1.0 + lax.erf(pre * math.sqrt(0.5)))).astype(BF)
        added += dot32(hidden, downs[step, span, :])
    acc[...] += added

    @pl.when(step == pieces - 1)
    def _():
        if not priors:
            res_ref[...] = swap(acc[...]).astype(res_ref.dtype)
        else:
            acc[...] = swap(acc[...])
            own = pltpu.make_async_copy(acc, res_ref.at[res_ref.shape[0] - share :], sems.at[2 * pieces, 0])
            own.start()
            for k in range(priors):
                stored(k).wait()
            own.wait()


def mlp(scalars, contexts, own_ids, id_row, all_rows, table, mask_row, gain_row, weights, units, priors, total, kind):
    pieces = len(weights) // 2
    share = own_ids.shape[0]
    width = all_rows.shape[1]
    ins = [*contexts, own_ids, id_row, all_rows, table, mask_row, gain_row, *priors]
    return pl.pallas_call(
        functools.partial(mlp_kernel, pieces, share, len(priors)),
        grid=(pieces,),
        in_specs=[SMEM] + [whole(a) for a in ins] + [pl.BlockSpec(memory_space=pl.ANY)] * len(weights),
        out_specs=pl.BlockSpec(memory_space=pl.ANY) if priors else pl.BlockSpec((share, width), lambda i: (0, 0)),
        out_shape=jax.ShapeDtypeStruct((total, width), kind),
        scratch_shapes=[
            pltpu.VMEM((pieces, width, units), BF),
            pltpu.VMEM((pieces, units, width), BF),
            pltpu.VMEM((pieces, contexts[0].shape[1], width), BF),
            pltpu.VMEM((share, width), F32),
            pltpu.VMEM((share, width), BF),
            pltpu.SemaphoreType.DMA((2 * pieces + 1 + len(priors), 2 + units // (width // 2))),
        ]
        + [pltpu.VMEM(p.shape, F32) for p in priors],
        compiler_params=PARAMS,
        cost_estimate=pl.CostEstimate(
            flops=30 * share * width * width, bytes_accessed=18 * width * width, transcendentals=4 * share * width
        ),
        name="mlp",
    )(scalars, *ins, *weights)


def place_kernel(pieces, scalars, *refs):
    sources, (_held, out_ref), (sems, *stages) = refs[:pieces], refs[pieces : pieces + 2], refs[pieces + 2 :]

    def move(k):
        count = sources[k].shape[0]
        place = pl.ds(pl.multiple_of(scalars[k], 16), count)
        return pltpu.make_async_copy(stages[k], out_ref.at[place], sems.at[k])

    for k in range(pieces):
        stages[k][...] = sources[k][...].astype(F32)
        move(k).start()
    for k in range(pieces):
        move(k).wait()


def put_rows(decoded, pieces, places):
    count = len(pieces)
    return pl.pallas_call(
        functools.partial(place_kernel, count),
        in_specs=[SMEM] + [pl.BlockSpec(memory_space=pltpu.VMEM)] * count + [pl.BlockSpec(memory_space=pl.ANY)],
        out_specs=pl.BlockSpec(memory_space=pl.ANY),
        out_shape=jax.ShapeDtypeStruct(decoded.shape, decoded.dtype),
        scratch_shapes=[pltpu.SemaphoreType.DMA((count,))] + [pltpu.VMEM(p.shape, F32) for p in pieces],
        input_output_aliases={count + 1: 0},
        compiler_params=PARAMS,
        name="put_rows",
    )(jnp.stack(places), *pieces, decoded)


def shards(
    enc_rows,
    vis_index,
    owner_of,
    enc_gain,
    embed_weight,
    mask_token,
    attn_gain,
    qkv_weight,
    out_weight,
    mlp_gain,
    up_weight,
    down_weight,
):
    section = lax.axis_index("section")
    section_ref = section.astype(I32).reshape(1)
    mp_size = lax.axis_size("mp")
    mp_index = lax.axis_index("mp")
    patch_total = owner_of.shape[0]
    own_rows = patch_total // lax.axis_size("seq")
    features = mask_token.shape[0]
    half = features // 2
    width = qkv_weight.shape[2]
    heads = width // HD
    slabs = patch_total // CUBE
    places = CUBE + slabs
    vmem = lambda shape, kind: jax.ShapeDtypeStruct(shape, kind)

    embed_other = shifted(embed_weight, "section", 1)
    qkv_mine = qkv_weight.reshape(half, 3 * width)
    qkv_other = shifted(qkv_mine, "section", 1)
    all_ids = gather_rows(vis_index[0], "seq")
    embedded = pl.pallas_call(
        embed_kernel,
        in_specs=[SMEM] + [pl.BlockSpec(memory_space=pltpu.VMEM)] * 4,
        out_specs=pl.BlockSpec(memory_space=pltpu.VMEM),
        out_shape=vmem((enc_rows.shape[1], features), BF),
        compiler_params=PARAMS,
        name="embed",
    )(section_ref, enc_rows[0], enc_gain[None, :], embed_weight, embed_other)
    embedded, all_ids = lax.optimization_barrier((embedded, all_ids))
    all_rows = gather_rows(embedded, "seq")
    id_col = all_ids[:, None]
    id_row = all_ids[None, :]
    visible = all_ids.shape[0]

    table = jnp.asarray(place_table(slabs, features))
    mask_row = mask_token[None, :]
    gain_attn = attn_gain[None, :]
    groups = 3 * heads
    qkv_wide, proj, means, squares = pl.pallas_call(
        functools.partial(table_kernel, groups),
        in_specs=[SMEM] + [pl.BlockSpec(memory_space=pltpu.VMEM)] * 5,
        out_specs=[pl.BlockSpec(memory_space=pltpu.VMEM)] * 4,
        out_shape=[
            vmem((features, groups * LANES), BF),
            vmem((places, groups * LANES), F32),
            vmem((places, LANES), F32),
            vmem((places, LANES), F32),
        ],
        compiler_params=PARAMS,
        name="tables",
    )(section_ref, table, mask_row, gain_attn, qkv_mine, qkv_other)

    padded = patch_total + (-patch_total % KEY_PAD)
    slab_rows = 4 * CUBE
    blocks = -(-padded // slab_rows)
    ins = [proj, means, squares, id_row]
    key_spec = pl.BlockSpec((heads, slab_rows, LANES), lambda i: (0, i, 0))
    km, vm, top = pl.pallas_call(
        functools.partial(masked_kernel, heads, patch_total),
        grid=(blocks,),
        in_specs=[whole(a) for a in ins],
        out_specs=[key_spec, key_spec, pl.BlockSpec((16, LANES), lambda i: (0, 0))],
        out_shape=[vmem((heads, padded, LANES), BF)] * 2 + [vmem((16, LANES), F32)],
        scratch_shapes=[pltpu.VMEM((CUBE, LANES), BF)],
        compiler_params=PARAMS,
        name="masked",
    )(*ins)

    group = HD
    own_ids = pl.pallas_call(
        owned_kernel,
        in_specs=[SMEM, pl.BlockSpec(memory_space=pltpu.VMEM)],
        out_specs=pl.BlockSpec(memory_space=pltpu.VMEM),
        out_shape=vmem((own_rows, 1), I32),
        compiler_params=PARAMS,
        name="owned",
    )(lax.axis_index("seq").astype(I32).reshape(1), owner_of.reshape(patch_total // group, group))

    row_block = 720 if own_rows % 720 == 0 else own_rows
    spaced = visible + (-visible % KEY_PAD)
    ins = [all_rows, id_col, id_row, own_ids, table, gain_attn, qkv_wide, proj, means, squares, top]
    specs = [whole(a) for a in ins]
    specs[3] = pl.BlockSpec((row_block, 1), lambda i: (jnp.maximum(i - 1, 0), 0))
    kv, vv, q_all = pl.pallas_call(
        functools.partial(queries_kernel, heads),
        grid=(1 + own_rows // row_block,),
        in_specs=specs,
        out_specs=[pl.BlockSpec((heads, spaced, LANES), lambda i: (0, 0, 0))] * 2
        + [pl.BlockSpec((heads, row_block, LANES), lambda i: (0, jnp.maximum(i - 1, 0), 0))],
        out_shape=[vmem((heads, spaced, LANES), BF)] * 2 + [vmem((heads, own_rows, LANES), BF)],
        scratch_shapes=[
            pltpu.VMEM((visible, heads * LANES), BF),
            pltpu.VMEM((8 * (-(-(heads + 2) // 8)), LANES), F32),
            pltpu.VMEM((2, places, (heads + 2) * LANES), BF),
        ],
        compiler_params=PARAMS,
        name="queries",
    )(*ins)

    units = up_weight.shape[1]
    packed = jnp.concatenate(
        [up_weight[:, i : i + half] for i in range(0, units, half)] + [down_weight, out_weight], axis=0
    )
    packed, _unused = lax.optimization_barrier((packed, embedded))
    mine = shift_pieces(packed, "mp")

    spans = [(0, own_rows)]
    if own_rows >= 2048:
        big = 896
        spans = [(0, big), (big, big), (2 * big, own_rows - 2 * big)]
    gain_row = mlp_gain[None, :]
    weights = []

    def finish(contexts, ids, places, priors, total, kind):
        scalars = jnp.concatenate([section_ref] + [p.reshape(1) for p in places])
        return mlp(scalars, contexts, ids, id_row, all_rows, table, mask_row, gain_row, weights, units, priors, total, kind)

    exchanged = []
    shares = []
    for first, rows in spans[:-1]:
        share = rows // mp_size
        context = attend(q_all, km, vm, kv, vv, first, rows)
        if not weights:
            *mine, _unused = lax.optimization_barrier((*mine, context))
            for piece in mine:
                weights += [piece, shifted(piece, "section", 1)]
        pieces = []
        for step in range(mp_size):
            start = (mp_index + step) % mp_size * share
            part = lax.dynamic_slice_in_dim(context, start, share, axis=0)
            pieces.append(part if step == 0 else shifted(part, "mp", step))
        exchanged.append(pieces)
        shares.append(lax.dynamic_slice_in_dim(own_ids, first + mp_index * share, share, axis=0))
    if not weights:
        for piece in mine:
            weights += [piece, shifted(piece, "section", 1)]
    priors = []
    places = []

    def spread(k, result):
        first, rows = spans[k]
        at = [(first + (mp_index - step) % mp_size * (rows // mp_size)).astype(I32) for step in range(mp_size)]
        return shift_pieces(result, "mp"), at

    if exchanged:
        done = finish(exchanged[0], shares[0], [], [], shares[0].shape[0], BF)
        q_all, done = lax.optimization_barrier((q_all, done))
        priors, places = spread(0, done)
    first, rows = spans[-1]
    context = attend(q_all, km, vm, kv, vv, first, rows)
    last = shift_pieces(context, "mp")
    if not exchanged:
        return finish(last, own_ids, [], [], own_rows, F32)[None]
    shares[1], context = lax.optimization_barrier((shares[1], context))
    done = finish(exchanged[1], shares[1], [], [], shares[1].shape[0], BF)
    last[0], done = lax.optimization_barrier((last[0], done))
    late, late_places = spread(1, done)
    decoded = finish(last, own_ids[first:], places, priors, own_rows, F32)
    return put_rows(decoded, late, late_places)[None]


def solution(mesh):
    in_specs = (
        P("section", "seq", None),
        P("section", "seq"),
        P(),
        P(),
        P("section", None),
        P(),
        P(),
        P("section", None, "mp"),
        P("mp", "section"),
        P(),
        P("section", "mp"),
        P("mp", "section"),
    )
    out_specs = P("section", "seq", None)
    return jax.shard_map(shards, mesh=mesh, in_specs=in_specs, out_specs=out_specs, check_vma=False)
```

```python
import functools
import math

import jax
import jax.numpy as jnp
import numpy as np
from jax import lax
from jax.experimental import pallas as pl
from jax.experimental.pallas import tpu as pltpu
from jax.sharding import PartitionSpec as P

GX = 6
HD = 64
LANES = 128
KEY_BLOCK = 1024
KEY_PAD = 256
OFF_BIAS = -1e30
HEADROOM = 88.0
WINDOW = 180.0
CUBE = GX * GX * GX
HIGH = lax.Precision.HIGHEST
BF = jnp.bfloat16
F32 = jnp.float32
I32 = jnp.int32
VMEM_LIMIT = 56 * 1024 * 1024
LOG_SCALE = math.log2(math.e) * HD ** (-0.5)
NT = (((1,), (1,)), ((), ()))
PARAMS = pltpu.CompilerParams(vmem_limit_bytes=VMEM_LIMIT)


def layer_norm(values, scales):
    centred = values - jnp.mean(values, axis=-1, keepdims=True)
    spread = jnp.mean(centred * centred, axis=-1, keepdims=True)
    return centred * lax.rsqrt(spread + 1e-06) * scales


def dot32(a, b):
    return jnp.dot(a, b, preferred_element_type=F32)


def split3(values):
    high = values.astype(BF)
    rest = values - high.astype(F32)
    mid = rest.astype(BF)
    return high, mid, (rest - mid.astype(F32)).astype(BF)


def split2(values):
    high = values.astype(BF)
    return high, (values - high.astype(F32)).astype(BF)


def shifted(values, axis, step):
    size = lax.axis_size(axis)
    return lax.ppermute(values, axis, [(i, (i + step) % size) for i in range(size)])


def shift_pieces(values, axis):
    return [values] + [shifted(values, axis, step) for step in range(1, lax.axis_size(axis))]


def gather_rows(values, axis):
    if lax.axis_size(axis) > 4:
        return lax.all_gather(values, axis, axis=0, tiled=True)
    return jnp.concatenate(shift_pieces(values, axis), axis=0)


def whole(array):
    return pl.BlockSpec(array.shape, lambda *_: (0,) * array.ndim)


SMEM = pl.BlockSpec(memory_space=pltpu.SMEM)


def place_table(slabs, features):
    quarter = features // 4
    frequency = (1.0 / 10000.0 ** (np.arange(quarter // 2, dtype=np.float32) / (quarter // 2))).astype(np.float32)
    angles = np.arange(max(slabs, GX), dtype=np.float32)[:, None] * frequency[None, :]
    codes = np.concatenate([np.sin(angles), np.cos(angles)], axis=1).astype(np.float32)
    place = np.arange(CUBE)
    cube = np.concatenate(
        [codes[place % GX], codes[place // GX % GX], codes[place // (GX * GX)], np.zeros((CUBE, quarter), np.float32)],
        axis=1,
    )
    slab = np.concatenate([np.zeros((slabs, 3 * quarter), np.float32), codes[:slabs]], axis=1)
    return np.concatenate([cube, slab], axis=0)


def embed_kernel(section_ref, rows_ref, gain_ref, mine_ref, other_ref, out_ref):
    normed = layer_norm(rows_ref[...].astype(F32), gain_ref[...].astype(F32)).astype(BF)
    half = normed.shape[1] // 2
    low, high = normed[:, :half], normed[:, half:]
    first = section_ref[0] == 0

    @pl.when(first)
    def _():
        out_ref[...] = (dot32(low, mine_ref[...]) + dot32(high, other_ref[...])).astype(BF)

    @pl.when(jnp.logical_not(first))
    def _():
        out_ref[...] = (dot32(low, other_ref[...]) + dot32(high, mine_ref[...])).astype(BF)


def table_kernel(
    groups, section_ref, table_ref, mask_ref, gain_ref, mine_ref, other_ref, weight_ref, proj_ref, sum_ref, square_ref
):
    features = table_ref.shape[1]
    places = table_ref.shape[0]
    first = section_ref[0] == 0
    mine, other = mine_ref[...], other_ref[...]
    full = jnp.concatenate([jnp.where(first, mine, other), jnp.where(first, other, mine)], axis=0)
    gain = gain_ref[...].astype(F32)
    mask = mask_ref[...].astype(F32)
    mask = mask - jnp.mean(mask, axis=1, keepdims=True)
    table = table_ref[...]
    row = lax.broadcasted_iota(I32, table.shape, 0)
    lane = lax.broadcasted_iota(I32, table.shape, 1)
    rows = table + jnp.where(row < CUBE, mask, 0.0)
    gained = jnp.concatenate([rows * gain, jnp.broadcast_to(gain, (16, features))], axis=0)
    proj = sum(dot32(part, full) for part in split3(gained))
    last = lane >= features - features // 4
    squared = jnp.where(row < CUBE, jnp.where(last, 0.0, rows), jnp.where(last, rows + mask, 0.0))
    total = jnp.sum(rows, axis=1, keepdims=True)
    square = jnp.sum(squared * squared, axis=1, keepdims=True)
    column = lax.broadcasted_iota(I32, (1, groups * HD), 1)
    scale = jnp.where(column < groups * HD // 3, LOG_SCALE, 1.0)
    proj = (proj[:places, :] - (total / features) * proj[places : places + 1, :]) * scale
    for group in range(groups):
        span = slice(group * HD, (group + 1) * HD)
        wide = slice(group * LANES, (group + 1) * LANES)
        weight_ref[:, wide] = jnp.concatenate([full[:, span], jnp.zeros((features, HD), BF)], axis=1)
        proj_ref[:, wide] = jnp.concatenate([proj[:, span], jnp.zeros((places, HD), F32)], axis=1)
    sum_ref[...] = jnp.broadcast_to(total / features, sum_ref.shape)
    square_ref[...] = jnp.broadcast_to(square / features, square_ref.shape)


def top_rows(values):
    return jnp.max(values.reshape(values.shape[0] // 8, 8, LANES), axis=0)


def square_sums(values):
    return dot32((values * values).astype(BF), jnp.ones((LANES, LANES), BF))


def masked_kernel(heads, patch_total, proj_ref, sum_ref, square_ref, ids_ref, km_ref, vm_ref, top_ref, shown):
    step = pl.program_id(0)
    parts = km_ref.shape[1] // CUBE
    slabs = patch_total // CUBE
    lane = lax.broadcasted_iota(I32, (1, LANES), 1)

    @pl.when(step == 0)
    def _():
        ids = ids_ref[...]
        slab = ids // CUBE
        inner = ids - slab * CUBE
        rows = lax.broadcasted_iota(I32, (CUBE, ids.shape[1]), 0)
        columns = lax.broadcasted_iota(I32, (LANES, ids.shape[1]), 0)
        by_place = jnp.where(rows == inner, 1.0, 0.0).astype(BF)
        by_slab = jnp.where(columns == slab, 1.0, 0.0).astype(BF)
        shown[...] = lax.dot_general(by_place, by_slab, NT, preferred_element_type=F32).astype(BF)
        largest = lambda x: jnp.max(jnp.max(x, axis=0, keepdims=True), axis=1, keepdims=True)
        norms = lambda x: jnp.sqrt(jnp.max(jnp.sum(x * x, axis=1, keepdims=True), axis=0, keepdims=True))
        key_top = jnp.zeros((1, 1), F32)
        value_top = jnp.zeros((1, 1), F32)
        for head in range(heads):
            wide = slice((heads + head) * LANES, (heads + head + 1) * LANES)
            inner, outer = proj_ref[:CUBE, wide], proj_ref[CUBE:, wide]
            middle = jnp.mean(outer, axis=0, keepdims=True)
            key_top = jnp.maximum(key_top, norms(inner + middle) + norms(outer - middle))
            wide = slice((2 * heads + head) * LANES, (2 * heads + head + 1) * LANES)
            value_top = jnp.maximum(value_top, largest(jnp.abs(proj_ref[:CUBE, wide])) + largest(jnp.abs(proj_ref[CUBE:, wide])))
        top_ref[0:8, :] = jnp.zeros((8, LANES), F32)
        top_ref[8:16, :] = jnp.broadcast_to(key_top, (8, LANES))
        top_ref[16:24, :] = jnp.broadcast_to(value_top, (8, LANES))

    value_extra = jnp.where(lane >= HD, 1.0, 0.0)
    scales = []
    extras = []
    slab_rows = []
    for part in range(parts):
        slab = step * parts + part
        row = CUBE + jnp.minimum(slab, slabs - 1)
        slab_rows.append(proj_ref[pl.ds(row, 1), :])
        mean = sum_ref[:CUBE, :] + sum_ref[pl.ds(row, 1), :]
        spread = square_ref[:CUBE, :] + square_ref[pl.ds(row, 1), :] - mean * mean
        scales.append(lax.rsqrt(spread + 1e-06))
        pick = (lax.broadcasted_iota(I32, (LANES, LANES), 0) == slab) & (
            lax.broadcasted_iota(I32, (LANES, LANES), 1) == HD
        )
        key_extra = dot32(shown[...], jnp.where(pick, OFF_BIAS, 0.0).astype(BF))
        constant = jnp.where((lane > HD) & (lane < HD + 4), 1.0, jnp.where((lane == HD) & (slab >= slabs), OFF_BIAS, 0.0))
        extras.append(key_extra + constant)
    for scale in scales:
        top_ref[0:8, :] = jnp.maximum(top_ref[0:8, :], top_rows(scale))
    scale = jnp.concatenate(scales, axis=0)
    key_extra = jnp.concatenate(extras, axis=0)
    for head in range(heads):
        for first, extra, target in ((heads, key_extra, km_ref), (2 * heads, value_extra, vm_ref)):
            wide = slice((first + head) * LANES, (first + head + 1) * LANES)
            block = jnp.concatenate([proj_ref[:CUBE, wide] + row[:, wide] for row in slab_rows], axis=0)
            target[head] = (block * scale + extra).astype(BF)


def owned_kernel(seq_ref, owner_ref, ids_ref):
    groups, size = owner_ref.shape
    rows = ids_ref.shape[0]
    flags = jnp.where(owner_ref[...] == seq_ref[0], 1.0, 0.0).astype(BF)

    def upper(count):
        shape = (count, count)
        return jnp.where(lax.broadcasted_iota(I32, shape, 0) <= lax.broadcasted_iota(I32, shape, 1), 1.0, 0.0).astype(BF)

    local = dot32(flags, upper(size))
    totals = lax.dot_general(jnp.ones((8, size), BF), flags, NT, preferred_element_type=F32)
    ends = dot32(totals.astype(BF), upper(groups))
    begins = (ends - totals)[0:1, :]
    ends = ends[0:1, :]
    slot = lax.broadcasted_iota(I32, (rows, 1), 0).astype(F32)
    group = jnp.sum(jnp.where(ends <= slot, 1.0, 0.0), axis=1, keepdims=True)
    lane = lax.broadcasted_iota(I32, (rows, groups), 1).astype(F32)
    hot = jnp.where(lane == group, 1.0, 0.0)
    begin = jnp.sum(hot * begins, axis=1, keepdims=True)
    counts = dot32(hot.astype(BF), local.astype(BF))
    within = jnp.sum(jnp.where(counts <= slot - begin, 1.0, 0.0), axis=1, keepdims=True)
    ids_ref[...] = (group * size + within).astype(I32)


def place_hot(ids, places):
    lane = lax.broadcasted_iota(I32, (ids.shape[0], places), 1)
    slab = ids // CUBE
    inner = ids - slab * CUBE
    return jnp.where((lane == inner) | (lane == slab + CUBE), 1.0, 0.0).astype(BF)


def queries_kernel(
    heads, rows_ref, idc_ref, idr_ref, own_ref, table_ref, gain_ref, weight_ref, proj_ref, sum_ref, square_ref, top_ref,
    kv_ref, vv_ref, q_ref, seen_q, bounds, tables,
):
    step = pl.program_id(0)
    wide = heads * LANES

    @pl.when(step == 0)
    def _():
        count = rows_ref.shape[0]
        hot = place_hot(idc_ref[...], table_ref.shape[0])
        place = sum(dot32(hot, part) for part in split2(table_ref[...]))
        seen = layer_norm(rows_ref[...].astype(F32) + place, gain_ref[...].astype(F32)).astype(BF)
        seen_q[...] = (dot32(seen, weight_ref[:, :wide]) * LOG_SCALE).astype(BF)
        lane = lax.broadcasted_iota(I32, (1, LANES), 1)
        extra = jnp.where((lane > HD) & (lane < HD + 4), 1.0, 0.0)
        ones = jnp.where(lane >= HD, 1.0, 0.0)
        scale = jnp.max(top_ref[0:8, :], axis=0, keepdims=True)
        masked_key = scale * top_ref[8:9, :]
        top = jnp.zeros((8, LANES), F32)
        high = scale * top_ref[16:24, :]
        spare = kv_ref.shape[1] - count
        for head in range(heads):
            first = (heads + head) * LANES
            keys = dot32(seen, weight_ref[:, first : first + LANES])
            top = jnp.maximum(top, top_rows(square_sums(keys)))
            middle = jnp.mean(keys, axis=0, keepdims=True)
            middle = jnp.sum(middle * middle, axis=1, keepdims=True)
            bounds[head : head + 1, :] = jnp.broadcast_to(jnp.sqrt(middle) * 1.03, (1, LANES))
            kv_ref[head, :count, :] = (keys + extra).astype(BF)
            first = (2 * heads + head) * LANES
            values = dot32(seen, weight_ref[:, first : first + LANES])
            high = jnp.maximum(high, top_rows(jnp.abs(values)))
            vv_ref[head, :count, :] = (values + ones).astype(BF)
            if spare:
                off = lax.broadcasted_iota(I32, (spare, LANES), 1) == HD
                kv_ref[head, count:, :] = jnp.where(off, OFF_BIAS, 0.0).astype(BF)
                vv_ref[head, count:, :] = jnp.ones((spare, LANES), BF)
        seen_key = jnp.sqrt(jnp.max(top, axis=0, keepdims=True))
        bounds[heads : heads + 1, :] = jnp.maximum(seen_key, masked_key) * 1.03
        largest = jnp.max(jnp.max(high, axis=0, keepdims=True), axis=1, keepdims=True)
        bounds[heads + 1 : heads + 2, :] = jnp.broadcast_to(largest, (1, LANES))
        joined = jnp.concatenate([proj_ref[:, :wide], sum_ref[...], square_ref[...]], axis=1)
        for i, part in enumerate(split2(joined)):
            tables[i] = part

    @pl.when(step > 0)
    def _():
        ids = own_ref[...]
        count = ids.shape[0]
        hot = place_hot(ids, table_ref.shape[0])
        mixed = dot32(hot, tables[0]) + dot32(hot, tables[1])
        mean = mixed[:, wide : wide + LANES]
        scale = lax.rsqrt(mixed[:, wide + LANES :] - mean * mean + 1e-06)
        match = jnp.where(ids == idr_ref[...], 1.0, 0.0)
        shown = jnp.max(match, axis=1, keepdims=True) > 0.5
        picked = dot32(match.astype(BF), seen_q[...])
        lane = lax.broadcasted_iota(I32, (count, LANES), 1)
        limit = bounds[heads : heads + 1, :]
        fine = bounds[heads + 1 : heads + 2, :] < 2.0**25
        for head in range(heads):
            span = slice(head * LANES, (head + 1) * LANES)
            part = jnp.where(shown, picked[:, span], scale * mixed[:, span])
            norm = jnp.sqrt(square_sums(part))
            ceiling = norm * limit
            slack = jnp.where(fine, ceiling + norm * bounds[head : head + 1, :], 1e30)
            extra = jnp.where(lane == HD, 1.0, jnp.where(lane == HD + 1, HEADROOM - ceiling, 0.0))
            extra = jnp.where(lane == HD + 4, slack, extra)
            q_ref[head] = jnp.where(lane < HD, part, extra).astype(BF)


def attend_kernel(offset, rows, q_ref, km_ref, vm_ref, kv_ref, vv_ref, out_ref, q_scr, acc, ctx, p_even, p_odd):
    head = pl.program_id(0)
    q_scr[...] = q_ref[0, offset : offset + rows, :]
    block = p_even.shape[1]
    steps = km_ref.shape[1] // block
    rest = km_ref.shape[1] - steps * block
    tails = [(km_ref, vm_ref, steps * block, rest)] if rest else []
    visible = kv_ref.shape[1]
    tails += [(kv_ref, vv_ref, i, min(block, visible - i)) for i in range(0, visible, block)]

    def keys_of(i):
        if isinstance(i, int) and i >= steps:
            keys, _, start, size = tails[i - steps]
            return keys[0, start : start + size, :]
        return km_ref[0, pl.ds(i * block, block), :]

    def values_of(i):
        if isinstance(i, int) and i >= steps:
            _, values, start, size = tails[i - steps]
            return values[0, start : start + size, :]
        return vm_ref[0, pl.ds(i * block, block), :]

    def scores(i):
        return lax.dot_general(q_scr[...], keys_of(i), NT, preferred_element_type=F32)

    total = steps + len(tails)
    lane = lax.broadcasted_iota(I32, (rows, LANES), 1)
    slack = jnp.max(jnp.where(lane == HD + 4, q_scr[...].astype(F32), -1e30))

    @pl.when(jnp.logical_not(slack <= WINDOW))
    def _():
        q_scr[...] = jnp.where(lane > HD, 0.0, q_scr[...].astype(F32)).astype(BF)

        def look(i, best):
            return jnp.maximum(best, jnp.max(scores(i), axis=1, keepdims=True))

        peak = lax.fori_loop(0, steps, look, jnp.full((rows, 1), -3e38, F32))
        for i in range(steps, total):
            peak = look(i, peak)
        high, mid, low = split3(peak)
        new = jnp.where(lane == HD + 1, -high.astype(F32), q_scr[...].astype(F32))
        new = jnp.where(lane == HD + 2, -mid.astype(F32), new)
        new = jnp.where(lane == HD + 3, -low.astype(F32), new)
        q_scr[...] = new.astype(BF)

    def width_of(i):
        return tails[i - steps][3] if isinstance(i, int) and i >= steps else block

    def weigh(i, target):
        target[:, : width_of(i)] = jnp.exp2(scores(i)).astype(BF)

    def add(weights, i):
        acc[...] += dot32(weights[:, : width_of(i)], values_of(i))

    acc[...] = jnp.zeros_like(acc)
    slots = (p_even, p_odd)
    weigh(0, p_even)

    def body(j, carry):
        i = 2 * j + 1
        weigh(i, p_odd)
        add(p_even, i - 1)
        weigh(i + 1, p_even)
        add(p_odd, i)
        return carry

    pairs = (steps - 1) // 2
    lax.fori_loop(0, pairs, body, 0)
    for i in range(1 + 2 * pairs, total + 1):
        if i < total:
            weigh(i, slots[i % 2])
        add(slots[1 - i % 2], i - 1)
    totals = acc[...]
    ctx[head] = totals[:, :HD] / totals[:, HD:]

    @pl.when(head == pl.num_programs(0) - 1)
    def _():
        out_ref[...] = jnp.concatenate([ctx[i] for i in range(ctx.shape[0])], axis=1).astype(BF)


def attend(q_all, km, vm, kv, vv, offset, rows):
    heads, total, _ = q_all.shape
    masked, visible = km.shape[1], kv.shape[1]
    per_head = lambda size: pl.BlockSpec((1, size, LANES), lambda h: (h, 0, 0))
    return pl.pallas_call(
        functools.partial(attend_kernel, offset, rows),
        grid=(heads,),
        in_specs=[per_head(total), per_head(masked), per_head(masked), per_head(visible), per_head(visible)],
        out_specs=pl.BlockSpec((rows, heads * HD), lambda h: (0, 0)),
        out_shape=jax.ShapeDtypeStruct((rows, heads * HD), BF),
        scratch_shapes=[
            pltpu.VMEM((rows, LANES), BF),
            pltpu.VMEM((rows, LANES), F32),
            pltpu.VMEM((heads, rows, HD), F32),
            pltpu.VMEM((rows, KEY_BLOCK), BF),
            pltpu.VMEM((rows, KEY_BLOCK), BF),
        ],
        compiler_params=PARAMS,
        cost_estimate=pl.CostEstimate(
            flops=8 * heads * rows * (masked + visible) * LANES,
            bytes_accessed=4 * heads * masked * LANES,
            transcendentals=heads * rows * masked,
        ),
        name="attend",
    )(q_all, km, vm, kv, vv)


def gelu(x):
    size = jnp.abs(x)
    base = 1.0 + 0.2316419 * size
    t = pl.reciprocal(base)
    poly = 0.5307027145
    for c in (-0.7265760135, 0.7107068705, -0.142248368, 0.127414796):
        poly = poly * t + c
    tail = poly * t * jnp.exp2(x * x * (-0.5 * math.log2(math.e)))
    return x * jnp.where(x < 0.0, tail, 1.0 - tail)


def mlp_kernel(pieces, share, priors, scalars, *refs):
    ctx_refs, refs = refs[:pieces], refs[pieces:]
    own_ref, idr_ref, rows_ref, table_ref, mask_ref, gain_ref = refs[:6]
    row0 = pl.multiple_of(scalars[1], 16)
    earlier, refs = refs[6 : 6 + priors], refs[6 + priors :]
    weights, refs = refs[: 2 * pieces], refs[2 * pieces :]
    res_ref, ups, downs, outs, acc, mlp_in, sems = refs[:7]
    stages = refs[7:]
    step = pl.program_id(0)
    half = weights[0].shape[1]
    up = ups.shape[2]
    tail = up + downs.shape[1]
    first = scalars[0]
    swap = lambda a: jnp.where(first == 0, a, jnp.concatenate([a[:, half:], a[:, :half]], axis=1))

    def out_copy(i):
        side = slice(i % 2 * half, (i % 2 + 1) * half)
        return pltpu.make_async_copy(weights[i].at[tail:], outs.at[i // 2, :, side], sems.at[i, 0])

    def copies(i):
        side = slice(i % 2 * half, (i % 2 + 1) * half)
        moves = [
            pltpu.make_async_copy(
                weights[i].at[k * half : (k + 1) * half],
                ups.at[i // 2, side, k * half : (k + 1) * half],
                sems.at[i, 1 + k],
            )
            for k in range(up // half)
        ]
        last = sems.at[i, 1 + up // half]
        return moves + [pltpu.make_async_copy(weights[i].at[up:tail], downs.at[i // 2, :, side], last)]

    def stored(k):
        count = earlier[k].shape[0]
        place = pl.ds(pl.multiple_of(scalars[2 + k], 16), count)
        return pltpu.make_async_copy(stages[k], res_ref.at[place], sems.at[2 * pieces + 1 + k, 0])

    @pl.when(step == 0)
    def _():
        for i in range(2 * pieces):
            out_copy(i).start()
        for i in range(2 * pieces):
            for copy in copies(i):
                copy.start()
        ids = own_ref[...] if share == own_ref.shape[0] else own_ref[pl.ds(row0, share), :]
        hot = place_hot(ids, table_ref.shape[0])
        place = sum(dot32(hot, part) for part in split2(table_ref[...]))
        match = jnp.where(ids == idr_ref[...], 1.0, 0.0)
        shown = jnp.max(match, axis=1, keepdims=True) > 0.5
        stream = jnp.where(shown, dot32(match.astype(BF), rows_ref[...]), mask_ref[...].astype(F32)) + place
        acc[...] = swap(stream)
        for i in range(pieces):
            out_copy(2 * i).wait()
            out_copy(2 * i + 1).wait()
            acc[...] += dot32(ctx_refs[i][...], outs[i])
        mlp_in[...] = layer_norm(acc[...], swap(gain_ref[...].astype(F32))).astype(BF)

    for i in range(pieces):

        @pl.when(step == i)
        def _(i=i):
            for copy in copies(2 * i) + copies(2 * i + 1):
                copy.wait()
            for k in range(i, priors, pieces):
                stages[k][...] = earlier[k][...].astype(F32)
                stored(k).start()

    wide = 256 if up % 256 == 0 else up
    blocks = [slice(k, k + wide) for k in range(0, up, wide)]
    pres = [dot32(mlp_in[...], ups[step, :, span]) for span in blocks]
    added = 0.0
    for pre, span in zip(pres, blocks):
        hidden = gelu(pre).astype(BF)
        added += dot32(hidden, downs[step, span, :])
    acc[...] += added

    @pl.when(step == pieces - 1)
    def _():
        if not priors:
            res_ref[...] = swap(acc[...]).astype(res_ref.dtype)
        else:
            acc[...] = swap(acc[...])
            own = pltpu.make_async_copy(acc, res_ref.at[res_ref.shape[0] - share :], sems.at[2 * pieces, 0])
            own.start()
            for k in range(priors):
                stored(k).wait()
            own.wait()


def mlp(scalars, contexts, own_ids, id_row, all_rows, table, mask_row, gain_row, weights, units, priors, total, kind):
    pieces = len(weights) // 2
    share = contexts[0].shape[0]
    width = all_rows.shape[1]
    ins = [*contexts, own_ids, id_row, all_rows, table, mask_row, gain_row, *priors]
    return pl.pallas_call(
        functools.partial(mlp_kernel, pieces, share, len(priors)),
        grid=(pieces,),
        in_specs=[SMEM] + [whole(a) for a in ins] + [pl.BlockSpec(memory_space=pl.ANY)] * len(weights),
        out_specs=pl.BlockSpec(memory_space=pl.ANY) if priors else pl.BlockSpec((share, width), lambda i: (0, 0)),
        out_shape=jax.ShapeDtypeStruct((total, width), kind),
        scratch_shapes=[
            pltpu.VMEM((pieces, width, units), BF),
            pltpu.VMEM((pieces, units, width), BF),
            pltpu.VMEM((pieces, contexts[0].shape[1], width), BF),
            pltpu.VMEM((share, width), F32),
            pltpu.VMEM((share, width), BF),
            pltpu.SemaphoreType.DMA((2 * pieces + 1 + len(priors), 2 + units // (width // 2))),
        ]
        + [pltpu.VMEM(p.shape, F32) for p in priors],
        compiler_params=PARAMS,
        cost_estimate=pl.CostEstimate(
            flops=30 * share * width * width, bytes_accessed=18 * width * width, transcendentals=4 * share * width
        ),
        name="mlp",
    )(scalars, *ins, *weights)


def place_kernel(pieces, scalars, *refs):
    sources, (_held, out_ref), (sems, *stages) = refs[:pieces], refs[pieces : pieces + 2], refs[pieces + 2 :]

    def move(k):
        count = sources[k].shape[0]
        place = pl.ds(pl.multiple_of(scalars[k], 16), count)
        return pltpu.make_async_copy(stages[k], out_ref.at[place], sems.at[k])

    for k in range(pieces):
        stages[k][...] = sources[k][...].astype(F32)
        move(k).start()
    for k in range(pieces):
        move(k).wait()


def put_rows(decoded, pieces, places):
    count = len(pieces)
    return pl.pallas_call(
        functools.partial(place_kernel, count),
        in_specs=[SMEM] + [pl.BlockSpec(memory_space=pltpu.VMEM)] * count + [pl.BlockSpec(memory_space=pl.ANY)],
        out_specs=pl.BlockSpec(memory_space=pl.ANY),
        out_shape=jax.ShapeDtypeStruct(decoded.shape, decoded.dtype),
        scratch_shapes=[pltpu.SemaphoreType.DMA((count,))] + [pltpu.VMEM(p.shape, F32) for p in pieces],
        input_output_aliases={count + 1: 0},
        compiler_params=PARAMS,
        name="put_rows",
    )(jnp.stack(places), *pieces, decoded)


def shards(
    enc_rows,
    vis_index,
    owner_of,
    enc_gain,
    embed_weight,
    mask_token,
    attn_gain,
    qkv_weight,
    out_weight,
    mlp_gain,
    up_weight,
    down_weight,
):
    section = lax.axis_index("section")
    section_ref = section.astype(I32).reshape(1)
    mp_size = lax.axis_size("mp")
    mp_index = lax.axis_index("mp")
    patch_total = owner_of.shape[0]
    own_rows = patch_total // lax.axis_size("seq")
    features = mask_token.shape[0]
    half = features // 2
    width = qkv_weight.shape[2]
    heads = width // HD
    slabs = patch_total // CUBE
    places = CUBE + slabs
    vmem = lambda shape, kind: jax.ShapeDtypeStruct(shape, kind)

    embed_other = shifted(embed_weight, "section", 1)
    qkv_mine = qkv_weight.reshape(half, 3 * width)
    qkv_other = shifted(qkv_mine, "section", 1)
    all_ids = gather_rows(vis_index[0], "seq")
    embedded = pl.pallas_call(
        embed_kernel,
        in_specs=[SMEM] + [pl.BlockSpec(memory_space=pltpu.VMEM)] * 4,
        out_specs=pl.BlockSpec(memory_space=pltpu.VMEM),
        out_shape=vmem((enc_rows.shape[1], features), BF),
        compiler_params=PARAMS,
        name="embed",
    )(section_ref, enc_rows[0], enc_gain[None, :], embed_weight, embed_other)
    embedded, all_ids = lax.optimization_barrier((embedded, all_ids))
    all_rows = gather_rows(embedded, "seq")
    id_col = all_ids[:, None]
    id_row = all_ids[None, :]
    visible = all_ids.shape[0]

    table = jnp.asarray(place_table(slabs, features))
    mask_row = mask_token[None, :]
    gain_attn = attn_gain[None, :]
    groups = 3 * heads
    qkv_wide, proj, means, squares = pl.pallas_call(
        functools.partial(table_kernel, groups),
        in_specs=[SMEM] + [pl.BlockSpec(memory_space=pltpu.VMEM)] * 5,
        out_specs=[pl.BlockSpec(memory_space=pltpu.VMEM)] * 4,
        out_shape=[
            vmem((features, groups * LANES), BF),
            vmem((places, groups * LANES), F32),
            vmem((places, LANES), F32),
            vmem((places, LANES), F32),
        ],
        compiler_params=PARAMS,
        name="tables",
    )(section_ref, table, mask_row, gain_attn, qkv_mine, qkv_other)

    padded = patch_total + (-patch_total % KEY_PAD)
    slab_rows = 4 * CUBE
    blocks = -(-padded // slab_rows)
    ins = [proj, means, squares, id_row]
    key_spec = pl.BlockSpec((heads, slab_rows, LANES), lambda i: (0, i, 0))
    km, vm, top = pl.pallas_call(
        functools.partial(masked_kernel, heads, patch_total),
        grid=(blocks,),
        in_specs=[whole(a) for a in ins],
        out_specs=[key_spec, key_spec, pl.BlockSpec((24, LANES), lambda i: (0, 0))],
        out_shape=[vmem((heads, padded, LANES), BF)] * 2 + [vmem((24, LANES), F32)],
        scratch_shapes=[pltpu.VMEM((CUBE, LANES), BF)],
        compiler_params=PARAMS,
        name="masked",
    )(*ins)

    group = HD
    own_ids = pl.pallas_call(
        owned_kernel,
        in_specs=[SMEM, pl.BlockSpec(memory_space=pltpu.VMEM)],
        out_specs=pl.BlockSpec(memory_space=pltpu.VMEM),
        out_shape=vmem((own_rows, 1), I32),
        compiler_params=PARAMS,
        name="owned",
    )(lax.axis_index("seq").astype(I32).reshape(1), owner_of.reshape(patch_total // group, group))

    row_block = 720 if own_rows % 720 == 0 else own_rows
    spaced = visible + (-visible % KEY_PAD)
    ins = [all_rows, id_col, id_row, own_ids, table, gain_attn, qkv_wide, proj, means, squares, top]
    specs = [whole(a) for a in ins]
    specs[3] = pl.BlockSpec((row_block, 1), lambda i: (jnp.maximum(i - 1, 0), 0))
    kv, vv, q_all = pl.pallas_call(
        functools.partial(queries_kernel, heads),
        grid=(1 + own_rows // row_block,),
        in_specs=specs,
        out_specs=[pl.BlockSpec((heads, spaced, LANES), lambda i: (0, 0, 0))] * 2
        + [pl.BlockSpec((heads, row_block, LANES), lambda i: (0, jnp.maximum(i - 1, 0), 0))],
        out_shape=[vmem((heads, spaced, LANES), BF)] * 2 + [vmem((heads, own_rows, LANES), BF)],
        scratch_shapes=[
            pltpu.VMEM((visible, heads * LANES), BF),
            pltpu.VMEM((8 * (-(-(heads + 2) // 8)), LANES), F32),
            pltpu.VMEM((2, places, (heads + 2) * LANES), BF),
        ],
        compiler_params=PARAMS,
        name="queries",
    )(*ins)

    units = up_weight.shape[1]
    packed = jnp.concatenate(
        [up_weight[:, i : i + half] for i in range(0, units, half)] + [down_weight, out_weight], axis=0
    )
    packed, _unused = lax.optimization_barrier((packed, embedded))
    mine = shift_pieces(packed, "mp")

    spans = [(0, own_rows)]
    if own_rows >= 2048:
        spans = [(0, 1152), (1152, 640), (1792, own_rows - 1792)]
    gain_row = mlp_gain[None, :]
    weights = []

    def finish(contexts, row0, places, priors, total, kind):
        scalars = jnp.stack([section.astype(I32), jnp.asarray(row0, I32), *places])
        return mlp(scalars, contexts, own_ids, id_row, all_rows, table, mask_row, gain_row, weights, units, priors, total, kind)

    exchanged = []
    shares = []
    for first, rows in spans[:-1]:
        share = rows // mp_size
        context = attend(q_all, km, vm, kv, vv, first, rows)
        if not weights:
            *mine, _unused = lax.optimization_barrier((*mine, context))
            for piece in mine:
                weights += [piece, shifted(piece, "section", 1)]
        pieces = []
        for step in range(mp_size):
            start = (mp_index + step) % mp_size * share
            part = lax.dynamic_slice_in_dim(context, start, share, axis=0)
            pieces.append(part if step == 0 else shifted(part, "mp", step))
        exchanged.append(pieces)
        shares.append(first + mp_index * share)
    if not weights:
        for piece in mine:
            weights += [piece, shifted(piece, "section", 1)]
    priors = []
    places = []

    def spread(k, result):
        first, rows = spans[k]
        at = [(first + (mp_index - step) % mp_size * (rows // mp_size)).astype(I32) for step in range(mp_size)]
        return shift_pieces(result, "mp"), at

    if exchanged:
        done = finish(exchanged[0], shares[0], [], [], exchanged[0][0].shape[0], BF)
        q_all, done, *exchanged[1] = lax.optimization_barrier((q_all, done, *exchanged[1]))
        priors, places = spread(0, done)
    first, rows = spans[-1]
    context = attend(q_all, km, vm, kv, vv, first, rows)
    last = shift_pieces(context, "mp")
    if not exchanged:
        return finish(last, 0, [], [], own_rows, F32)[None]
    exchanged[1][0], context, *priors = lax.optimization_barrier((exchanged[1][0], context, *priors))
    done = finish(exchanged[1], shares[1], [], [], exchanged[1][0].shape[0], BF)
    last[0], done = lax.optimization_barrier((last[0], done))
    late, late_places = spread(1, done)
    decoded = finish(last, first, places, priors, own_rows, F32)
    return put_rows(decoded, late, late_places)[None]


def solution(mesh):
    in_specs = (
        P("section", "seq", None),
        P("section", "seq"),
        P(),
        P(),
        P("section", None),
        P(),
        P(),
        P("section", None, "mp"),
        P("mp", "section"),
        P(),
        P("section", "mp"),
        P("mp", "section"),
    )
    out_specs = P("section", "seq", None)
    return jax.shard_map(shards, mesh=mesh, in_specs=in_specs, out_specs=out_specs, check_vma=False)
```

```python
import functools
import math

import jax
import jax.numpy as jnp
import numpy as np
from jax import lax
from jax.experimental import pallas as pl
from jax.experimental.pallas import tpu as pltpu
from jax.sharding import PartitionSpec as P

GX = 6
HD = 64
LANES = 128
KEY_BLOCK = 1024
KEY_PAD = 256
OFF_BIAS = -1e30
HEADROOM = 88.0
WINDOW = 180.0
CUBE = GX * GX * GX
HIGH = lax.Precision.HIGHEST
BF = jnp.bfloat16
F32 = jnp.float32
I32 = jnp.int32
VMEM_LIMIT = 56 * 1024 * 1024
LOG_SCALE = math.log2(math.e) * HD ** (-0.5)
NT = (((1,), (1,)), ((), ()))
PARAMS = pltpu.CompilerParams(vmem_limit_bytes=VMEM_LIMIT)


def layer_norm(values, scales):
    centred = values - jnp.mean(values, axis=-1, keepdims=True)
    spread = jnp.mean(centred * centred, axis=-1, keepdims=True)
    return centred * lax.rsqrt(spread + 1e-06) * scales


def dot32(a, b):
    return jnp.dot(a, b, preferred_element_type=F32)


def split3(values):
    high = values.astype(BF)
    rest = values - high.astype(F32)
    mid = rest.astype(BF)
    return high, mid, (rest - mid.astype(F32)).astype(BF)


def split2(values):
    high = values.astype(BF)
    return high, (values - high.astype(F32)).astype(BF)


def shifted(values, axis, step):
    size = lax.axis_size(axis)
    return lax.ppermute(values, axis, [(i, (i + step) % size) for i in range(size)])


def shift_pieces(values, axis):
    return [values] + [shifted(values, axis, step) for step in range(1, lax.axis_size(axis))]


def gather_pieces(values, axis):
    if lax.axis_size(axis) > 4:
        return [lax.all_gather(values, axis, axis=0, tiled=True)]
    return shift_pieces(values, axis)


def whole(array):
    return pl.BlockSpec(array.shape, lambda *_: (0,) * array.ndim)


SMEM = pl.BlockSpec(memory_space=pltpu.SMEM)


def place_table(slabs, features):
    quarter = features // 4
    frequency = (1.0 / 10000.0 ** (np.arange(quarter // 2, dtype=np.float32) / (quarter // 2))).astype(np.float32)
    angles = np.arange(max(slabs, GX), dtype=np.float32)[:, None] * frequency[None, :]
    codes = np.concatenate([np.sin(angles), np.cos(angles)], axis=1).astype(np.float32)
    place = np.arange(CUBE)
    cube = np.concatenate(
        [codes[place % GX], codes[place // GX % GX], codes[place // (GX * GX)], np.zeros((CUBE, quarter), np.float32)],
        axis=1,
    )
    slab = np.concatenate([np.zeros((slabs, 3 * quarter), np.float32), codes[:slabs]], axis=1)
    return np.concatenate([cube, slab], axis=0)


def embed_kernel(position, rows_ref, gain_ref, mine_ref, other_ref, out_ref):
    normed = layer_norm(rows_ref[...].astype(F32), gain_ref[...].astype(F32)).astype(BF)
    half = normed.shape[1] // 2
    low, high = normed[:, :half], normed[:, half:]
    first = position[0] == 0

    @pl.when(first)
    def _():
        out_ref[...] = (dot32(low, mine_ref[...]) + dot32(high, other_ref[...])).astype(BF)

    @pl.when(jnp.logical_not(first))
    def _():
        out_ref[...] = (dot32(low, other_ref[...]) + dot32(high, mine_ref[...])).astype(BF)


def table_kernel(
    groups, position, table_ref, mask_ref, gain_ref, mine_ref, other_ref, weight_ref, proj_ref, sum_ref, square_ref
):
    features = table_ref.shape[1]
    places = table_ref.shape[0]
    first = position[0] == 0
    mine, other = mine_ref[...], other_ref[...]
    full = jnp.concatenate([jnp.where(first, mine, other), jnp.where(first, other, mine)], axis=0)
    gain = gain_ref[...].astype(F32)
    mask = mask_ref[...].astype(F32)
    mask = mask - jnp.mean(mask, axis=1, keepdims=True)
    table = table_ref[...]
    row = lax.broadcasted_iota(I32, table.shape, 0)
    lane = lax.broadcasted_iota(I32, table.shape, 1)
    rows = table + jnp.where(row < CUBE, mask, 0.0)
    gained = jnp.concatenate([rows * gain, jnp.broadcast_to(gain, (16, features))], axis=0)
    proj = sum(dot32(part, full) for part in split3(gained))
    last = lane >= features - features // 4
    squared = jnp.where(row < CUBE, jnp.where(last, 0.0, rows), jnp.where(last, rows + mask, 0.0))
    total = jnp.sum(rows, axis=1, keepdims=True)
    square = jnp.sum(squared * squared, axis=1, keepdims=True)
    column = lax.broadcasted_iota(I32, (1, groups * HD), 1)
    scale = jnp.where(column < groups * HD // 3, LOG_SCALE, 1.0)
    proj = (proj[:places, :] - (total / features) * proj[places : places + 1, :]) * scale
    for group in range(groups):
        span = slice(group * HD, (group + 1) * HD)
        wide = slice(group * LANES, (group + 1) * LANES)
        weight_ref[:, wide] = jnp.concatenate([full[:, span], jnp.zeros((features, HD), BF)], axis=1)
        proj_ref[:, wide] = jnp.concatenate([proj[:, span], jnp.zeros((places, HD), F32)], axis=1)
    sum_ref[...] = jnp.broadcast_to(total / features, sum_ref.shape)
    square_ref[...] = jnp.broadcast_to(square / features, square_ref.shape)


def top_rows(values):
    return jnp.max(values.reshape(values.shape[0] // 8, 8, LANES), axis=0)


def square_sums(values):
    return dot32((values * values).astype(BF), jnp.ones((LANES, LANES), BF))


def masked_kernel(heads, patch_total, proj_ref, sum_ref, square_ref, ids_ref, km_ref, vm_ref, top_ref, shown):
    step = pl.program_id(0)
    parts = km_ref.shape[1] // CUBE
    slabs = patch_total // CUBE
    lane = lax.broadcasted_iota(I32, (1, LANES), 1)

    @pl.when(step == 0)
    def _():
        ids = ids_ref[...]
        slab = slab_of(ids)
        inner = ids - slab * CUBE
        rows = lax.broadcasted_iota(I32, (CUBE, ids.shape[1]), 0)
        columns = lax.broadcasted_iota(I32, (LANES, ids.shape[1]), 0)
        by_place = jnp.where(rows == inner, 1.0, 0.0).astype(BF)
        by_slab = jnp.where(columns == slab, 1.0, 0.0).astype(BF)
        shown[...] = lax.dot_general(by_place, by_slab, NT, preferred_element_type=F32).astype(BF)
        largest = lambda x: jnp.max(jnp.max(x, axis=0, keepdims=True), axis=1, keepdims=True)
        norms = lambda x: jnp.sqrt(jnp.max(jnp.sum(x * x, axis=1, keepdims=True), axis=0, keepdims=True))
        key_top = jnp.zeros((1, 1), F32)
        value_top = jnp.zeros((1, 1), F32)
        for head in range(heads):
            wide = slice((heads + head) * LANES, (heads + head + 1) * LANES)
            inner, outer = proj_ref[:CUBE, wide], proj_ref[CUBE:, wide]
            middle = jnp.mean(outer, axis=0, keepdims=True)
            key_top = jnp.maximum(key_top, norms(inner + middle) + norms(outer - middle))
            wide = slice((2 * heads + head) * LANES, (2 * heads + head + 1) * LANES)
            value_top = jnp.maximum(value_top, largest(jnp.abs(proj_ref[:CUBE, wide])) + largest(jnp.abs(proj_ref[CUBE:, wide])))
        top_ref[0:8, :] = jnp.zeros((8, LANES), F32)
        top_ref[8:16, :] = jnp.broadcast_to(key_top, (8, LANES))
        top_ref[16:24, :] = jnp.broadcast_to(value_top, (8, LANES))

    value_extra = jnp.where(lane >= HD, 1.0, 0.0)
    scales = []
    extras = []
    slab_rows = []
    for part in range(parts):
        slab = step * parts + part
        row = CUBE + jnp.minimum(slab, slabs - 1)
        slab_rows.append(proj_ref[pl.ds(row, 1), :])
        mean = sum_ref[:CUBE, :] + sum_ref[pl.ds(row, 1), :]
        spread = square_ref[:CUBE, :] + square_ref[pl.ds(row, 1), :] - mean * mean
        scales.append(lax.rsqrt(spread + 1e-06))
        pick = (lax.broadcasted_iota(I32, (LANES, LANES), 0) == slab) & (
            lax.broadcasted_iota(I32, (LANES, LANES), 1) == HD
        )
        key_extra = dot32(shown[...], jnp.where(pick, OFF_BIAS, 0.0).astype(BF))
        constant = jnp.where((lane > HD) & (lane < HD + 4), 1.0, jnp.where((lane == HD) & (slab >= slabs), OFF_BIAS, 0.0))
        extras.append(key_extra + constant)
    for scale in scales:
        top_ref[0:8, :] = jnp.maximum(top_ref[0:8, :], top_rows(scale))
    scale = jnp.concatenate(scales, axis=0)
    key_extra = jnp.concatenate(extras, axis=0)
    for head in range(heads):
        for first, extra, target in ((heads, key_extra, km_ref), (2 * heads, value_extra, vm_ref)):
            wide = slice((first + head) * LANES, (first + head + 1) * LANES)
            block = jnp.concatenate([proj_ref[:CUBE, wide] + row[:, wide] for row in slab_rows], axis=0)
            target[head] = (block * scale + extra).astype(BF)


def owned_kernel(seq_ref, owner_ref, ids_ref):
    groups, size = owner_ref.shape
    rows = ids_ref.shape[0]
    flags = jnp.where(owner_ref[...] == seq_ref[2], 1.0, 0.0).astype(BF)

    def upper(count):
        shape = (count, count)
        return jnp.where(lax.broadcasted_iota(I32, shape, 0) <= lax.broadcasted_iota(I32, shape, 1), 1.0, 0.0).astype(BF)

    local = dot32(flags, upper(size))
    totals = lax.dot_general(jnp.ones((8, size), BF), flags, NT, preferred_element_type=F32)
    ends = dot32(totals.astype(BF), upper(groups))
    begins = (ends - totals)[0:1, :]
    ends = ends[0:1, :]
    slot = lax.broadcasted_iota(I32, (rows, 1), 0).astype(F32)
    group = jnp.sum(jnp.where(ends <= slot, 1.0, 0.0), axis=1, keepdims=True)
    lane = lax.broadcasted_iota(I32, (rows, groups), 1).astype(F32)
    hot = jnp.where(lane == group, 1.0, 0.0)
    begin = jnp.sum(hot * begins, axis=1, keepdims=True)
    counts = dot32(hot.astype(BF), local.astype(BF))
    within = jnp.sum(jnp.where(counts <= slot - begin, 1.0, 0.0), axis=1, keepdims=True)
    ids_ref[...] = (group * size + within).astype(I32)


def slab_of(ids):
    return jnp.floor((ids.astype(F32) + 0.5) * (1.0 / CUBE)).astype(I32)


def place_hot(ids, places):
    lane = lax.broadcasted_iota(I32, (ids.shape[0], places), 1)
    slab = slab_of(ids)
    inner = ids - slab * CUBE
    return jnp.where((lane == inner) | (lane == slab + CUBE), 1.0, 0.0).astype(BF)


def queries_kernel(heads, pieces, *refs):
    row_refs = refs[:pieces]
    queries_body(heads, row_refs, *refs[pieces:])


def queries_body(
    heads, row_refs, idc_ref, idr_ref, own_ref, table_ref, gain_ref, weight_ref, proj_ref, sum_ref, square_ref, top_ref,
    kv_ref, vv_ref, q_ref, seen_q, bounds, tables,
):
    step = pl.program_id(0)
    wide = heads * LANES

    @pl.when(step == 0)
    def _():
        count = idc_ref.shape[0]
        rows = jnp.concatenate([ref[...].astype(F32) for ref in row_refs], axis=0)
        hot = place_hot(idc_ref[...], table_ref.shape[0])
        place = sum(dot32(hot, part) for part in split2(table_ref[...]))
        seen = layer_norm(rows + place, gain_ref[...].astype(F32)).astype(BF)
        seen_q[...] = (dot32(seen, weight_ref[:, :wide]) * LOG_SCALE).astype(BF)
        lane = lax.broadcasted_iota(I32, (1, LANES), 1)
        extra = jnp.where((lane > HD) & (lane < HD + 4), 1.0, 0.0)
        ones = jnp.where(lane >= HD, 1.0, 0.0)
        scale = jnp.max(top_ref[0:8, :], axis=0, keepdims=True)
        masked_key = scale * top_ref[8:9, :]
        top = jnp.zeros((8, LANES), F32)
        high = scale * top_ref[16:24, :]
        spare = kv_ref.shape[1] - count
        for head in range(heads):
            first = (heads + head) * LANES
            keys = dot32(seen, weight_ref[:, first : first + LANES])
            top = jnp.maximum(top, top_rows(square_sums(keys)))
            middle = jnp.mean(keys, axis=0, keepdims=True)
            middle = jnp.sum(middle * middle, axis=1, keepdims=True)
            bounds[head : head + 1, :] = jnp.broadcast_to(jnp.sqrt(middle) * 1.03, (1, LANES))
            kv_ref[head, :count, :] = (keys + extra).astype(BF)
            first = (2 * heads + head) * LANES
            values = dot32(seen, weight_ref[:, first : first + LANES])
            high = jnp.maximum(high, top_rows(jnp.abs(values)))
            vv_ref[head, :count, :] = (values + ones).astype(BF)
            if spare:
                off = lax.broadcasted_iota(I32, (spare, LANES), 1) == HD
                kv_ref[head, count:, :] = jnp.where(off, OFF_BIAS, 0.0).astype(BF)
                vv_ref[head, count:, :] = jnp.ones((spare, LANES), BF)
        seen_key = jnp.sqrt(jnp.max(top, axis=0, keepdims=True))
        bounds[heads : heads + 1, :] = jnp.maximum(seen_key, masked_key) * 1.03
        largest = jnp.max(jnp.max(high, axis=0, keepdims=True), axis=1, keepdims=True)
        bounds[heads + 1 : heads + 2, :] = jnp.broadcast_to(largest, (1, LANES))
        joined = jnp.concatenate([proj_ref[:, :wide], sum_ref[...], square_ref[...]], axis=1)
        for i, part in enumerate(split2(joined)):
            tables[i] = part

    @pl.when(step > 0)
    def _():
        ids = own_ref[...]
        count = ids.shape[0]
        hot = place_hot(ids, table_ref.shape[0])
        mixed = dot32(hot, tables[0]) + dot32(hot, tables[1])
        mean = mixed[:, wide : wide + LANES]
        scale = lax.rsqrt(mixed[:, wide + LANES :] - mean * mean + 1e-06)
        match = jnp.where(ids == idr_ref[...], 1.0, 0.0)
        shown = jnp.max(match, axis=1, keepdims=True) > 0.5
        picked = dot32(match.astype(BF), seen_q[...])
        lane = lax.broadcasted_iota(I32, (count, LANES), 1)
        limit = bounds[heads : heads + 1, :]
        fine = bounds[heads + 1 : heads + 2, :] < 2.0**25
        for head in range(heads):
            span = slice(head * LANES, (head + 1) * LANES)
            part = jnp.where(shown, picked[:, span], scale * mixed[:, span])
            norm = jnp.sqrt(square_sums(part))
            ceiling = norm * limit
            slack = jnp.where(fine, ceiling + norm * bounds[head : head + 1, :], 1e30)
            extra = jnp.where(lane == HD, 1.0, jnp.where(lane == HD + 1, HEADROOM - ceiling, 0.0))
            extra = jnp.where(lane == HD + 4, slack, extra)
            q_ref[head] = jnp.where(lane < HD, part, extra).astype(BF)


def attend_kernel(offset, rows, pieces, position, q_ref, km_ref, vm_ref, kv_ref, vv_ref, *refs):
    outs, (q_scr, acc, ctx, p_even, p_odd) = refs[:pieces], refs[pieces:]
    head = pl.program_id(0)
    q_scr[...] = q_ref[0, offset : offset + rows, :]
    block = p_even.shape[1]
    steps = km_ref.shape[1] // block
    rest = km_ref.shape[1] - steps * block
    tails = [(km_ref, vm_ref, steps * block, rest)] if rest else []
    visible = kv_ref.shape[1]
    tails += [(kv_ref, vv_ref, i, min(block, visible - i)) for i in range(0, visible, block)]

    def keys_of(i):
        if isinstance(i, int) and i >= steps:
            keys, _, start, size = tails[i - steps]
            return keys[0, start : start + size, :]
        return km_ref[0, pl.ds(i * block, block), :]

    def values_of(i):
        if isinstance(i, int) and i >= steps:
            _, values, start, size = tails[i - steps]
            return values[0, start : start + size, :]
        return vm_ref[0, pl.ds(i * block, block), :]

    def scores(i):
        return lax.dot_general(q_scr[...], keys_of(i), NT, preferred_element_type=F32)

    total = steps + len(tails)
    lane = lax.broadcasted_iota(I32, (rows, LANES), 1)
    slack = jnp.max(jnp.where(lane == HD + 4, q_scr[...].astype(F32), -1e30))

    @pl.when(jnp.logical_not(slack <= WINDOW))
    def _():
        q_scr[...] = jnp.where(lane > HD, 0.0, q_scr[...].astype(F32)).astype(BF)

        def look(i, best):
            return jnp.maximum(best, jnp.max(scores(i), axis=1, keepdims=True))

        peak = lax.fori_loop(0, steps, look, jnp.full((rows, 1), -3e38, F32))
        for i in range(steps, total):
            peak = look(i, peak)
        high, mid, low = split3(peak)
        new = jnp.where(lane == HD + 1, -high.astype(F32), q_scr[...].astype(F32))
        new = jnp.where(lane == HD + 2, -mid.astype(F32), new)
        new = jnp.where(lane == HD + 3, -low.astype(F32), new)
        q_scr[...] = new.astype(BF)

    def width_of(i):
        return tails[i - steps][3] if isinstance(i, int) and i >= steps else block

    def weigh(i, target):
        target[:, : width_of(i)] = jnp.exp2(scores(i)).astype(BF)

    def add(weights, i):
        acc[...] += dot32(weights[:, : width_of(i)], values_of(i))

    acc[...] = jnp.zeros_like(acc)
    slots = (p_even, p_odd)
    weigh(0, p_even)

    def body(j, carry):
        i = 2 * j + 1
        weigh(i, p_odd)
        add(p_even, i - 1)
        weigh(i + 1, p_even)
        add(p_odd, i)
        return carry

    pairs = (steps - 1) // 2
    lax.fori_loop(0, pairs, body, 0)
    for i in range(1 + 2 * pairs, total + 1):
        if i < total:
            weigh(i, slots[i % 2])
        add(slots[1 - i % 2], i - 1)
    totals = acc[...]
    ctx[head] = totals[:, :HD] / totals[:, HD:]

    @pl.when(head == pl.num_programs(0) - 1)
    def _():
        share = rows // pieces
        for step, out in enumerate(outs):
            target = lax.rem(position[1] + step, pieces)
            span = pl.ds(pl.multiple_of(target * share, 16), share) if pieces > 1 else slice(None)
            out[...] = jnp.concatenate([ctx[i, span, :] for i in range(ctx.shape[0])], axis=1).astype(BF)


def attend(position, q_all, km, vm, kv, vv, offset, rows, pieces):
    heads, total, _ = q_all.shape
    masked, visible = km.shape[1], kv.shape[1]
    per_head = lambda size: pl.BlockSpec((1, size, LANES), lambda h: (h, 0, 0))
    shape = (rows // pieces, heads * HD)
    return pl.pallas_call(
        functools.partial(attend_kernel, offset, rows, pieces),
        grid=(heads,),
        in_specs=[SMEM, per_head(total), per_head(masked), per_head(masked), per_head(visible), per_head(visible)],
        out_specs=[pl.BlockSpec(shape, lambda h: (0, 0))] * pieces,
        out_shape=[jax.ShapeDtypeStruct(shape, BF)] * pieces,
        scratch_shapes=[
            pltpu.VMEM((rows, LANES), BF),
            pltpu.VMEM((rows, LANES), F32),
            pltpu.VMEM((heads, rows, HD), F32),
            pltpu.VMEM((rows, KEY_BLOCK), BF),
            pltpu.VMEM((rows, KEY_BLOCK), BF),
        ],
        compiler_params=PARAMS,
        cost_estimate=pl.CostEstimate(
            flops=8 * heads * rows * (masked + visible) * LANES,
            bytes_accessed=4 * heads * masked * LANES,
            transcendentals=heads * rows * masked,
        ),
        name="attend",
    )(position, q_all, km, vm, kv, vv)


def gelu(x):
    size = jnp.abs(x)
    base = 1.0 + 0.2316419 * size
    t = pl.reciprocal(base, approx=True)
    t = t * (2.0 - base * t)
    poly = 0.5307027145
    for c in (-0.7265760135, 0.7107068705, -0.142248368, 0.127414796):
        poly = poly * t + c
    tail = poly * t * jnp.exp2(x * x * (-0.5 * math.log2(math.e)))
    return x * jnp.where(x < 0.0, tail, 1.0 - tail)


def mlp_kernel(pieces, row_pieces, first_row, spread, position, *refs):
    ctx_refs, refs = refs[:pieces], refs[pieces:]
    row_refs, refs = refs[:row_pieces], refs[row_pieces:]
    own_ref, idr_ref, table_ref, mask_ref, gain_ref = refs[:5]
    weights, (res_ref, ups, downs, outs, acc, mlp_in, sems) = refs[5 : 5 + 2 * pieces], refs[5 + 2 * pieces :]
    step = pl.program_id(0)
    share = acc.shape[0]
    half = weights[0].shape[1]
    up = ups.shape[2]
    tail = up + downs.shape[1]
    swap = lambda a: jnp.where(position[0] == 0, a, jnp.concatenate([a[:, half:], a[:, :half]], axis=1))

    def out_copy(i):
        side = slice(i % 2 * half, (i % 2 + 1) * half)
        return pltpu.make_async_copy(weights[i].at[tail:], outs.at[i // 2, :, side], sems.at[i, 0])

    def copies(i):
        side = slice(i % 2 * half, (i % 2 + 1) * half)
        moves = [
            pltpu.make_async_copy(
                weights[i].at[k * half : (k + 1) * half],
                ups.at[i // 2, side, k * half : (k + 1) * half],
                sems.at[i, 1 + k],
            )
            for k in range(up // half)
        ]
        last = sems.at[i, 1 + up // half]
        return moves + [pltpu.make_async_copy(weights[i].at[up:tail], downs.at[i // 2, :, side], last)]

    @pl.when(step == 0)
    def _():
        for i in range(2 * pieces):
            out_copy(i).start()
        for i in range(2 * pieces):
            for copy in copies(i):
                copy.start()
        if share == own_ref.shape[0]:
            ids = own_ref[...]
        elif spread:
            ids = own_ref[pl.ds(pl.multiple_of(first_row + position[1] * share, 16), share), :]
        else:
            ids = own_ref[first_row : first_row + share, :]
        hot = place_hot(ids, table_ref.shape[0])
        place = sum(dot32(hot, part) for part in split2(table_ref[...]))
        match = jnp.where(ids == idr_ref[...], 1.0, 0.0)
        shown = jnp.max(match, axis=1, keepdims=True) > 0.5
        rows = jnp.concatenate([ref[...] for ref in row_refs], axis=0)
        stream = jnp.where(shown, dot32(match.astype(BF), rows), mask_ref[...].astype(F32)) + place
        acc[...] = swap(stream)
        for i in range(pieces):
            out_copy(2 * i).wait()
            out_copy(2 * i + 1).wait()
            acc[...] += dot32(ctx_refs[i][...], outs[i])
        mlp_in[...] = layer_norm(acc[...], swap(gain_ref[...].astype(F32))).astype(BF)

    for i in range(pieces):

        @pl.when(step == i)
        def _(i=i):
            for copy in copies(2 * i) + copies(2 * i + 1):
                copy.wait()

    wide = 256 if up % 256 == 0 else up
    blocks = [slice(k, k + wide) for k in range(0, up, wide)]
    pres = [dot32(mlp_in[...], ups[step, :, span]) for span in blocks]
    added = 0.0
    for pre, span in zip(pres, blocks):
        added += dot32(gelu(pre).astype(BF), downs[step, span, :])
    acc[...] += added

    @pl.when(step == pieces - 1)
    def _():
        if res_ref.shape[0] == share:
            res_ref[...] = swap(acc[...]).astype(res_ref.dtype)
        else:
            acc[...] = swap(acc[...])
            own = pltpu.make_async_copy(acc, res_ref.at[first_row : first_row + share], sems.at[2 * pieces, 0])
            own.start()
            own.wait()


def mlp(position, contexts, all_rows, own_ids, id_row, table, mask_row, gain_row, weights, units, first_row, spread, total):
    pieces = len(weights) // 2
    share = contexts[0].shape[0]
    width = table.shape[1]
    ins = [*contexts, *all_rows, own_ids, id_row, table, mask_row, gain_row]
    out_rows = share if spread else total
    inside = out_rows == share
    return pl.pallas_call(
        functools.partial(mlp_kernel, pieces, len(all_rows), first_row, spread),
        grid=(pieces,),
        in_specs=[SMEM] + [whole(a) for a in ins] + [pl.BlockSpec(memory_space=pl.ANY)] * len(weights),
        out_specs=pl.BlockSpec((share, width), lambda i: (0, 0)) if inside else pl.BlockSpec(memory_space=pl.ANY),
        out_shape=jax.ShapeDtypeStruct((out_rows, width), BF if spread else F32),
        scratch_shapes=[
            pltpu.VMEM((pieces, width, units), BF),
            pltpu.VMEM((pieces, units, width), BF),
            pltpu.VMEM((pieces, contexts[0].shape[1], width), BF),
            pltpu.VMEM((share, width), F32),
            pltpu.VMEM((share, width), BF),
            pltpu.SemaphoreType.DMA((2 * pieces + 1, 2 + units // (width // 2))),
        ],
        compiler_params=PARAMS,
        cost_estimate=pl.CostEstimate(
            flops=30 * share * width * width, bytes_accessed=18 * width * width, transcendentals=4 * share * width
        ),
        name="mlp",
    )(position, *ins, *weights)


def place_kernel(pieces, first_row, position, *refs):
    sources, (_held, out_ref), (sems, *stages) = refs[:pieces], refs[pieces : pieces + 2], refs[pieces + 2 :]

    def move(k):
        count = sources[k].shape[0]
        source = lax.rem(position[1] + (pieces - k), pieces)
        place = pl.ds(pl.multiple_of(first_row + source * count, 16), count)
        return pltpu.make_async_copy(stages[k], out_ref.at[place], sems.at[k])

    for k in range(pieces):
        stages[k][...] = sources[k][...].astype(F32)
        move(k).start()
    for k in range(pieces):
        move(k).wait()


def put_rows(position, decoded, pieces, first_row):
    count = len(pieces)
    return pl.pallas_call(
        functools.partial(place_kernel, count, first_row),
        in_specs=[SMEM] + [pl.BlockSpec(memory_space=pltpu.VMEM)] * count + [pl.BlockSpec(memory_space=pl.ANY)],
        out_specs=pl.BlockSpec(memory_space=pl.ANY),
        out_shape=jax.ShapeDtypeStruct(decoded.shape, decoded.dtype),
        scratch_shapes=[pltpu.SemaphoreType.DMA((count,))] + [pltpu.VMEM(p.shape, F32) for p in pieces],
        input_output_aliases={count + 1: 0},
        compiler_params=PARAMS,
        name="put_rows",
    )(position, *pieces, decoded)


def shards(
    enc_rows,
    vis_index,
    owner_of,
    enc_gain,
    embed_weight,
    mask_token,
    attn_gain,
    qkv_weight,
    out_weight,
    mlp_gain,
    up_weight,
    down_weight,
):
    section = lax.axis_index("section")
    mp_size = lax.axis_size("mp")
    position = jnp.stack([section, lax.axis_index("mp"), lax.axis_index("seq")]).astype(I32)
    patch_total = owner_of.shape[0]
    own_rows = patch_total // lax.axis_size("seq")
    features = mask_token.shape[0]
    half = features // 2
    width = qkv_weight.shape[2]
    heads = width // HD
    slabs = patch_total // CUBE
    places = CUBE + slabs
    vmem = lambda shape, kind: jax.ShapeDtypeStruct(shape, kind)

    embed_other = shifted(embed_weight, "section", 1)
    qkv_mine = qkv_weight.reshape(half, 3 * width)
    qkv_other = shifted(qkv_mine, "section", 1)
    all_ids = jnp.concatenate(gather_pieces(vis_index[0], "seq"))
    embedded = pl.pallas_call(
        embed_kernel,
        in_specs=[SMEM] + [pl.BlockSpec(memory_space=pltpu.VMEM)] * 4,
        out_specs=pl.BlockSpec(memory_space=pltpu.VMEM),
        out_shape=vmem((enc_rows.shape[1], features), BF),
        compiler_params=PARAMS,
        name="embed",
    )(position, enc_rows[0], enc_gain[None, :], embed_weight, embed_other)
    embedded, all_ids = lax.optimization_barrier((embedded, all_ids))
    all_rows = gather_pieces(embedded, "seq")
    id_col = all_ids[:, None]
    id_row = all_ids[None, :]
    visible = all_ids.shape[0]

    table = jnp.asarray(place_table(slabs, features))
    mask_row = mask_token[None, :]
    gain_attn = attn_gain[None, :]
    groups = 3 * heads
    qkv_wide, proj, means, squares = pl.pallas_call(
        functools.partial(table_kernel, groups),
        in_specs=[SMEM] + [pl.BlockSpec(memory_space=pltpu.VMEM)] * 5,
        out_specs=[pl.BlockSpec(memory_space=pltpu.VMEM)] * 4,
        out_shape=[
            vmem((features, groups * LANES), BF),
            vmem((places, groups * LANES), F32),
            vmem((places, LANES), F32),
            vmem((places, LANES), F32),
        ],
        compiler_params=PARAMS,
        name="tables",
    )(position, table, mask_row, gain_attn, qkv_mine, qkv_other)

    padded = patch_total + (-patch_total % KEY_PAD)
    slab_rows = 4 * CUBE
    blocks = -(-padded // slab_rows)
    ins = [proj, means, squares, id_row]
    key_spec = pl.BlockSpec((heads, slab_rows, LANES), lambda i: (0, i, 0))
    km, vm, top = pl.pallas_call(
        functools.partial(masked_kernel, heads, patch_total),
        grid=(blocks,),
        in_specs=[whole(a) for a in ins],
        out_specs=[key_spec, key_spec, pl.BlockSpec((24, LANES), lambda i: (0, 0))],
        out_shape=[vmem((heads, padded, LANES), BF)] * 2 + [vmem((24, LANES), F32)],
        scratch_shapes=[pltpu.VMEM((CUBE, LANES), BF)],
        compiler_params=PARAMS,
        name="masked",
    )(*ins)

    group = HD
    own_ids = pl.pallas_call(
        owned_kernel,
        in_specs=[SMEM, pl.BlockSpec(memory_space=pltpu.VMEM)],
        out_specs=pl.BlockSpec(memory_space=pltpu.VMEM),
        out_shape=vmem((own_rows, 1), I32),
        compiler_params=PARAMS,
        name="owned",
    )(position, owner_of.reshape(patch_total // group, group))

    row_block = 720 if own_rows % 720 == 0 else own_rows
    spaced = visible + (-visible % KEY_PAD)
    ins = [*all_rows, id_col, id_row, own_ids, table, gain_attn, qkv_wide, proj, means, squares, top]
    specs = [whole(a) for a in ins]
    specs[len(all_rows) + 2] = pl.BlockSpec((row_block, 1), lambda i: (jnp.maximum(i - 1, 0), 0))
    kv, vv, q_all = pl.pallas_call(
        functools.partial(queries_kernel, heads, len(all_rows)),
        grid=(1 + own_rows // row_block,),
        in_specs=specs,
        out_specs=[pl.BlockSpec((heads, spaced, LANES), lambda i: (0, 0, 0))] * 2
        + [pl.BlockSpec((heads, row_block, LANES), lambda i: (0, jnp.maximum(i - 1, 0), 0))],
        out_shape=[vmem((heads, spaced, LANES), BF)] * 2 + [vmem((heads, own_rows, LANES), BF)],
        scratch_shapes=[
            pltpu.VMEM((visible, heads * LANES), BF),
            pltpu.VMEM((8 * (-(-(heads + 2) // 8)), LANES), F32),
            pltpu.VMEM((2, places, (heads + 2) * LANES), BF),
        ],
        compiler_params=PARAMS,
        name="queries",
    )(*ins)

    units = up_weight.shape[1]
    packed = jnp.concatenate(
        [up_weight[:, i : i + half] for i in range(0, units, half)] + [down_weight, out_weight], axis=0
    )
    packed, _unused = lax.optimization_barrier((packed, embedded))
    mine = shift_pieces(packed, "mp")

    gain_row = mlp_gain[None, :]
    big = 1536 if own_rows >= 2048 and mp_size > 1 else 0
    rest = own_rows - big
    weights = []

    def pair_weights(after):
        pieces = mine
        if after is not None:
            *pieces, _unused = lax.optimization_barrier((*mine, after))
        for piece in pieces:
            weights.extend([piece, shifted(piece, "section", 1)])

    def finish(contexts, first_row, spread):
        return mlp(
            position, contexts, all_rows, own_ids, id_row, table, mask_row, gain_row, weights, units, first_row, spread, own_rows
        )

    if not big:
        (context,) = attend(position, q_all, km, vm, kv, vv, 0, rest, 1)
        pair_weights(None)
        return finish(shift_pieces(context, "mp"), 0, False)[None]
    parts = attend(position, q_all, km, vm, kv, vv, 0, big, mp_size)
    pair_weights(parts[0])
    exchanged = [part if step == 0 else shifted(part, "mp", step) for step, part in enumerate(parts)]
    (context,) = attend(position, q_all, km, vm, kv, vv, big, rest, 1)
    last = shift_pieces(context, "mp")
    *exchanged, _unused = lax.optimization_barrier((*exchanged, context))
    done = finish(exchanged, 0, True)
    *last, done = lax.optimization_barrier((*last, done))
    pieces = shift_pieces(done, "mp")
    decoded = finish(last, big, False)
    return put_rows(position, decoded, pieces, 0)[None]


def solution(mesh):
    in_specs = (
        P("section", "seq", None),
        P("section", "seq"),
        P(),
        P(),
        P("section", None),
        P(),
        P(),
        P("section", None, "mp"),
        P("mp", "section"),
        P(),
        P("section", "mp"),
        P("mp", "section"),
    )
    out_specs = P("section", "seq", None)
    return jax.shard_map(shards, mesh=mesh, in_specs=in_specs, out_specs=out_specs, check_vma=False)
```

```python
import functools
import math

import jax
import jax.numpy as jnp
import numpy as np
from jax import lax
from jax.experimental import pallas as pl
from jax.experimental.pallas import tpu as pltpu
from jax.sharding import PartitionSpec as P

GX = 6
HD = 64
LANES = 128
KEY_BLOCK = 2048
KEY_PAD = 256
OFF_BIAS = -1e30
HEADROOM = 88.0
WINDOW = 180.0
CUBE = GX * GX * GX
HIGH = lax.Precision.HIGHEST
BF = jnp.bfloat16
F32 = jnp.float32
I32 = jnp.int32
VMEM_LIMIT = 56 * 1024 * 1024
LOG_SCALE = math.log2(math.e) * HD ** (-0.5)
NT = (((1,), (1,)), ((), ()))
PARAMS = pltpu.CompilerParams(vmem_limit_bytes=VMEM_LIMIT)


def layer_norm(values, scales):
    centred = values - jnp.mean(values, axis=-1, keepdims=True)
    spread = jnp.mean(centred * centred, axis=-1, keepdims=True)
    return centred * lax.rsqrt(spread + 1e-06) * scales


def dot32(a, b):
    return jnp.dot(a, b, preferred_element_type=F32)


def split3(values):
    high = values.astype(BF)
    rest = values - high.astype(F32)
    mid = rest.astype(BF)
    return high, mid, (rest - mid.astype(F32)).astype(BF)


def split2(values):
    high = values.astype(BF)
    return high, (values - high.astype(F32)).astype(BF)


def shifted(values, axis, step):
    size = lax.axis_size(axis)
    return lax.ppermute(values, axis, [(i, (i + step) % size) for i in range(size)])


def shift_pieces(values, axis):
    return [values] + [shifted(values, axis, step) for step in range(1, lax.axis_size(axis))]


def gather_pieces(values, axis):
    if lax.axis_size(axis) > 4:
        return [lax.all_gather(values, axis, axis=0, tiled=True)]
    return shift_pieces(values, axis)


def whole(array):
    return pl.BlockSpec(array.shape, lambda *_: (0,) * array.ndim)


SMEM = pl.BlockSpec(memory_space=pltpu.SMEM)


def place_table(slabs, features):
    quarter = features // 4
    frequency = (1.0 / 10000.0 ** (np.arange(quarter // 2, dtype=np.float32) / (quarter // 2))).astype(np.float32)
    angles = np.arange(max(slabs, GX), dtype=np.float32)[:, None] * frequency[None, :]
    codes = np.concatenate([np.sin(angles), np.cos(angles)], axis=1).astype(np.float32)
    place = np.arange(CUBE)
    cube = np.concatenate(
        [codes[place % GX], codes[place // GX % GX], codes[place // (GX * GX)], np.zeros((CUBE, quarter), np.float32)],
        axis=1,
    )
    slab = np.concatenate([np.zeros((slabs, 3 * quarter), np.float32), codes[:slabs]], axis=1)
    return np.concatenate([cube, slab], axis=0)


def embed_kernel(position, rows_ref, gain_ref, mine_ref, other_ref, out_ref):
    normed = layer_norm(rows_ref[...].astype(F32), gain_ref[...].astype(F32)).astype(BF)
    half = normed.shape[1] // 2
    low, high = normed[:, :half], normed[:, half:]
    first = position[0] == 0

    @pl.when(first)
    def _():
        out_ref[...] = (dot32(low, mine_ref[...]) + dot32(high, other_ref[...])).astype(BF)

    @pl.when(jnp.logical_not(first))
    def _():
        out_ref[...] = (dot32(low, other_ref[...]) + dot32(high, mine_ref[...])).astype(BF)


def table_kernel(
    groups, position, table_ref, small_ref, mine_ref, other_ref, weight_ref, proj_ref, sum_ref, square_ref
):
    features = table_ref.shape[1]
    places = table_ref.shape[0]
    first = position[0] == 0
    mine, other = mine_ref[...], other_ref[...]
    full = jnp.concatenate([jnp.where(first, mine, other), jnp.where(first, other, mine)], axis=0)
    gain = small_ref[0:1, :].astype(F32)
    mask = small_ref[1:2, :].astype(F32)
    mask = mask - jnp.mean(mask, axis=1, keepdims=True)
    table = table_ref[...]
    row = lax.broadcasted_iota(I32, table.shape, 0)
    lane = lax.broadcasted_iota(I32, table.shape, 1)
    rows = table + jnp.where(row < CUBE, mask, 0.0)
    gained = jnp.concatenate([rows * gain, jnp.broadcast_to(gain, (16, features))], axis=0)
    proj = sum(dot32(part, full) for part in split3(gained))
    last = lane >= features - features // 4
    squared = jnp.where(row < CUBE, jnp.where(last, 0.0, rows), jnp.where(last, rows + mask, 0.0))
    total = jnp.sum(rows, axis=1, keepdims=True)
    square = jnp.sum(squared * squared, axis=1, keepdims=True)
    column = lax.broadcasted_iota(I32, (1, groups * HD), 1)
    scale = jnp.where(column < groups * HD // 3, LOG_SCALE, 1.0)
    proj = (proj[:places, :] - (total / features) * proj[places : places + 1, :]) * scale
    for group in range(groups):
        span = slice(group * HD, (group + 1) * HD)
        wide = slice(group * LANES, (group + 1) * LANES)
        weight_ref[:, wide] = jnp.concatenate([full[:, span], jnp.zeros((features, HD), BF)], axis=1)
        proj_ref[:, wide] = jnp.concatenate([proj[:, span], jnp.zeros((places, HD), F32)], axis=1)
    sum_ref[...] = jnp.broadcast_to(total / features, sum_ref.shape)
    square_ref[...] = jnp.broadcast_to(square / features, square_ref.shape)


def top_rows(values):
    return jnp.max(values.reshape(values.shape[0] // 8, 8, LANES), axis=0)


def square_sums(values):
    return dot32((values * values).astype(BF), jnp.ones((LANES, LANES), BF))


def masked_kernel(heads, proj_ref, sum_ref, square_ref, ids_ref, km_ref, vm_ref, top_ref, shown):
    step = pl.program_id(0)
    parts = km_ref.shape[1] // CUBE
    lane = lax.broadcasted_iota(I32, (1, LANES), 1)

    @pl.when(step == 0)
    def _():
        ids = ids_ref[...]
        slab = slab_of(ids)
        inner = ids - slab * CUBE
        rows = lax.broadcasted_iota(I32, (CUBE, ids.shape[1]), 0)
        columns = lax.broadcasted_iota(I32, (LANES, ids.shape[1]), 0)
        by_place = jnp.where(rows == inner, 1.0, 0.0).astype(BF)
        by_slab = jnp.where(columns == slab, 1.0, 0.0).astype(BF)
        shown[...] = lax.dot_general(by_place, by_slab, NT, preferred_element_type=F32).astype(BF)
        largest = lambda x: jnp.max(jnp.max(x, axis=0, keepdims=True), axis=1, keepdims=True)
        norms = lambda x: jnp.sqrt(jnp.max(jnp.sum(x * x, axis=1, keepdims=True), axis=0, keepdims=True))
        key_top = jnp.zeros((1, 1), F32)
        value_top = jnp.zeros((1, 1), F32)
        for head in range(heads):
            wide = slice((heads + head) * LANES, (heads + head + 1) * LANES)
            inner, outer = proj_ref[:CUBE, wide], proj_ref[CUBE:, wide]
            middle = jnp.mean(outer, axis=0, keepdims=True)
            key_top = jnp.maximum(key_top, norms(inner + middle) + norms(outer - middle))
            wide = slice((2 * heads + head) * LANES, (2 * heads + head + 1) * LANES)
            value_top = jnp.maximum(value_top, largest(jnp.abs(proj_ref[:CUBE, wide])) + largest(jnp.abs(proj_ref[CUBE:, wide])))
        top_ref[0:8, :] = jnp.zeros((8, LANES), F32)
        top_ref[8:16, :] = jnp.broadcast_to(key_top, (8, LANES))
        top_ref[16:24, :] = jnp.broadcast_to(value_top, (8, LANES))

    value_extra = jnp.where(lane >= HD, 1.0, 0.0)
    scales = []
    extras = []
    slab_rows = []
    for part in range(parts):
        slab = step * parts + part
        row = CUBE + slab
        slab_rows.append(proj_ref[pl.ds(row, 1), :])
        mean = sum_ref[:CUBE, :] + sum_ref[pl.ds(row, 1), :]
        spread = square_ref[:CUBE, :] + square_ref[pl.ds(row, 1), :] - mean * mean
        scales.append(lax.rsqrt(spread + 1e-06))
        pick = (lax.broadcasted_iota(I32, (LANES, LANES), 0) == slab) & (
            lax.broadcasted_iota(I32, (LANES, LANES), 1) == HD
        )
        key_extra = dot32(shown[...], jnp.where(pick, OFF_BIAS, 0.0).astype(BF))
        extras.append(key_extra + jnp.where((lane > HD) & (lane < HD + 4), 1.0, 0.0))
    for scale in scales:
        top_ref[0:8, :] = jnp.maximum(top_ref[0:8, :], top_rows(scale))
    scale = jnp.concatenate(scales, axis=0)
    key_extra = jnp.concatenate(extras, axis=0)
    for head in range(heads):
        for first, extra, target in ((heads, key_extra, km_ref), (2 * heads, value_extra, vm_ref)):
            wide = slice((first + head) * LANES, (first + head + 1) * LANES)
            block = jnp.concatenate([proj_ref[:CUBE, wide] + row[:, wide] for row in slab_rows], axis=0)
            target[head] = (block * scale + extra).astype(BF)


def owned_kernel(seq_ref, owner_ref, ids_ref):
    groups, size = owner_ref.shape
    rows = ids_ref.shape[0]
    flags = jnp.where(owner_ref[...] == seq_ref[2], 1.0, 0.0).astype(BF)

    def upper(count):
        shape = (count, count)
        return jnp.where(lax.broadcasted_iota(I32, shape, 0) <= lax.broadcasted_iota(I32, shape, 1), 1.0, 0.0).astype(BF)

    local = dot32(flags, upper(size))
    totals = lax.dot_general(jnp.ones((8, size), BF), flags, NT, preferred_element_type=F32)
    ends = dot32(totals.astype(BF), upper(groups))
    begins = (ends - totals)[0:1, :]
    ends = ends[0:1, :]
    slot = lax.broadcasted_iota(I32, (rows, 1), 0).astype(F32)
    group = jnp.sum(jnp.where(ends <= slot, 1.0, 0.0), axis=1, keepdims=True)
    lane = lax.broadcasted_iota(I32, (rows, groups), 1).astype(F32)
    hot = jnp.where(lane == group, 1.0, 0.0)
    begin = jnp.sum(hot * begins, axis=1, keepdims=True)
    counts = dot32(hot.astype(BF), local.astype(BF))
    within = jnp.sum(jnp.where(counts <= slot - begin, 1.0, 0.0), axis=1, keepdims=True)
    ids_ref[...] = (group * size + within).astype(I32)


def slab_of(ids):
    return jnp.floor((ids.astype(F32) + 0.5) * (1.0 / CUBE)).astype(I32)


def place_hot(ids, places):
    lane = lax.broadcasted_iota(I32, (ids.shape[0], places), 1)
    slab = slab_of(ids)
    inner = ids - slab * CUBE
    return jnp.where((lane == inner) | (lane == slab + CUBE), 1.0, 0.0).astype(BF)


def queries_kernel(heads, pieces, *refs):
    queries_body(heads, refs[:pieces], *refs[pieces:])


def queries_body(
    heads, row_refs, idr_ref, own_ref, table_ref, small_ref, weight_ref, proj_ref, sum_ref, square_ref, top_ref,
    kv_ref, vv_ref, q_ref, seen_q, bounds, tables,
):
    step = pl.program_id(0)
    wide = heads * LANES

    @pl.when(step == 0)
    def _():
        count = idr_ref.shape[1]
        square = (count, count)
        here = lax.broadcasted_iota(I32, square, 0) == lax.broadcasted_iota(I32, square, 1)
        ids = jnp.sum(jnp.where(here, idr_ref[...].astype(F32), 0.0), axis=1, keepdims=True)
        rows = jnp.concatenate([ref[...].astype(F32) for ref in row_refs], axis=0)
        hot = place_hot(ids.astype(I32), table_ref.shape[0])
        place = sum(dot32(hot, part) for part in split2(table_ref[...]))
        seen = layer_norm(rows + place, small_ref[0:1, :].astype(F32)).astype(BF)
        seen_q[...] = (dot32(seen, weight_ref[:, :wide]) * LOG_SCALE).astype(BF)
        both = dot32(seen, weight_ref[:, wide:])
        lane = lax.broadcasted_iota(I32, (1, LANES), 1)
        extra = jnp.where((lane > HD) & (lane < HD + 4), 1.0, 0.0)
        ones = jnp.where(lane >= HD, 1.0, 0.0)
        scale = jnp.max(top_ref[0:8, :], axis=0, keepdims=True)
        scale = jnp.max(scale, axis=1, keepdims=True)
        masked_key = scale * top_ref[8:9, :]
        top = jnp.zeros((8, LANES), F32)
        high = scale * top_ref[16:24, :]
        spare = kv_ref.shape[1] - count
        for head in range(heads):
            keys = both[:, head * LANES : (head + 1) * LANES]
            top = jnp.maximum(top, top_rows(square_sums(keys)))
            middle = jnp.mean(keys, axis=0, keepdims=True)
            middle = jnp.sum(middle * middle, axis=1, keepdims=True)
            bounds[head : head + 1, :] = jnp.broadcast_to(jnp.sqrt(middle) * 1.03, (1, LANES))
            kv_ref[head, :count, :] = (keys + extra).astype(BF)
            values = both[:, (heads + head) * LANES : (heads + head + 1) * LANES]
            high = jnp.maximum(high, top_rows(jnp.abs(values)))
            vv_ref[head, :count, :] = (values + ones).astype(BF)
            if spare:
                off = lax.broadcasted_iota(I32, (spare, LANES), 1) == HD
                kv_ref[head, count:, :] = jnp.where(off, OFF_BIAS, 0.0).astype(BF)
                vv_ref[head, count:, :] = jnp.ones((spare, LANES), BF)
        seen_key = jnp.sqrt(jnp.max(top, axis=0, keepdims=True))
        bounds[heads : heads + 1, :] = jnp.maximum(seen_key, masked_key) * 1.03
        largest = jnp.max(jnp.max(high, axis=0, keepdims=True), axis=1, keepdims=True)
        bounds[heads + 1 : heads + 2, :] = jnp.broadcast_to(largest, (1, LANES))
        joined = jnp.concatenate([proj_ref[:, :wide], sum_ref[...], square_ref[...]], axis=1)
        for i, part in enumerate(split2(joined)):
            tables[i] = part

    @pl.when(step > 0)
    def _():
        ids = own_ref[...]
        count = ids.shape[0]
        hot = place_hot(ids, table_ref.shape[0])
        mixed = dot32(hot, tables[0]) + dot32(hot, tables[1])
        mean = mixed[:, wide : wide + LANES]
        scale = lax.rsqrt(mixed[:, wide + LANES :] - mean * mean + 1e-06)
        match = jnp.where(ids == idr_ref[...], 1.0, 0.0)
        shown = jnp.max(match, axis=1, keepdims=True) > 0.5
        picked = dot32(match.astype(BF), seen_q[...])
        lane = lax.broadcasted_iota(I32, (count, LANES), 1)
        limit = bounds[heads : heads + 1, :]
        fine = bounds[heads + 1 : heads + 2, :] < 2.0**25
        for head in range(heads):
            span = slice(head * LANES, (head + 1) * LANES)
            part = jnp.where(shown, picked[:, span], scale * mixed[:, span])
            norm = jnp.sqrt(square_sums(part))
            ceiling = norm * limit
            slack = jnp.where(fine, ceiling + norm * bounds[head : head + 1, :], 1e30)
            extra = jnp.where(lane == HD, 1.0, jnp.where(lane == HD + 1, HEADROOM - ceiling, 0.0))
            extra = jnp.where(lane == HD + 4, slack, extra)
            q_ref[head] = jnp.where(lane < HD, part, extra).astype(BF)


def attend_kernel(offset, rows, pieces, position, q_ref, km_ref, vm_ref, kv_ref, vv_ref, *refs):
    outs, (q_scr, acc, ctx, p_even, p_odd) = refs[:pieces], refs[pieces:]
    head = pl.program_id(0)
    q_scr[...] = q_ref[0, offset : offset + rows, :]
    block = p_even.shape[1]
    steps = km_ref.shape[1] // block
    rest = km_ref.shape[1] - steps * block
    tails = [(km_ref, vm_ref, steps * block, rest)] if rest else []
    visible = kv_ref.shape[1]
    tails += [(kv_ref, vv_ref, i, min(block, visible - i)) for i in range(0, visible, block)]

    def keys_of(i):
        if isinstance(i, int) and i >= steps:
            keys, _, start, size = tails[i - steps]
            return keys[0, start : start + size, :]
        return km_ref[0, pl.ds(i * block, block), :]

    def values_of(i):
        if isinstance(i, int) and i >= steps:
            _, values, start, size = tails[i - steps]
            return values[0, start : start + size, :]
        return vm_ref[0, pl.ds(i * block, block), :]

    def scores(i):
        return lax.dot_general(q_scr[...], keys_of(i), NT, preferred_element_type=F32)

    total = steps + len(tails)
    lane = lax.broadcasted_iota(I32, (rows, LANES), 1)
    slack = jnp.max(jnp.where(lane == HD + 4, q_scr[...].astype(F32), -1e30))

    @pl.when(jnp.logical_not(slack <= WINDOW))
    def _():
        q_scr[...] = jnp.where(lane > HD, 0.0, q_scr[...].astype(F32)).astype(BF)

        def look(i, best):
            return jnp.maximum(best, jnp.max(scores(i), axis=1, keepdims=True))

        peak = lax.fori_loop(0, steps, look, jnp.full((rows, 1), -3e38, F32))
        for i in range(steps, total):
            peak = look(i, peak)
        high, mid, low = split3(peak)
        new = jnp.where(lane == HD + 1, -high.astype(F32), q_scr[...].astype(F32))
        new = jnp.where(lane == HD + 2, -mid.astype(F32), new)
        new = jnp.where(lane == HD + 3, -low.astype(F32), new)
        q_scr[...] = new.astype(BF)

    def width_of(i):
        return tails[i - steps][3] if isinstance(i, int) and i >= steps else block

    def weigh(i, target):
        target[:, : width_of(i)] = jnp.exp2(scores(i)).astype(BF)

    def add(weights, i):
        acc[...] += dot32(weights[:, : width_of(i)], values_of(i))

    acc[...] = jnp.zeros_like(acc)
    slots = (p_even, p_odd)
    weigh(0, p_even)

    def body(j, carry):
        i = 2 * j + 1
        weigh(i, p_odd)
        add(p_even, i - 1)
        weigh(i + 1, p_even)
        add(p_odd, i)
        return carry

    pairs = (steps - 1) // 2
    lax.fori_loop(0, pairs, body, 0)
    for i in range(1 + 2 * pairs, total + 1):
        if i < total:
            weigh(i, slots[i % 2])
        add(slots[1 - i % 2], i - 1)
    totals = acc[...]
    ctx[head] = totals[:, :HD] / totals[:, HD:]

    @pl.when(head == pl.num_programs(0) - 1)
    def _():
        for step, out in enumerate(outs):
            target = lax.rem(position[1] + step, pieces)
            span = pl.ds(pl.multiple_of(target * (rows // pieces), 16), rows // pieces) if pieces > 1 else slice(None)
            out[...] = jnp.concatenate([ctx[i, span, :] for i in range(ctx.shape[0])], axis=1).astype(BF)


def attend(position, q_all, km, vm, kv, vv, offset, rows, pieces):
    heads, total, _ = q_all.shape
    masked, visible = km.shape[1], kv.shape[1]
    per_head = lambda size: pl.BlockSpec((1, size, LANES), lambda h: (h, 0, 0))
    shape = (rows // pieces, heads * HD)
    block = min(KEY_BLOCK, masked)
    return pl.pallas_call(
        functools.partial(attend_kernel, offset, rows, pieces),
        grid=(heads,),
        in_specs=[SMEM, per_head(total), per_head(masked), per_head(masked), per_head(visible), per_head(visible)],
        out_specs=[pl.BlockSpec(shape, lambda h: (0, 0))] * pieces,
        out_shape=[jax.ShapeDtypeStruct(shape, BF)] * pieces,
        scratch_shapes=[
            pltpu.VMEM((rows, LANES), BF),
            pltpu.VMEM((rows, LANES), F32),
            pltpu.VMEM((heads, rows, HD), F32),
            pltpu.VMEM((rows, block), BF),
            pltpu.VMEM((rows, block), BF),
        ],
        compiler_params=PARAMS,
        cost_estimate=pl.CostEstimate(
            flops=8 * heads * rows * (masked + visible) * LANES,
            bytes_accessed=4 * heads * masked * LANES,
            transcendentals=heads * rows * masked,
        ),
        name="attend",
    )(position, q_all, km, vm, kv, vv)


def gelu(x):
    size = jnp.abs(x)
    base = 1.0 + 0.2316419 * size
    t = pl.reciprocal(base, approx=True)
    t = t * (2.0 - base * t)
    poly = 0.5307027145
    for c in (-0.7265760135, 0.7107068705, -0.142248368, 0.127414796):
        poly = poly * t + c
    tail = poly * t * jnp.exp2(x * x * (-0.5 * math.log2(math.e)))
    return x * jnp.where(x < 0.0, tail, 1.0 - tail)


def mlp_kernel(pieces, row_pieces, layout, first_row, spread, position, *refs):
    ctx_refs, refs = refs[:pieces], refs[pieces:]
    row_refs, refs = refs[:row_pieces], refs[row_pieces:]
    own_ref, idr_ref, table_ref, small_ref = refs[:4]
    sources, (res_ref, ups, downs, outs, acc, mlp_in, sems) = refs[4:-7], refs[-7:]
    weights = [sources[k].at[j] for k, j in layout]
    step = pl.program_id(0)
    share = acc.shape[0]
    half = weights[0].shape[1]
    up = ups.shape[2]
    tail = up + downs.shape[1]
    swap = lambda a: jnp.where(position[0] == 0, a, jnp.concatenate([a[:, half:], a[:, :half]], axis=1))

    def out_copy(i):
        side = slice(i % 2 * half, (i % 2 + 1) * half)
        return pltpu.make_async_copy(weights[i].at[tail:], outs.at[i // 2, :, side], sems.at[i, 0])

    def copies(i):
        side = slice(i % 2 * half, (i % 2 + 1) * half)
        moves = [
            pltpu.make_async_copy(
                weights[i].at[k * half : (k + 1) * half],
                ups.at[i // 2, side, k * half : (k + 1) * half],
                sems.at[i, 1 + k],
            )
            for k in range(up // half)
        ]
        last = sems.at[i, 1 + up // half]
        return moves + [pltpu.make_async_copy(weights[i].at[up:tail], downs.at[i // 2, :, side], last)]

    @pl.when(step == 0)
    def _():
        for i in range(2 * pieces):
            out_copy(i).start()
        for i in range(2 * pieces):
            for copy in copies(i):
                copy.start()
        if share == own_ref.shape[0]:
            ids = own_ref[...]
        elif spread:
            ids = own_ref[pl.ds(pl.multiple_of(first_row + position[1] * share, 16), share), :]
        else:
            ids = own_ref[first_row : first_row + share, :]
        hot = place_hot(ids, table_ref.shape[0])
        place = sum(dot32(hot, part) for part in split2(table_ref[...]))
        match = jnp.where(ids == idr_ref[...], 1.0, 0.0)
        shown = jnp.max(match, axis=1, keepdims=True) > 0.5
        rows = jnp.concatenate([ref[...] for ref in row_refs], axis=0)
        stream = jnp.where(shown, dot32(match.astype(BF), rows), small_ref[1:2, :].astype(F32)) + place
        acc[...] = swap(stream)
        for i in range(pieces):
            out_copy(2 * i).wait()
            out_copy(2 * i + 1).wait()
            acc[...] += dot32(ctx_refs[i][...], outs[i])
        mlp_in[...] = layer_norm(acc[...], swap(small_ref[2:3, :].astype(F32))).astype(BF)

    for i in range(pieces):

        @pl.when(step == i)
        def _(i=i):
            for copy in copies(2 * i) + copies(2 * i + 1):
                copy.wait()

    wide = 256 if up % 256 == 0 else up
    blocks = [slice(k, k + wide) for k in range(0, up, wide)]
    pres = [dot32(mlp_in[...], ups[step, :, span]) for span in blocks]
    added = 0.0
    for pre, span in zip(pres, blocks):
        added += dot32(gelu(pre).astype(BF), downs[step, span, :])
    acc[...] += added

    @pl.when(step == pieces - 1)
    def _():
        if res_ref.shape[0] == share:
            res_ref[...] = swap(acc[...]).astype(res_ref.dtype)
        else:
            acc[...] = swap(acc[...])
            own = pltpu.make_async_copy(acc, res_ref.at[first_row : first_row + share], sems.at[2 * pieces, 0])
            own.start()
            own.wait()


def mlp(position, contexts, all_rows, own_ids, id_row, table, small, mine, others, units, first_row, spread, total):
    pieces = len(mine)
    weights = [*mine, *others]
    layout = [(k, j) for k, w in enumerate(weights) for j in range(w.shape[0])]
    layout = [layout[i // 2 + i % 2 * pieces] for i in range(2 * pieces)]
    share = contexts[0].shape[0]
    width = table.shape[1]
    ins = [*contexts, *all_rows, own_ids, id_row, table, small]
    out_rows = share if spread else total
    inside = out_rows == share
    return pl.pallas_call(
        functools.partial(mlp_kernel, pieces, len(all_rows), layout, first_row, spread),
        grid=(pieces,),
        in_specs=[SMEM] + [whole(a) for a in ins] + [pl.BlockSpec(memory_space=pl.ANY)] * len(weights),
        out_specs=pl.BlockSpec((share, width), lambda i: (0, 0)) if inside else pl.BlockSpec(memory_space=pl.ANY),
        out_shape=jax.ShapeDtypeStruct((out_rows, width), BF if spread else F32),
        scratch_shapes=[
            pltpu.VMEM((pieces, width, units), BF),
            pltpu.VMEM((pieces, units, width), BF),
            pltpu.VMEM((pieces, contexts[0].shape[1], width), BF),
            pltpu.VMEM((share, width), F32),
            pltpu.VMEM((share, width), BF),
            pltpu.SemaphoreType.DMA((2 * pieces + 1, 2 + units // (width // 2))),
        ],
        compiler_params=PARAMS,
        cost_estimate=pl.CostEstimate(
            flops=30 * share * width * width, bytes_accessed=18 * width * width, transcendentals=4 * share * width
        ),
        name="mlp",
    )(position, *ins, *weights)


def place_kernel(pieces, first_row, position, *refs):
    sources, (_held, out_ref), (sems, *stages) = refs[:pieces], refs[pieces : pieces + 2], refs[pieces + 2 :]

    def move(k):
        count = sources[k].shape[0]
        source = lax.rem(position[1] + (pieces - k), pieces)
        place = pl.ds(pl.multiple_of(first_row + source * count, 16), count)
        return pltpu.make_async_copy(stages[k], out_ref.at[place], sems.at[k])

    for k in range(pieces):
        stages[k][...] = sources[k][...].astype(F32)
        move(k).start()
    for k in range(pieces):
        move(k).wait()


def put_rows(position, decoded, pieces, first_row):
    count = len(pieces)
    return pl.pallas_call(
        functools.partial(place_kernel, count, first_row),
        in_specs=[SMEM] + [pl.BlockSpec(memory_space=pltpu.VMEM)] * count + [pl.BlockSpec(memory_space=pl.ANY)],
        out_specs=pl.BlockSpec(memory_space=pl.ANY),
        out_shape=jax.ShapeDtypeStruct(decoded.shape, decoded.dtype),
        scratch_shapes=[pltpu.SemaphoreType.DMA((count,))] + [pltpu.VMEM(p.shape, F32) for p in pieces],
        input_output_aliases={count + 1: 0},
        compiler_params=PARAMS,
        name="put_rows",
    )(position, *pieces, decoded)


def shards(
    enc_rows,
    vis_index,
    owner_of,
    enc_gain,
    embed_weight,
    mask_token,
    attn_gain,
    qkv_weight,
    out_weight,
    mlp_gain,
    up_weight,
    down_weight,
):
    section = lax.axis_index("section")
    mp_size = lax.axis_size("mp")
    position = jnp.stack([section, lax.axis_index("mp"), lax.axis_index("seq")]).astype(I32)
    patch_total = owner_of.shape[0]
    own_rows = patch_total // lax.axis_size("seq")
    features = mask_token.shape[0]
    half = features // 2
    width = qkv_weight.shape[2]
    heads = width // HD
    slabs = patch_total // CUBE
    places = CUBE + slabs
    vmem = lambda shape, kind: jax.ShapeDtypeStruct(shape, kind)

    embed_other = shifted(embed_weight, "section", 1)
    qkv_mine = qkv_weight.reshape(half, 3 * width)
    qkv_other = shifted(qkv_mine, "section", 1)
    all_ids = gather_pieces(vis_index, "seq")
    embedded = pl.pallas_call(
        embed_kernel,
        in_specs=[SMEM] + [pl.BlockSpec(memory_space=pltpu.VMEM)] * 4,
        out_specs=pl.BlockSpec(memory_space=pltpu.VMEM),
        out_shape=vmem((enc_rows.shape[1], features), BF),
        compiler_params=PARAMS,
        name="embed",
    )(position, enc_rows[0], enc_gain[None, :], embed_weight, embed_other)
    embedded, *all_ids = lax.optimization_barrier((embedded, *all_ids))
    all_rows = gather_pieces(embedded, "seq")
    id_row = jnp.concatenate([a.reshape(1, -1) for a in all_ids], axis=1)
    visible = id_row.shape[1]

    table = jnp.asarray(place_table(slabs, features))
    small = jnp.stack([attn_gain, mask_token, mlp_gain])
    groups = 3 * heads
    qkv_wide, proj, means, squares = pl.pallas_call(
        functools.partial(table_kernel, groups),
        in_specs=[SMEM] + [pl.BlockSpec(memory_space=pltpu.VMEM)] * 4,
        out_specs=[pl.BlockSpec(memory_space=pltpu.VMEM)] * 4,
        out_shape=[
            vmem((features, groups * LANES), BF),
            vmem((places, groups * LANES), F32),
            vmem((places, LANES), F32),
            vmem((places, LANES), F32),
        ],
        compiler_params=PARAMS,
        name="tables",
    )(position, table, small, qkv_mine, qkv_other)

    blocks = 4 if slabs % 4 == 0 and patch_total % 64 == 0 else 1
    slab_rows = patch_total // blocks
    ins = [proj, means, squares, id_row]
    key_spec = pl.BlockSpec((heads, slab_rows, LANES), lambda i: (0, i, 0))
    km, vm, top = pl.pallas_call(
        functools.partial(masked_kernel, heads),
        grid=(blocks,),
        in_specs=[whole(a) for a in ins],
        out_specs=[key_spec, key_spec, pl.BlockSpec((24, LANES), lambda i: (0, 0))],
        out_shape=[vmem((heads, patch_total, LANES), BF)] * 2 + [vmem((24, LANES), F32)],
        scratch_shapes=[pltpu.VMEM((CUBE, LANES), BF)],
        compiler_params=PARAMS,
        name="masked",
    )(*ins)

    group = HD
    own_ids = pl.pallas_call(
        owned_kernel,
        in_specs=[SMEM, pl.BlockSpec(memory_space=pltpu.VMEM)],
        out_specs=pl.BlockSpec(memory_space=pltpu.VMEM),
        out_shape=vmem((own_rows, 1), I32),
        compiler_params=PARAMS,
        name="owned",
    )(position, owner_of.reshape(patch_total // group, group))

    row_block = 720 if own_rows % 720 == 0 else own_rows
    spaced = visible + (-visible % KEY_PAD)
    ins = [*all_rows, id_row, own_ids, table, small, qkv_wide, proj, means, squares, top]
    specs = [whole(a) for a in ins]
    specs[len(all_rows) + 1] = pl.BlockSpec((row_block, 1), lambda i: (jnp.maximum(i - 1, 0), 0))
    kv, vv, q_all = pl.pallas_call(
        functools.partial(queries_kernel, heads, len(all_rows)),
        grid=(1 + own_rows // row_block,),
        in_specs=specs,
        out_specs=[pl.BlockSpec((heads, spaced, LANES), lambda i: (0, 0, 0))] * 2
        + [pl.BlockSpec((heads, row_block, LANES), lambda i: (0, jnp.maximum(i - 1, 0), 0))],
        out_shape=[vmem((heads, spaced, LANES), BF)] * 2 + [vmem((heads, own_rows, LANES), BF)],
        scratch_shapes=[
            pltpu.VMEM((visible, heads * LANES), BF),
            pltpu.VMEM((8 * (-(-(heads + 2) // 8)), LANES), F32),
            pltpu.VMEM((2, places, (heads + 2) * LANES), BF),
        ],
        compiler_params=PARAMS,
        name="queries",
    )(*ins)

    units = up_weight.shape[1]
    packed = jnp.concatenate(
        [up_weight[:, i : i + half] for i in range(0, units, half)] + [down_weight, out_weight], axis=0
    )
    packed, _unused = lax.optimization_barrier((packed, embedded))
    packed_other = shifted(packed, "section", 1)
    mine = shift_pieces(packed, "mp")

    big = 1408 if own_rows >= 2048 and mp_size > 1 else 0
    rest = own_rows - big

    q_all, packed_other = lax.optimization_barrier((q_all, packed_other))

    def pair_weights(after):
        pieces = mine
        if after is not None:
            *pieces, _unused = lax.optimization_barrier((*mine, after))
        others = [packed_other[None]]
        for i in range(1, len(pieces), 2):
            others.append(shifted(jnp.stack(pieces[i : i + 2]), "section", 1))
        return [p[None] for p in pieces], others

    def finish(weights, contexts, first_row, spread):
        return mlp(position, contexts, all_rows, own_ids, id_row, table, small, *weights, units, first_row, spread, own_rows)

    if not big:
        (context,) = attend(position, q_all, km, vm, kv, vv, 0, rest, 1)
        return finish(pair_weights(None), shift_pieces(context, "mp"), 0, False)[None]
    parts = attend(position, q_all, km, vm, kv, vv, 0, big, mp_size)
    weights = pair_weights(parts[0])
    exchanged = [part if step == 0 else shifted(part, "mp", step) for step, part in enumerate(parts)]
    (context,) = attend(position, q_all, km, vm, kv, vv, big, rest, 1)
    last = shift_pieces(context, "mp")
    *exchanged, _unused = lax.optimization_barrier((*exchanged, context))
    done = finish(weights, exchanged, 0, True)
    *last, done = lax.optimization_barrier((*last, done))
    pieces = shift_pieces(done, "mp")
    decoded = finish(weights, last, big, False)
    return put_rows(position, decoded, pieces, 0)[None]


def solution(mesh):
    in_specs = (
        P("section", "seq", None),
        P("section", "seq"),
        P(),
        P(),
        P("section", None),
        P(),
        P(),
        P("section", None, "mp"),
        P("mp", "section"),
        P(),
        P("section", "mp"),
        P("mp", "section"),
    )
    out_specs = P("section", "seq", None)
    return jax.shard_map(shards, mesh=mesh, in_specs=in_specs, out_specs=out_specs, check_vma=False)
```

```python
import functools
import math

import jax
import jax.numpy as jnp
import numpy as np
from jax import lax
from jax.experimental import pallas as pl
from jax.experimental.pallas import tpu as pltpu
from jax.sharding import PartitionSpec as P

GX = 6
HD = 64
LANES = 128
KEY_BLOCK = 2048
KEY_PAD = 256
OFF_BIAS = -1e30
HEADROOM = 88.0
WINDOW = 180.0
CUBE = GX * GX * GX
HIGH = lax.Precision.HIGHEST
BF = jnp.bfloat16
F32 = jnp.float32
I32 = jnp.int32
MIB = 1024 * 1024
LOG_SCALE = math.log2(math.e) * HD ** (-0.5)
NT = (((1,), (1,)), ((), ()))


def vmem_limit(mib):
    return pltpu.CompilerParams(vmem_limit_bytes=mib * MIB)


def layer_norm(values, scales):
    centred = values - jnp.mean(values, axis=-1, keepdims=True)
    spread = jnp.mean(centred * centred, axis=-1, keepdims=True)
    return centred * lax.rsqrt(spread + 1e-06) * scales


def dot32(a, b):
    return jnp.dot(a, b, preferred_element_type=F32)


def split3(values):
    high = values.astype(BF)
    rest = values - high.astype(F32)
    mid = rest.astype(BF)
    return high, mid, (rest - mid.astype(F32)).astype(BF)


def split2(values):
    high = values.astype(BF)
    return high, (values - high.astype(F32)).astype(BF)


def shifted(values, axis, step):
    size = lax.axis_size(axis)
    return lax.ppermute(values, axis, [(i, (i + step) % size) for i in range(size)])


def shift_pieces(values, axis):
    return [values] + [shifted(values, axis, step) for step in range(1, lax.axis_size(axis))]


def gather_pieces(values, axis):
    if lax.axis_size(axis) > 4:
        return [lax.all_gather(values, axis, axis=0, tiled=True)]
    return shift_pieces(values, axis)


def whole(array):
    return pl.BlockSpec(array.shape, lambda *_: (0,) * array.ndim)


SMEM = pl.BlockSpec(memory_space=pltpu.SMEM)


def place_table(slabs, features):
    quarter = features // 4
    frequency = (1.0 / 10000.0 ** (np.arange(quarter // 2, dtype=np.float32) / (quarter // 2))).astype(np.float32)
    angles = np.arange(max(slabs, GX), dtype=np.float32)[:, None] * frequency[None, :]
    codes = np.concatenate([np.sin(angles), np.cos(angles)], axis=1).astype(np.float32)
    place = np.arange(CUBE)
    cube = np.concatenate(
        [codes[place % GX], codes[place // GX % GX], codes[place // (GX * GX)], np.zeros((CUBE, quarter), np.float32)],
        axis=1,
    )
    slab = np.concatenate([np.zeros((slabs, 3 * quarter), np.float32), codes[:slabs]], axis=1)
    return np.concatenate([cube, slab], axis=0)


def embed_kernel(position, rows_ref, gain_ref, mine_ref, other_ref, out_ref):
    normed = layer_norm(rows_ref[...].astype(F32), gain_ref[...].astype(F32)).astype(BF)
    half = normed.shape[1] // 2
    low, high = normed[:, :half], normed[:, half:]
    first = position[0] == 0

    @pl.when(first)
    def _():
        out_ref[...] = (dot32(low, mine_ref[...]) + dot32(high, other_ref[...])).astype(BF)

    @pl.when(jnp.logical_not(first))
    def _():
        out_ref[...] = (dot32(low, other_ref[...]) + dot32(high, mine_ref[...])).astype(BF)


def table_kernel(
    groups, position, table_ref, small_ref, mine_ref, other_ref, weight_ref, proj_ref, sum_ref, square_ref
):
    features = table_ref.shape[1]
    places = table_ref.shape[0]
    first = position[0] == 0
    mine, other = mine_ref[...], other_ref[...]
    full = jnp.concatenate([jnp.where(first, mine, other), jnp.where(first, other, mine)], axis=0)
    gain = small_ref[0:1, :].astype(F32)
    mask = small_ref[1:2, :].astype(F32)
    mask = mask - jnp.mean(mask, axis=1, keepdims=True)
    table = table_ref[...]
    row = lax.broadcasted_iota(I32, table.shape, 0)
    lane = lax.broadcasted_iota(I32, table.shape, 1)
    rows = table + jnp.where(row < CUBE, mask, 0.0)
    gained = jnp.concatenate([rows * gain, jnp.broadcast_to(gain, (16, features))], axis=0)
    proj = sum(dot32(part, full) for part in split3(gained))
    last = lane >= features - features // 4
    squared = jnp.where(row < CUBE, jnp.where(last, 0.0, rows), jnp.where(last, rows + mask, 0.0))
    total = jnp.sum(rows, axis=1, keepdims=True)
    square = jnp.sum(squared * squared, axis=1, keepdims=True)
    column = lax.broadcasted_iota(I32, (1, groups * HD), 1)
    scale = jnp.where(column < groups * HD // 3, LOG_SCALE, 1.0)
    proj = (proj[:places, :] - (total / features) * proj[places : places + 1, :]) * scale
    for group in range(groups):
        span = slice(group * HD, (group + 1) * HD)
        wide = slice(group * LANES, (group + 1) * LANES)
        weight_ref[:, wide] = jnp.concatenate([full[:, span], jnp.zeros((features, HD), BF)], axis=1)
        proj_ref[:, wide] = jnp.concatenate([proj[:, span], jnp.zeros((places, HD), F32)], axis=1)
    sum_ref[...] = jnp.broadcast_to(total / features, sum_ref.shape)
    square_ref[...] = jnp.broadcast_to(square / features, square_ref.shape)


def top_rows(values):
    return jnp.max(values.reshape(values.shape[0] // 8, 8, LANES), axis=0)


def square_sums(values):
    return dot32((values * values).astype(BF), jnp.ones((LANES, LANES), BF))


def masked_kernel(heads, proj_ref, sum_ref, square_ref, ids_ref, km_ref, vm_ref, top_ref, shown):
    step = pl.program_id(0)
    parts = km_ref.shape[1] // CUBE
    lane = lax.broadcasted_iota(I32, (1, LANES), 1)

    @pl.when(step == 0)
    def _():
        ids = ids_ref[...]
        slab = slab_of(ids)
        inner = ids - slab * CUBE
        rows = lax.broadcasted_iota(I32, (CUBE, ids.shape[1]), 0)
        columns = lax.broadcasted_iota(I32, (LANES, ids.shape[1]), 0)
        by_place = jnp.where(rows == inner, 1.0, 0.0).astype(BF)
        by_slab = jnp.where(columns == slab, 1.0, 0.0).astype(BF)
        shown[...] = lax.dot_general(by_place, by_slab, NT, preferred_element_type=F32).astype(BF)
        largest = lambda x: jnp.max(jnp.max(x, axis=0, keepdims=True), axis=1, keepdims=True)
        norms = lambda x: jnp.sqrt(jnp.max(jnp.sum(x * x, axis=1, keepdims=True), axis=0, keepdims=True))
        key_top = jnp.zeros((1, 1), F32)
        value_top = jnp.zeros((1, 1), F32)
        for head in range(heads):
            wide = slice((heads + head) * LANES, (heads + head + 1) * LANES)
            inner, outer = proj_ref[:CUBE, wide], proj_ref[CUBE:, wide]
            middle = jnp.mean(outer, axis=0, keepdims=True)
            key_top = jnp.maximum(key_top, norms(inner + middle) + norms(outer - middle))
            wide = slice((2 * heads + head) * LANES, (2 * heads + head + 1) * LANES)
            value_top = jnp.maximum(value_top, largest(jnp.abs(proj_ref[:CUBE, wide])) + largest(jnp.abs(proj_ref[CUBE:, wide])))
        top_ref[0:8, :] = jnp.zeros((8, LANES), F32)
        top_ref[8:16, :] = jnp.broadcast_to(key_top, (8, LANES))
        top_ref[16:24, :] = jnp.broadcast_to(value_top, (8, LANES))

    value_extra = jnp.where(lane >= HD, 1.0, 0.0)
    scales = []
    extras = []
    slab_rows = []
    for part in range(parts):
        slab = step * parts + part
        row = CUBE + slab
        slab_rows.append(proj_ref[pl.ds(row, 1), :])
        mean = sum_ref[:CUBE, :] + sum_ref[pl.ds(row, 1), :]
        spread = square_ref[:CUBE, :] + square_ref[pl.ds(row, 1), :] - mean * mean
        scales.append(lax.rsqrt(spread + 1e-06))
        pick = (lax.broadcasted_iota(I32, (LANES, LANES), 0) == slab) & (
            lax.broadcasted_iota(I32, (LANES, LANES), 1) == HD
        )
        key_extra = dot32(shown[...], jnp.where(pick, OFF_BIAS, 0.0).astype(BF))
        extras.append(key_extra + jnp.where((lane > HD) & (lane < HD + 4), 1.0, 0.0))
    for scale in scales:
        top_ref[0:8, :] = jnp.maximum(top_ref[0:8, :], top_rows(scale))
    scale = jnp.concatenate(scales, axis=0)
    key_extra = jnp.concatenate(extras, axis=0)
    for head in range(heads):
        for first, extra, target in ((heads, key_extra, km_ref), (2 * heads, value_extra, vm_ref)):
            wide = slice((first + head) * LANES, (first + head + 1) * LANES)
            block = jnp.concatenate([proj_ref[:CUBE, wide] + row[:, wide] for row in slab_rows], axis=0)
            target[head] = (block * scale + extra).astype(BF)


def owned_kernel(seq_ref, owner_ref, ids_ref):
    groups, size = owner_ref.shape
    rows = ids_ref.shape[0]
    flags = jnp.where(owner_ref[...] == seq_ref[2], 1.0, 0.0).astype(BF)

    def upper(count):
        shape = (count, count)
        return jnp.where(lax.broadcasted_iota(I32, shape, 0) <= lax.broadcasted_iota(I32, shape, 1), 1.0, 0.0).astype(BF)

    local = dot32(flags, upper(size))
    totals = lax.dot_general(jnp.ones((8, size), BF), flags, NT, preferred_element_type=F32)
    ends = dot32(totals.astype(BF), upper(groups))
    begins = (ends - totals)[0:1, :]
    ends = ends[0:1, :]
    slot = lax.broadcasted_iota(I32, (rows, 1), 0).astype(F32)
    group = jnp.sum(jnp.where(ends <= slot, 1.0, 0.0), axis=1, keepdims=True)
    lane = lax.broadcasted_iota(I32, (rows, groups), 1).astype(F32)
    hot = jnp.where(lane == group, 1.0, 0.0)
    begin = jnp.sum(hot * begins, axis=1, keepdims=True)
    counts = dot32(hot.astype(BF), local.astype(BF))
    within = jnp.sum(jnp.where(counts <= slot - begin, 1.0, 0.0), axis=1, keepdims=True)
    ids_ref[...] = (group * size + within).astype(I32)


def slab_of(ids):
    return jnp.floor((ids.astype(F32) + 0.5) * (1.0 / CUBE)).astype(I32)


def place_hot(ids, places):
    lane = lax.broadcasted_iota(I32, (ids.shape[0], places), 1)
    slab = slab_of(ids)
    inner = ids - slab * CUBE
    return jnp.where((lane == inner) | (lane == slab + CUBE), 1.0, 0.0).astype(BF)


def queries_kernel(heads, pieces, *refs):
    queries_body(heads, refs[:pieces], *refs[pieces:])


def queries_body(
    heads, row_refs, idr_ref, own_ref, table_ref, small_ref, weight_ref, proj_ref, sum_ref, square_ref, top_ref,
    kv_ref, vv_ref, q_ref, seen_q, bounds, tables,
):
    step = pl.program_id(0)
    wide = heads * LANES

    @pl.when(step == 0)
    def _():
        count = idr_ref.shape[1]
        square = (count, count)
        here = lax.broadcasted_iota(I32, square, 0) == lax.broadcasted_iota(I32, square, 1)
        ids = jnp.sum(jnp.where(here, idr_ref[...].astype(F32), 0.0), axis=1, keepdims=True)
        rows = jnp.concatenate([ref[...].astype(F32) for ref in row_refs], axis=0)
        hot = place_hot(ids.astype(I32), table_ref.shape[0])
        place = sum(dot32(hot, part) for part in split2(table_ref[...]))
        seen = layer_norm(rows + place, small_ref[0:1, :].astype(F32)).astype(BF)
        seen_q[...] = (dot32(seen, weight_ref[:, :wide]) * LOG_SCALE).astype(BF)
        both = dot32(seen, weight_ref[:, wide:])
        lane = lax.broadcasted_iota(I32, (1, LANES), 1)
        extra = jnp.where((lane > HD) & (lane < HD + 4), 1.0, 0.0)
        ones = jnp.where(lane >= HD, 1.0, 0.0)
        scale = jnp.max(top_ref[0:8, :], axis=0, keepdims=True)
        scale = jnp.max(scale, axis=1, keepdims=True)
        masked_key = scale * top_ref[8:9, :]
        top = jnp.zeros((8, LANES), F32)
        high = scale * top_ref[16:24, :]
        spare = kv_ref.shape[1] - count
        for head in range(heads):
            keys = both[:, head * LANES : (head + 1) * LANES]
            top = jnp.maximum(top, top_rows(square_sums(keys)))
            middle = jnp.mean(keys, axis=0, keepdims=True)
            middle = jnp.sum(middle * middle, axis=1, keepdims=True)
            bounds[head : head + 1, :] = jnp.broadcast_to(jnp.sqrt(middle) * 1.03, (1, LANES))
            kv_ref[head, :count, :] = (keys + extra).astype(BF)
            values = both[:, (heads + head) * LANES : (heads + head + 1) * LANES]
            high = jnp.maximum(high, top_rows(jnp.abs(values)))
            vv_ref[head, :count, :] = (values + ones).astype(BF)
            if spare:
                off = lax.broadcasted_iota(I32, (spare, LANES), 1) == HD
                kv_ref[head, count:, :] = jnp.where(off, OFF_BIAS, 0.0).astype(BF)
                vv_ref[head, count:, :] = jnp.ones((spare, LANES), BF)
        seen_key = jnp.sqrt(jnp.max(top, axis=0, keepdims=True))
        bounds[heads : heads + 1, :] = jnp.maximum(seen_key, masked_key) * 1.03
        largest = jnp.max(jnp.max(high, axis=0, keepdims=True), axis=1, keepdims=True)
        bounds[heads + 1 : heads + 2, :] = jnp.broadcast_to(largest, (1, LANES))
        joined = jnp.concatenate([proj_ref[:, :wide], sum_ref[...], square_ref[...]], axis=1)
        for i, part in enumerate(split2(joined)):
            tables[i] = part

    @pl.when(step > 0)
    def _():
        ids = own_ref[...]
        count = ids.shape[0]
        hot = place_hot(ids, table_ref.shape[0])
        mixed = dot32(hot, tables[0]) + dot32(hot, tables[1])
        mean = mixed[:, wide : wide + LANES]
        scale = lax.rsqrt(mixed[:, wide + LANES :] - mean * mean + 1e-06)
        match = jnp.where(ids == idr_ref[...], 1.0, 0.0)
        shown = jnp.max(match, axis=1, keepdims=True) > 0.5
        picked = dot32(match.astype(BF), seen_q[...])
        lane = lax.broadcasted_iota(I32, (count, LANES), 1)
        limit = bounds[heads : heads + 1, :]
        fine = bounds[heads + 1 : heads + 2, :] < 2.0**25
        for head in range(heads):
            span = slice(head * LANES, (head + 1) * LANES)
            part = jnp.where(shown, picked[:, span], scale * mixed[:, span])
            norm = jnp.sqrt(square_sums(part))
            ceiling = norm * limit
            slack = jnp.where(fine, ceiling + norm * bounds[head : head + 1, :], 1e30)
            extra = jnp.where(lane == HD, 1.0, jnp.where(lane == HD + 1, HEADROOM - ceiling, 0.0))
            extra = jnp.where(lane == HD + 4, slack, extra)
            q_ref[head] = jnp.where(lane < HD, part, extra).astype(BF)


def attend_kernel(offset, rows, pieces, position, q_ref, km_ref, vm_ref, kv_ref, vv_ref, *refs):
    outs, (q_scr, acc, ctx, p_even, p_odd) = refs[:pieces], refs[pieces:]
    head = pl.program_id(0)
    q_scr[...] = q_ref[0, offset : offset + rows, :]
    block = p_even.shape[1]
    steps = km_ref.shape[1] // block
    rest = km_ref.shape[1] - steps * block
    tails = [(km_ref, vm_ref, steps * block, rest)] if rest else []
    visible = kv_ref.shape[1]
    tails += [(kv_ref, vv_ref, i, min(block, visible - i)) for i in range(0, visible, block)]

    def keys_of(i):
        if isinstance(i, int) and i >= steps:
            keys, _, start, size = tails[i - steps]
            return keys[0, start : start + size, :]
        return km_ref[0, pl.ds(i * block, block), :]

    def values_of(i):
        if isinstance(i, int) and i >= steps:
            _, values, start, size = tails[i - steps]
            return values[0, start : start + size, :]
        return vm_ref[0, pl.ds(i * block, block), :]

    def scores(i):
        return lax.dot_general(q_scr[...], keys_of(i), NT, preferred_element_type=F32)

    total = steps + len(tails)
    lane = lax.broadcasted_iota(I32, (rows, LANES), 1)
    slack = jnp.max(jnp.where(lane == HD + 4, q_scr[...].astype(F32), -1e30))

    @pl.when(jnp.logical_not(slack <= WINDOW))
    def _():
        q_scr[...] = jnp.where(lane > HD, 0.0, q_scr[...].astype(F32)).astype(BF)

        def look(i, best):
            return jnp.maximum(best, jnp.max(scores(i), axis=1, keepdims=True))

        peak = lax.fori_loop(0, steps, look, jnp.full((rows, 1), -3e38, F32))
        for i in range(steps, total):
            peak = look(i, peak)
        high, mid, low = split3(peak)
        new = jnp.where(lane == HD + 1, -high.astype(F32), q_scr[...].astype(F32))
        new = jnp.where(lane == HD + 2, -mid.astype(F32), new)
        new = jnp.where(lane == HD + 3, -low.astype(F32), new)
        q_scr[...] = new.astype(BF)

    def width_of(i):
        return tails[i - steps][3] if isinstance(i, int) and i >= steps else block

    def weigh(i, target):
        target[:, : width_of(i)] = jnp.exp2(scores(i)).astype(BF)

    def add(weights, i):
        acc[...] += dot32(weights[:, : width_of(i)], values_of(i))

    acc[...] = jnp.zeros_like(acc)
    slots = (p_even, p_odd)
    weigh(0, p_even)

    def body(j, carry):
        i = 2 * j + 1
        weigh(i, p_odd)
        add(p_even, i - 1)
        weigh(i + 1, p_even)
        add(p_odd, i)
        return carry

    pairs = (steps - 1) // 2
    lax.fori_loop(0, pairs, body, 0)
    for i in range(1 + 2 * pairs, total + 1):
        if i < total:
            weigh(i, slots[i % 2])
        add(slots[1 - i % 2], i - 1)
    totals = acc[...]
    ctx[head] = totals[:, :HD] / totals[:, HD:]

    @pl.when(head == pl.num_programs(0) - 1)
    def _():
        for step, out in enumerate(outs):
            target = lax.rem(position[1] + step, pieces)
            span = pl.ds(pl.multiple_of(target * (rows // pieces), 16), rows // pieces) if pieces > 1 else slice(None)
            out[...] = jnp.concatenate([ctx[i, span, :] for i in range(ctx.shape[0])], axis=1).astype(BF)


def attend(position, q_all, km, vm, kv, vv, offset, rows, pieces):
    heads, total, _ = q_all.shape
    masked, visible = km.shape[1], kv.shape[1]
    per_head = lambda size: pl.BlockSpec((1, size, LANES), lambda h: (h, 0, 0))
    shape = (rows // pieces, heads * HD)
    block = min(KEY_BLOCK, masked)
    return pl.pallas_call(
        functools.partial(attend_kernel, offset, rows, pieces),
        grid=(heads,),
        in_specs=[SMEM, per_head(total), per_head(masked), per_head(masked), per_head(visible), per_head(visible)],
        out_specs=[pl.BlockSpec(shape, lambda h: (0, 0))] * pieces,
        out_shape=[jax.ShapeDtypeStruct(shape, BF)] * pieces,
        scratch_shapes=[
            pltpu.VMEM((rows, LANES), BF),
            pltpu.VMEM((rows, LANES), F32),
            pltpu.VMEM((heads, rows, HD), F32),
            pltpu.VMEM((rows, block), BF),
            pltpu.VMEM((rows, block), BF),
        ],
        compiler_params=vmem_limit(48),
        cost_estimate=pl.CostEstimate(
            flops=8 * heads * rows * (masked + visible) * LANES,
            bytes_accessed=4 * heads * masked * LANES,
            transcendentals=heads * rows * masked,
        ),
        name="attend",
    )(position, q_all, km, vm, kv, vv)


def gelu(x):
    size = jnp.abs(x)
    base = 1.0 + 0.2316419 * size
    t = pl.reciprocal(base, approx=True)
    t = t * (2.0 - base * t)
    poly = 0.5307027145
    for c in (-0.7265760135, 0.7107068705, -0.142248368, 0.127414796):
        poly = poly * t + c
    tail = (size * t) * poly * jnp.exp2(size * size * (-0.5 * math.log2(math.e)))
    return jnp.maximum(x, 0.0) - tail


def mlp_kernel(pieces, row_pieces, layout, first_row, spread, position, *refs):
    ctx_refs, refs = refs[:pieces], refs[pieces:]
    row_refs, refs = refs[:row_pieces], refs[row_pieces:]
    own_ref, idr_ref, table_ref, small_ref = refs[:4]
    sources, (res_ref, ups, downs, outs, acc, mlp_in, sems) = refs[4:-7], refs[-7:]
    weights = [sources[k].at[j] for k, j in layout]
    step = pl.program_id(0)
    share = acc.shape[0]
    half = weights[0].shape[1]
    up = ups.shape[2]
    tail = up + downs.shape[1]
    swap = lambda a: jnp.where(position[0] == 0, a, jnp.concatenate([a[:, half:], a[:, :half]], axis=1))

    def out_copy(i):
        side = slice(i % 2 * half, (i % 2 + 1) * half)
        return pltpu.make_async_copy(weights[i].at[tail:], outs.at[i // 2, :, side], sems.at[i, 0])

    def copies(i):
        side = slice(i % 2 * half, (i % 2 + 1) * half)
        moves = [
            pltpu.make_async_copy(
                weights[i].at[k * half : (k + 1) * half],
                ups.at[i // 2, side, k * half : (k + 1) * half],
                sems.at[i, 1 + k],
            )
            for k in range(up // half)
        ]
        last = sems.at[i, 1 + up // half]
        return moves + [pltpu.make_async_copy(weights[i].at[up:tail], downs.at[i // 2, :, side], last)]

    @pl.when(step == 0)
    def _():
        for i in range(2 * pieces):
            out_copy(i).start()
        for i in range(2 * pieces):
            for copy in copies(i):
                copy.start()
        if share == own_ref.shape[0]:
            ids = own_ref[...]
        elif spread:
            ids = own_ref[pl.ds(pl.multiple_of(first_row + position[1] * share, 16), share), :]
        else:
            ids = own_ref[first_row : first_row + share, :]
        hot = place_hot(ids, table_ref.shape[0])
        place = sum(dot32(hot, part) for part in split2(table_ref[...]))
        match = jnp.where(ids == idr_ref[...], 1.0, 0.0)
        shown = jnp.max(match, axis=1, keepdims=True) > 0.5
        rows = jnp.concatenate([ref[...] for ref in row_refs], axis=0)
        stream = jnp.where(shown, dot32(match.astype(BF), rows), small_ref[1:2, :].astype(F32)) + place
        acc[...] = swap(stream)
        for i in range(pieces):
            out_copy(2 * i).wait()
            out_copy(2 * i + 1).wait()
            acc[...] += dot32(ctx_refs[i][...], outs[i])
        mlp_in[...] = layer_norm(acc[...], swap(small_ref[2:3, :].astype(F32))).astype(BF)

    for i in range(pieces):

        @pl.when(step == i)
        def _(i=i):
            for copy in copies(2 * i) + copies(2 * i + 1):
                copy.wait()

    wide = 256 if up % 256 == 0 else up
    blocks = [slice(k, k + wide) for k in range(0, up, wide)]
    pres = [dot32(mlp_in[...], ups[step, :, span]) for span in blocks]
    added = 0.0
    for pre, span in zip(pres, blocks):
        added += dot32(gelu(pre).astype(BF), downs[step, span, :])
    acc[...] += added

    @pl.when(step == pieces - 1)
    def _():
        if res_ref.shape[0] == share:
            res_ref[...] = swap(acc[...]).astype(res_ref.dtype)
        else:
            acc[...] = swap(acc[...])
            own = pltpu.make_async_copy(acc, res_ref.at[first_row : first_row + share], sems.at[2 * pieces, 0])
            own.start()
            own.wait()


def mlp(position, contexts, all_rows, own_ids, id_row, table, small, mine, others, units, first_row, spread, total):
    pieces = len(mine)
    weights = [*mine, *others]
    layout = [(k, j) for k, w in enumerate(weights) for j in range(w.shape[0])]
    layout = [layout[i // 2 + i % 2 * pieces] for i in range(2 * pieces)]
    share = contexts[0].shape[0]
    width = table.shape[1]
    ins = [*contexts, *all_rows, own_ids, id_row, table, small]
    out_rows = share if spread else total
    inside = out_rows == share
    return pl.pallas_call(
        functools.partial(mlp_kernel, pieces, len(all_rows), layout, first_row, spread),
        grid=(pieces,),
        in_specs=[SMEM] + [whole(a) for a in ins] + [pl.BlockSpec(memory_space=pl.ANY)] * len(weights),
        out_specs=pl.BlockSpec((share, width), lambda i: (0, 0)) if inside else pl.BlockSpec(memory_space=pl.ANY),
        out_shape=jax.ShapeDtypeStruct((out_rows, width), BF if spread else F32),
        scratch_shapes=[
            pltpu.VMEM((pieces, width, units), BF),
            pltpu.VMEM((pieces, units, width), BF),
            pltpu.VMEM((pieces, contexts[0].shape[1], width), BF),
            pltpu.VMEM((share, width), F32),
            pltpu.VMEM((share, width), BF),
            pltpu.SemaphoreType.DMA((2 * pieces + 1, 2 + units // (width // 2))),
        ],
        compiler_params=vmem_limit(32),
        cost_estimate=pl.CostEstimate(
            flops=30 * share * width * width, bytes_accessed=18 * width * width, transcendentals=4 * share * width
        ),
        name="mlp",
    )(position, *ins, *weights)


def place_kernel(pieces, first_row, position, *refs):
    sources, (_held, out_ref), (sems, *stages) = refs[:pieces], refs[pieces : pieces + 2], refs[pieces + 2 :]

    def move(k):
        count = sources[k].shape[0]
        source = lax.rem(position[1] + (pieces - k), pieces)
        place = pl.ds(pl.multiple_of(first_row + source * count, 16), count)
        return pltpu.make_async_copy(stages[k], out_ref.at[place], sems.at[k])

    for k in range(pieces):
        stages[k][...] = sources[k][...].astype(F32)
        move(k).start()
    for k in range(pieces):
        move(k).wait()


def put_rows(position, decoded, pieces, first_row):
    count = len(pieces)
    return pl.pallas_call(
        functools.partial(place_kernel, count, first_row),
        in_specs=[SMEM] + [pl.BlockSpec(memory_space=pltpu.VMEM)] * count + [pl.BlockSpec(memory_space=pl.ANY)],
        out_specs=pl.BlockSpec(memory_space=pl.ANY),
        out_shape=jax.ShapeDtypeStruct(decoded.shape, decoded.dtype),
        scratch_shapes=[pltpu.SemaphoreType.DMA((count,))] + [pltpu.VMEM(p.shape, F32) for p in pieces],
        input_output_aliases={count + 1: 0},
        compiler_params=vmem_limit(16),
        name="put_rows",
    )(position, *pieces, decoded)


def shards(
    enc_rows,
    vis_index,
    owner_of,
    enc_gain,
    embed_weight,
    mask_token,
    attn_gain,
    qkv_weight,
    out_weight,
    mlp_gain,
    up_weight,
    down_weight,
):
    section = lax.axis_index("section")
    mp_size = lax.axis_size("mp")
    position = jnp.stack([section, lax.axis_index("mp"), lax.axis_index("seq")]).astype(I32)
    patch_total = owner_of.shape[0]
    own_rows = patch_total // lax.axis_size("seq")
    features = mask_token.shape[0]
    half = features // 2
    width = qkv_weight.shape[2]
    heads = width // HD
    slabs = patch_total // CUBE
    places = CUBE + slabs
    vmem = lambda shape, kind: jax.ShapeDtypeStruct(shape, kind)

    embed_other = shifted(embed_weight, "section", 1)
    qkv_mine = qkv_weight.reshape(half, 3 * width)
    qkv_other = shifted(qkv_mine, "section", 1)
    all_ids = gather_pieces(vis_index, "seq")
    embedded = pl.pallas_call(
        embed_kernel,
        in_specs=[SMEM] + [pl.BlockSpec(memory_space=pltpu.VMEM)] * 4,
        out_specs=pl.BlockSpec(memory_space=pltpu.VMEM),
        out_shape=vmem((enc_rows.shape[1], features), BF),
        compiler_params=vmem_limit(12),
        name="embed",
    )(position, enc_rows[0], enc_gain[None, :], embed_weight, embed_other)
    embedded, *all_ids = lax.optimization_barrier((embedded, *all_ids))
    all_rows = gather_pieces(embedded, "seq")
    id_row = jnp.concatenate([a.reshape(1, -1) for a in all_ids], axis=1)
    visible = id_row.shape[1]

    table = jnp.asarray(place_table(slabs, features))
    small = jnp.stack([attn_gain, mask_token, mlp_gain])
    groups = 3 * heads
    qkv_wide, proj, means, squares = pl.pallas_call(
        functools.partial(table_kernel, groups),
        in_specs=[SMEM] + [pl.BlockSpec(memory_space=pltpu.VMEM)] * 4,
        out_specs=[pl.BlockSpec(memory_space=pltpu.VMEM)] * 4,
        out_shape=[
            vmem((features, groups * LANES), BF),
            vmem((places, groups * LANES), F32),
            vmem((places, LANES), F32),
            vmem((places, LANES), F32),
        ],
        compiler_params=vmem_limit(16),
        name="tables",
    )(position, table, small, qkv_mine, qkv_other)

    blocks = 4 if slabs % 4 == 0 and patch_total % 64 == 0 else 1
    slab_rows = patch_total // blocks
    ins = [proj, means, squares, id_row]
    key_spec = pl.BlockSpec((heads, slab_rows, LANES), lambda i: (0, i, 0))
    km, vm, top = pl.pallas_call(
        functools.partial(masked_kernel, heads),
        grid=(blocks,),
        in_specs=[whole(a) for a in ins],
        out_specs=[key_spec, key_spec, pl.BlockSpec((24, LANES), lambda i: (0, 0))],
        out_shape=[vmem((heads, patch_total, LANES), BF)] * 2 + [vmem((24, LANES), F32)],
        scratch_shapes=[pltpu.VMEM((CUBE, LANES), BF)],
        compiler_params=vmem_limit(24),
        name="masked",
    )(*ins)

    group = HD
    own_ids = pl.pallas_call(
        owned_kernel,
        in_specs=[SMEM, pl.BlockSpec(memory_space=pltpu.VMEM)],
        out_specs=pl.BlockSpec(memory_space=pltpu.VMEM),
        out_shape=vmem((own_rows, 1), I32),
        compiler_params=vmem_limit(12),
        name="owned",
    )(position, owner_of.reshape(patch_total // group, group))

    row_block = 720 if own_rows % 720 == 0 else own_rows
    spaced = visible + (-visible % KEY_PAD)
    ins = [*all_rows, id_row, own_ids, table, small, qkv_wide, proj, means, squares, top]
    specs = [whole(a) for a in ins]
    specs[len(all_rows) + 1] = pl.BlockSpec((row_block, 1), lambda i: (jnp.maximum(i - 1, 0), 0))
    kv, vv, q_all = pl.pallas_call(
        functools.partial(queries_kernel, heads, len(all_rows)),
        grid=(1 + own_rows // row_block,),
        in_specs=specs,
        out_specs=[pl.BlockSpec((heads, spaced, LANES), lambda i: (0, 0, 0))] * 2
        + [pl.BlockSpec((heads, row_block, LANES), lambda i: (0, jnp.maximum(i - 1, 0), 0))],
        out_shape=[vmem((heads, spaced, LANES), BF)] * 2 + [vmem((heads, own_rows, LANES), BF)],
        scratch_shapes=[
            pltpu.VMEM((visible, heads * LANES), BF),
            pltpu.VMEM((8 * (-(-(heads + 2) // 8)), LANES), F32),
            pltpu.VMEM((2, places, (heads + 2) * LANES), BF),
        ],
        compiler_params=vmem_limit(28),
        name="queries",
    )(*ins)

    units = up_weight.shape[1]
    packed = jnp.concatenate(
        [up_weight[:, i : i + half] for i in range(0, units, half)] + [down_weight, out_weight], axis=0
    )
    packed, _unused = lax.optimization_barrier((packed, embedded))
    packed_other = shifted(packed, "section", 1)
    mine = shift_pieces(packed, "mp")

    big = 1408 if own_rows >= 2048 and mp_size > 1 else 0
    rest = own_rows - big

    q_all, packed_other = lax.optimization_barrier((q_all, packed_other))

    def pair_weights(after):
        pieces = mine
        if after is not None:
            *pieces, _unused = lax.optimization_barrier((*mine, after))
        others = [packed_other[None]]
        for i in range(1, len(pieces), 2):
            others.append(shifted(jnp.stack(pieces[i : i + 2]), "section", 1))
        return [p[None] for p in pieces], others

    def finish(weights, contexts, first_row, spread):
        return mlp(position, contexts, all_rows, own_ids, id_row, table, small, *weights, units, first_row, spread, own_rows)

    if not big:
        (context,) = attend(position, q_all, km, vm, kv, vv, 0, rest, 1)
        return finish(pair_weights(None), shift_pieces(context, "mp"), 0, False)[None]
    parts = attend(position, q_all, km, vm, kv, vv, 0, big, mp_size)
    weights = pair_weights(parts[0])
    exchanged = [part if step == 0 else shifted(part, "mp", step) for step, part in enumerate(parts)]
    (context,) = attend(position, q_all, km, vm, kv, vv, big, rest, 1)
    last = shift_pieces(context, "mp")
    *exchanged, _unused = lax.optimization_barrier((*exchanged, context))
    done = finish(weights, exchanged, 0, True)
    *last, done = lax.optimization_barrier((*last, done))
    pieces = shift_pieces(done, "mp")
    decoded = finish(weights, last, big, False)
    return put_rows(position, decoded, pieces, 0)[None]


def solution(mesh):
    in_specs = (
        P("section", "seq", None),
        P("section", "seq"),
        P(),
        P(),
        P("section", None),
        P(),
        P(),
        P("section", None, "mp"),
        P("mp", "section"),
        P(),
        P("section", "mp"),
        P("mp", "section"),
    )
    out_specs = P("section", "seq", None)
    return jax.shard_map(shards, mesh=mesh, in_specs=in_specs, out_specs=out_specs, check_vma=False)
```

```python
import functools
import math

import jax
import jax.numpy as jnp
import numpy as np
from jax import lax
from jax.experimental import pallas as pl
from jax.experimental.pallas import tpu as pltpu
from jax.sharding import PartitionSpec as P

GX = 6
HD = 64
LANES = 128
KEY_BLOCK = 2048
KEY_PAD = 256
OFF_BIAS = -1e30
HEADROOM = 88.0
WINDOW = 180.0
CUBE = GX * GX * GX
HIGH = lax.Precision.HIGHEST
BF = jnp.bfloat16
F32 = jnp.float32
I32 = jnp.int32
MIB = 1024 * 1024
LOG_SCALE = math.log2(math.e) * HD ** (-0.5)
NT = (((1,), (1,)), ((), ()))


def vmem_limit(mib):
    return pltpu.CompilerParams(vmem_limit_bytes=mib * MIB)


def layer_norm(values, scales):
    centred = values - jnp.mean(values, axis=-1, keepdims=True)
    spread = jnp.mean(centred * centred, axis=-1, keepdims=True)
    return centred * lax.rsqrt(spread + 1e-06) * scales


def dot32(a, b):
    return jnp.dot(a, b, preferred_element_type=F32)


def split3(values):
    high = values.astype(BF)
    rest = values - high.astype(F32)
    mid = rest.astype(BF)
    return high, mid, (rest - mid.astype(F32)).astype(BF)


def split2(values):
    high = values.astype(BF)
    return high, (values - high.astype(F32)).astype(BF)


def shifted(values, axis, step):
    size = lax.axis_size(axis)
    return lax.ppermute(values, axis, [(i, (i + step) % size) for i in range(size)])


def shift_pieces(values, axis):
    return [values] + [shifted(values, axis, step) for step in range(1, lax.axis_size(axis))]


def gather_pieces(values, axis):
    if lax.axis_size(axis) > 4:
        return [lax.all_gather(values, axis, axis=0, tiled=True)]
    return shift_pieces(values, axis)


def whole(array):
    return pl.BlockSpec(array.shape, lambda *_: (0,) * array.ndim)


SMEM = pl.BlockSpec(memory_space=pltpu.SMEM)


def place_table(slabs, features):
    quarter = features // 4
    frequency = (1.0 / 10000.0 ** (np.arange(quarter // 2, dtype=np.float32) / (quarter // 2))).astype(np.float32)
    angles = np.arange(max(slabs, GX), dtype=np.float32)[:, None] * frequency[None, :]
    codes = np.concatenate([np.sin(angles), np.cos(angles)], axis=1).astype(np.float32)
    place = np.arange(CUBE)
    cube = np.concatenate(
        [codes[place % GX], codes[place // GX % GX], codes[place // (GX * GX)], np.zeros((CUBE, quarter), np.float32)],
        axis=1,
    )
    slab = np.concatenate([np.zeros((slabs, 3 * quarter), np.float32), codes[:slabs]], axis=1)
    return np.concatenate([cube, slab], axis=0)


def embed_kernel(position, rows_ref, gain_ref, mine_ref, other_ref, out_ref):
    normed = layer_norm(rows_ref[...].astype(F32), gain_ref[...].astype(F32)).astype(BF)
    half = normed.shape[1] // 2
    low, high = normed[:, :half], normed[:, half:]
    first = position[0] == 0

    @pl.when(first)
    def _():
        out_ref[...] = (dot32(low, mine_ref[...]) + dot32(high, other_ref[...])).astype(BF)

    @pl.when(jnp.logical_not(first))
    def _():
        out_ref[...] = (dot32(low, other_ref[...]) + dot32(high, mine_ref[...])).astype(BF)


def table_kernel(
    groups, position, table_ref, small_ref, mine_ref, other_ref, weight_ref, proj_ref, sum_ref, square_ref
):
    features = table_ref.shape[1]
    places = table_ref.shape[0]
    first = position[0] == 0
    mine, other = mine_ref[...], other_ref[...]
    full = jnp.concatenate([jnp.where(first, mine, other), jnp.where(first, other, mine)], axis=0)
    gain = small_ref[0:1, :].astype(F32)
    mask = small_ref[1:2, :].astype(F32)
    mask = mask - jnp.mean(mask, axis=1, keepdims=True)
    table = table_ref[...]
    row = lax.broadcasted_iota(I32, table.shape, 0)
    lane = lax.broadcasted_iota(I32, table.shape, 1)
    rows = table + jnp.where(row < CUBE, mask, 0.0)
    gained = jnp.concatenate([rows * gain, jnp.broadcast_to(gain, (16, features))], axis=0)
    proj = sum(dot32(part, full) for part in split3(gained))
    last = lane >= features - features // 4
    squared = jnp.where(row < CUBE, jnp.where(last, 0.0, rows), jnp.where(last, rows + mask, 0.0))
    total = jnp.sum(rows, axis=1, keepdims=True)
    square = jnp.sum(squared * squared, axis=1, keepdims=True)
    column = lax.broadcasted_iota(I32, (1, groups * HD), 1)
    scale = jnp.where(column < groups * HD // 3, LOG_SCALE, 1.0)
    proj = (proj[:places, :] - (total / features) * proj[places : places + 1, :]) * scale
    for group in range(groups):
        span = slice(group * HD, (group + 1) * HD)
        wide = slice(group * LANES, (group + 1) * LANES)
        weight_ref[:, wide] = jnp.concatenate([full[:, span], jnp.zeros((features, HD), BF)], axis=1)
        proj_ref[:, wide] = jnp.concatenate([proj[:, span], jnp.zeros((places, HD), F32)], axis=1)
    sum_ref[...] = jnp.broadcast_to(total / features, sum_ref.shape)
    square_ref[...] = jnp.broadcast_to(square / features, square_ref.shape)


def top_rows(values):
    return jnp.max(values.reshape(values.shape[0] // 8, 8, LANES), axis=0)


def square_sums(values):
    return dot32((values * values).astype(BF), jnp.ones((LANES, LANES), BF))


def masked_kernel(heads, proj_ref, sum_ref, square_ref, ids_ref, km_ref, vm_ref, top_ref, shown):
    step = pl.program_id(0)
    parts = km_ref.shape[1] // CUBE
    lane = lax.broadcasted_iota(I32, (1, LANES), 1)

    @pl.when(step == 0)
    def _():
        ids = ids_ref[...]
        slab = slab_of(ids)
        inner = ids - slab * CUBE
        rows = lax.broadcasted_iota(I32, (CUBE, ids.shape[1]), 0)
        columns = lax.broadcasted_iota(I32, (LANES, ids.shape[1]), 0)
        by_place = jnp.where(rows == inner, 1.0, 0.0).astype(BF)
        by_slab = jnp.where(columns == slab, 1.0, 0.0).astype(BF)
        shown[...] = lax.dot_general(by_place, by_slab, NT, preferred_element_type=F32).astype(BF)
        largest = lambda x: jnp.max(jnp.max(x, axis=0, keepdims=True), axis=1, keepdims=True)
        norms = lambda x: jnp.sqrt(jnp.max(jnp.sum(x * x, axis=1, keepdims=True), axis=0, keepdims=True))
        key_top = jnp.zeros((1, 1), F32)
        value_top = jnp.zeros((1, 1), F32)
        for head in range(heads):
            wide = slice((heads + head) * LANES, (heads + head + 1) * LANES)
            inner, outer = proj_ref[:CUBE, wide], proj_ref[CUBE:, wide]
            middle = jnp.mean(outer, axis=0, keepdims=True)
            key_top = jnp.maximum(key_top, norms(inner + middle) + norms(outer - middle))
            wide = slice((2 * heads + head) * LANES, (2 * heads + head + 1) * LANES)
            value_top = jnp.maximum(value_top, largest(jnp.abs(proj_ref[:CUBE, wide])) + largest(jnp.abs(proj_ref[CUBE:, wide])))
        top_ref[0:8, :] = jnp.zeros((8, LANES), F32)
        top_ref[8:16, :] = jnp.broadcast_to(key_top, (8, LANES))
        top_ref[16:24, :] = jnp.broadcast_to(value_top, (8, LANES))

    value_extra = jnp.where(lane >= HD, 1.0, 0.0)
    scales = []
    extras = []
    slab_rows = []
    for part in range(parts):
        slab = step * parts + part
        row = CUBE + slab
        slab_rows.append(proj_ref[pl.ds(row, 1), :])
        mean = sum_ref[:CUBE, :] + sum_ref[pl.ds(row, 1), :]
        spread = square_ref[:CUBE, :] + square_ref[pl.ds(row, 1), :] - mean * mean
        scales.append(lax.rsqrt(spread + 1e-06))
        pick = (lax.broadcasted_iota(I32, (LANES, LANES), 0) == slab) & (
            lax.broadcasted_iota(I32, (LANES, LANES), 1) == HD
        )
        key_extra = dot32(shown[...], jnp.where(pick, OFF_BIAS, 0.0).astype(BF))
        extras.append(key_extra + jnp.where((lane > HD) & (lane < HD + 4), 1.0, 0.0))
    for scale in scales:
        top_ref[0:8, :] = jnp.maximum(top_ref[0:8, :], top_rows(scale))
    scale = jnp.concatenate(scales, axis=0)
    key_extra = jnp.concatenate(extras, axis=0)
    for head in range(heads):
        for first, extra, target in ((heads, key_extra, km_ref), (2 * heads, value_extra, vm_ref)):
            wide = slice((first + head) * LANES, (first + head + 1) * LANES)
            block = jnp.concatenate([proj_ref[:CUBE, wide] + row[:, wide] for row in slab_rows], axis=0)
            target[head] = (block * scale + extra).astype(BF)


def owned_kernel(seq_ref, owner_ref, ids_ref):
    groups, size = owner_ref.shape
    rows = ids_ref.shape[0]
    flags = jnp.where(owner_ref[...] == seq_ref[2], 1.0, 0.0).astype(BF)

    def upper(count):
        shape = (count, count)
        return jnp.where(lax.broadcasted_iota(I32, shape, 0) <= lax.broadcasted_iota(I32, shape, 1), 1.0, 0.0).astype(BF)

    local = dot32(flags, upper(size))
    totals = lax.dot_general(jnp.ones((8, size), BF), flags, NT, preferred_element_type=F32)
    ends = dot32(totals.astype(BF), upper(groups))
    begins = (ends - totals)[0:1, :]
    ends = ends[0:1, :]
    slot = lax.broadcasted_iota(I32, (rows, 1), 0).astype(F32)
    group = jnp.sum(jnp.where(ends <= slot, 1.0, 0.0), axis=1, keepdims=True)
    lane = lax.broadcasted_iota(I32, (rows, groups), 1).astype(F32)
    hot = jnp.where(lane == group, 1.0, 0.0)
    begin = jnp.sum(hot * begins, axis=1, keepdims=True)
    counts = dot32(hot.astype(BF), local.astype(BF))
    within = jnp.sum(jnp.where(counts <= slot - begin, 1.0, 0.0), axis=1, keepdims=True)
    ids_ref[...] = (group * size + within).astype(I32)


def slab_of(ids):
    return jnp.floor((ids.astype(F32) + 0.5) * (1.0 / CUBE)).astype(I32)


def place_hot(ids, places):
    lane = lax.broadcasted_iota(I32, (ids.shape[0], places), 1)
    slab = slab_of(ids)
    inner = ids - slab * CUBE
    return jnp.where((lane == inner) | (lane == slab + CUBE), 1.0, 0.0).astype(BF)


def queries_kernel(heads, pieces, *refs):
    queries_body(heads, refs[:pieces], *refs[pieces:])


def queries_body(
    heads, row_refs, idr_ref, own_ref, table_ref, small_ref, weight_ref, proj_ref, sum_ref, square_ref, top_ref,
    kv_ref, vv_ref, q_ref, seen_q, bounds, tables,
):
    step = pl.program_id(0)
    wide = heads * LANES

    @pl.when(step == 0)
    def _():
        count = idr_ref.shape[1]
        square = (count, count)
        here = lax.broadcasted_iota(I32, square, 0) == lax.broadcasted_iota(I32, square, 1)
        ids = jnp.sum(jnp.where(here, idr_ref[...].astype(F32), 0.0), axis=1, keepdims=True)
        rows = jnp.concatenate([ref[...].astype(F32) for ref in row_refs], axis=0)
        hot = place_hot(ids.astype(I32), table_ref.shape[0])
        place = sum(dot32(hot, part) for part in split2(table_ref[...]))
        seen = layer_norm(rows + place, small_ref[0:1, :].astype(F32)).astype(BF)
        seen_q[...] = (dot32(seen, weight_ref[:, :wide]) * LOG_SCALE).astype(BF)
        both = dot32(seen, weight_ref[:, wide:])
        lane = lax.broadcasted_iota(I32, (1, LANES), 1)
        extra = jnp.where((lane > HD) & (lane < HD + 4), 1.0, 0.0)
        ones = jnp.where(lane >= HD, 1.0, 0.0)
        scale = jnp.max(top_ref[0:8, :], axis=0, keepdims=True)
        scale = jnp.max(scale, axis=1, keepdims=True)
        masked_key = scale * top_ref[8:9, :]
        top = jnp.zeros((8, LANES), F32)
        high = scale * top_ref[16:24, :]
        spare = kv_ref.shape[1] - count
        for head in range(heads):
            keys = both[:, head * LANES : (head + 1) * LANES]
            top = jnp.maximum(top, top_rows(square_sums(keys)))
            middle = jnp.mean(keys, axis=0, keepdims=True)
            middle = jnp.sum(middle * middle, axis=1, keepdims=True)
            bounds[head : head + 1, :] = jnp.broadcast_to(jnp.sqrt(middle) * 1.03, (1, LANES))
            kv_ref[head, :count, :] = (keys + extra).astype(BF)
            values = both[:, (heads + head) * LANES : (heads + head + 1) * LANES]
            high = jnp.maximum(high, top_rows(jnp.abs(values)))
            vv_ref[head, :count, :] = (values + ones).astype(BF)
            if spare:
                off = lax.broadcasted_iota(I32, (spare, LANES), 1) == HD
                kv_ref[head, count:, :] = jnp.where(off, OFF_BIAS, 0.0).astype(BF)
                vv_ref[head, count:, :] = jnp.ones((spare, LANES), BF)
        seen_key = jnp.sqrt(jnp.max(top, axis=0, keepdims=True))
        bounds[heads : heads + 1, :] = jnp.maximum(seen_key, masked_key) * 1.03
        largest = jnp.max(jnp.max(high, axis=0, keepdims=True), axis=1, keepdims=True)
        bounds[heads + 1 : heads + 2, :] = jnp.broadcast_to(largest, (1, LANES))
        joined = jnp.concatenate([proj_ref[:, :wide], sum_ref[...], square_ref[...]], axis=1)
        for i, part in enumerate(split2(joined)):
            tables[i] = part

    @pl.when(step > 0)
    def _():
        ids = own_ref[...]
        count = ids.shape[0]
        hot = place_hot(ids, table_ref.shape[0])
        mixed = dot32(hot, tables[0]) + dot32(hot, tables[1])
        mean = mixed[:, wide : wide + LANES]
        scale = lax.rsqrt(mixed[:, wide + LANES :] - mean * mean + 1e-06)
        match = jnp.where(ids == idr_ref[...], 1.0, 0.0)
        shown = jnp.max(match, axis=1, keepdims=True) > 0.5
        picked = dot32(match.astype(BF), seen_q[...])
        lane = lax.broadcasted_iota(I32, (count, LANES), 1)
        limit = bounds[heads : heads + 1, :]
        fine = bounds[heads + 1 : heads + 2, :] < 2.0**25
        for head in range(heads):
            span = slice(head * LANES, (head + 1) * LANES)
            part = jnp.where(shown, picked[:, span], scale * mixed[:, span])
            norm = jnp.sqrt(square_sums(part))
            ceiling = norm * limit
            slack = jnp.where(fine, ceiling + norm * bounds[head : head + 1, :], 1e30)
            extra = jnp.where(lane == HD, 1.0, jnp.where(lane == HD + 1, HEADROOM - ceiling, 0.0))
            extra = jnp.where(lane == HD + 4, slack, extra)
            q_ref[head] = jnp.where(lane < HD, part, extra).astype(BF)


def attend_kernel(offset, rows, pieces, position, q_ref, km_ref, vm_ref, kv_ref, vv_ref, *refs):
    outs, (q_scr, acc, ctx, p_even, p_odd) = refs[:pieces], refs[pieces:]
    head = pl.program_id(0)
    q_scr[...] = q_ref[0, offset : offset + rows, :]
    block = p_even.shape[1]
    steps = km_ref.shape[1] // block
    rest = km_ref.shape[1] - steps * block
    tails = [(km_ref, vm_ref, steps * block, rest)] if rest else []
    visible = kv_ref.shape[1]
    tails += [(kv_ref, vv_ref, i, min(block, visible - i)) for i in range(0, visible, block)]

    def keys_of(i):
        if isinstance(i, int) and i >= steps:
            keys, _, start, size = tails[i - steps]
            return keys[0, start : start + size, :]
        return km_ref[0, pl.ds(i * block, block), :]

    def values_of(i):
        if isinstance(i, int) and i >= steps:
            _, values, start, size = tails[i - steps]
            return values[0, start : start + size, :]
        return vm_ref[0, pl.ds(i * block, block), :]

    def scores(i):
        return lax.dot_general(q_scr[...], keys_of(i), NT, preferred_element_type=F32)

    total = steps + len(tails)
    lane = lax.broadcasted_iota(I32, (rows, LANES), 1)
    slack = jnp.max(jnp.where(lane == HD + 4, q_scr[...].astype(F32), -1e30))

    @pl.when(jnp.logical_not(slack <= WINDOW))
    def _():
        q_scr[...] = jnp.where(lane > HD, 0.0, q_scr[...].astype(F32)).astype(BF)

        def look(i, best):
            return jnp.maximum(best, jnp.max(scores(i), axis=1, keepdims=True))

        peak = lax.fori_loop(0, steps, look, jnp.full((rows, 1), -3e38, F32))
        for i in range(steps, total):
            peak = look(i, peak)
        high, mid, low = split3(peak)
        new = jnp.where(lane == HD + 1, -high.astype(F32), q_scr[...].astype(F32))
        new = jnp.where(lane == HD + 2, -mid.astype(F32), new)
        new = jnp.where(lane == HD + 3, -low.astype(F32), new)
        q_scr[...] = new.astype(BF)

    def width_of(i):
        return tails[i - steps][3] if isinstance(i, int) and i >= steps else block

    def weigh(i, target):
        target[:, : width_of(i)] = jnp.exp2(scores(i)).astype(BF)

    def add(weights, i):
        acc[...] += dot32(weights[:, : width_of(i)], values_of(i))

    acc[...] = jnp.zeros_like(acc)
    slots = (p_even, p_odd)
    weigh(0, p_even)

    def body(j, carry):
        i = 2 * j + 1
        weigh(i, p_odd)
        add(p_even, i - 1)
        weigh(i + 1, p_even)
        add(p_odd, i)
        return carry

    pairs = (steps - 1) // 2
    lax.fori_loop(0, pairs, body, 0)
    for i in range(1 + 2 * pairs, total + 1):
        if i < total:
            weigh(i, slots[i % 2])
        add(slots[1 - i % 2], i - 1)
    totals = acc[...]
    ctx[head] = totals[:, :HD] / totals[:, HD:]

    @pl.when(head == pl.num_programs(0) - 1)
    def _():
        for step, out in enumerate(outs):
            target = lax.rem(position[1] + step, pieces)
            span = pl.ds(pl.multiple_of(target * (rows // pieces), 16), rows // pieces) if pieces > 1 else slice(None)
            out[...] = jnp.concatenate([ctx[i, span, :] for i in range(ctx.shape[0])], axis=1).astype(BF)


def attend(position, q_all, km, vm, kv, vv, offset, rows, pieces):
    heads, total, _ = q_all.shape
    masked, visible = km.shape[1], kv.shape[1]
    per_head = lambda size: pl.BlockSpec((1, size, LANES), lambda h: (h, 0, 0))
    shape = (rows // pieces, heads * HD)
    block = min(KEY_BLOCK, masked)
    return pl.pallas_call(
        functools.partial(attend_kernel, offset, rows, pieces),
        grid=(heads,),
        in_specs=[SMEM, per_head(total), per_head(masked), per_head(masked), per_head(visible), per_head(visible)],
        out_specs=[pl.BlockSpec(shape, lambda h: (0, 0))] * pieces,
        out_shape=[jax.ShapeDtypeStruct(shape, BF)] * pieces,
        scratch_shapes=[
            pltpu.VMEM((rows, LANES), BF),
            pltpu.VMEM((rows, LANES), F32),
            pltpu.VMEM((heads, rows, HD), F32),
            pltpu.VMEM((rows, block), BF),
            pltpu.VMEM((rows, block), BF),
        ],
        compiler_params=vmem_limit(34),
        cost_estimate=pl.CostEstimate(
            flops=8 * heads * rows * (masked + visible) * LANES,
            bytes_accessed=4 * heads * masked * LANES,
            transcendentals=heads * rows * masked,
        ),
        name="attend",
    )(position, q_all, km, vm, kv, vv)


def gelu(x):
    size = jnp.abs(x)
    base = 1.0 + 0.2316419 * size
    t = pl.reciprocal(base, approx=True)
    t = t * (2.0 - base * t)
    poly = 0.5307027145
    for c in (-0.7265760135, 0.7107068705, -0.142248368, 0.127414796):
        poly = poly * t + c
    tail = (size * t) * poly * jnp.exp2(size * size * (-0.5 * math.log2(math.e)))
    return jnp.maximum(x, 0.0) - tail


def mlp_kernel(pieces, row_pieces, layout, first_row, spread, position, *refs):
    ctx_refs, refs = refs[:pieces], refs[pieces:]
    row_refs, refs = refs[:row_pieces], refs[row_pieces:]
    own_ref, idr_ref, table_ref, small_ref = refs[:4]
    sources, (res_ref, ups, downs, outs, acc, mlp_in, sems) = refs[4:-7], refs[-7:]
    weights = [sources[k].at[j] for k, j in layout]
    step = pl.program_id(0)
    share = acc.shape[0]
    half = weights[0].shape[1]
    up = ups.shape[2]
    tail = up + downs.shape[1]
    swap = lambda a: jnp.where(position[0] == 0, a, jnp.concatenate([a[:, half:], a[:, :half]], axis=1))

    def out_copy(i):
        side = slice(i % 2 * half, (i % 2 + 1) * half)
        return pltpu.make_async_copy(weights[i].at[tail:], outs.at[i // 2, :, side], sems.at[i, 0])

    def copies(i):
        side = slice(i % 2 * half, (i % 2 + 1) * half)
        moves = [
            pltpu.make_async_copy(
                weights[i].at[k * half : (k + 1) * half],
                ups.at[i // 2, side, k * half : (k + 1) * half],
                sems.at[i, 1 + k],
            )
            for k in range(up // half)
        ]
        last = sems.at[i, 1 + up // half]
        return moves + [pltpu.make_async_copy(weights[i].at[up:tail], downs.at[i // 2, :, side], last)]

    @pl.when(step == 0)
    def _():
        for i in range(2 * pieces):
            out_copy(i).start()
        for i in range(2 * pieces):
            for copy in copies(i):
                copy.start()
        if share == own_ref.shape[0]:
            ids = own_ref[...]
        elif spread:
            ids = own_ref[pl.ds(pl.multiple_of(first_row + position[1] * share, 16), share), :]
        else:
            ids = own_ref[first_row : first_row + share, :]
        hot = place_hot(ids, table_ref.shape[0])
        place = sum(dot32(hot, part) for part in split2(table_ref[...]))
        match = jnp.where(ids == idr_ref[...], 1.0, 0.0)
        shown = jnp.max(match, axis=1, keepdims=True) > 0.5
        rows = jnp.concatenate([ref[...] for ref in row_refs], axis=0)
        stream = jnp.where(shown, dot32(match.astype(BF), rows), small_ref[1:2, :].astype(F32)) + place
        acc[...] = swap(stream)
        for i in range(pieces):
            out_copy(2 * i).wait()
            out_copy(2 * i + 1).wait()
            acc[...] += dot32(ctx_refs[i][...], outs[i])
        mlp_in[...] = layer_norm(acc[...], swap(small_ref[2:3, :].astype(F32))).astype(BF)

    for i in range(pieces):

        @pl.when(step == i)
        def _(i=i):
            for copy in copies(2 * i) + copies(2 * i + 1):
                copy.wait()

    wide = 256 if up % 256 == 0 else up
    blocks = [slice(k, k + wide) for k in range(0, up, wide)]
    pres = [dot32(mlp_in[...], ups[step, :, span]) for span in blocks]
    added = 0.0
    for pre, span in zip(pres, blocks):
        added += dot32(gelu(pre).astype(BF), downs[step, span, :])
    acc[...] += added

    @pl.when(step == pieces - 1)
    def _():
        if res_ref.shape[0] == share:
            res_ref[...] = swap(acc[...]).astype(res_ref.dtype)
        else:
            acc[...] = swap(acc[...])
            own = pltpu.make_async_copy(acc, res_ref.at[first_row : first_row + share], sems.at[2 * pieces, 0])
            own.start()
            own.wait()


def mlp(position, contexts, all_rows, own_ids, id_row, table, small, mine, others, units, first_row, spread, total):
    pieces = len(mine)
    weights = [*mine, *others]
    layout = [(k, j) for k, w in enumerate(weights) for j in range(w.shape[0])]
    layout = [layout[i // 2 + i % 2 * pieces] for i in range(2 * pieces)]
    share = contexts[0].shape[0]
    width = table.shape[1]
    ins = [*contexts, *all_rows, own_ids, id_row, table, small]
    out_rows = share if spread else total
    inside = out_rows == share
    return pl.pallas_call(
        functools.partial(mlp_kernel, pieces, len(all_rows), layout, first_row, spread),
        grid=(pieces,),
        in_specs=[SMEM] + [whole(a) for a in ins] + [pl.BlockSpec(memory_space=pl.ANY)] * len(weights),
        out_specs=pl.BlockSpec((share, width), lambda i: (0, 0)) if inside else pl.BlockSpec(memory_space=pl.ANY),
        out_shape=jax.ShapeDtypeStruct((out_rows, width), BF if spread else F32),
        scratch_shapes=[
            pltpu.VMEM((pieces, width, units), BF),
            pltpu.VMEM((pieces, units, width), BF),
            pltpu.VMEM((pieces, contexts[0].shape[1], width), BF),
            pltpu.VMEM((share, width), F32),
            pltpu.VMEM((share, width), BF),
            pltpu.SemaphoreType.DMA((2 * pieces + 1, 2 + units // (width // 2))),
        ],
        compiler_params=vmem_limit(26),
        cost_estimate=pl.CostEstimate(
            flops=30 * share * width * width, bytes_accessed=18 * width * width, transcendentals=4 * share * width
        ),
        name="mlp",
    )(position, *ins, *weights)


def place_kernel(pieces, first_row, position, *refs):
    sources, (_held, out_ref), (sems, *stages) = refs[:pieces], refs[pieces : pieces + 2], refs[pieces + 2 :]

    def move(k):
        count = sources[k].shape[0]
        source = lax.rem(position[1] + (pieces - k), pieces)
        place = pl.ds(pl.multiple_of(first_row + source * count, 16), count)
        return pltpu.make_async_copy(stages[k], out_ref.at[place], sems.at[k])

    for k in range(pieces):
        stages[k][...] = sources[k][...].astype(F32)
        move(k).start()
    for k in range(pieces):
        move(k).wait()


def put_rows(position, decoded, pieces, first_row):
    count = len(pieces)
    return pl.pallas_call(
        functools.partial(place_kernel, count, first_row),
        in_specs=[SMEM] + [pl.BlockSpec(memory_space=pltpu.VMEM)] * count + [pl.BlockSpec(memory_space=pl.ANY)],
        out_specs=pl.BlockSpec(memory_space=pl.ANY),
        out_shape=jax.ShapeDtypeStruct(decoded.shape, decoded.dtype),
        scratch_shapes=[pltpu.SemaphoreType.DMA((count,))] + [pltpu.VMEM(p.shape, F32) for p in pieces],
        input_output_aliases={count + 1: 0},
        compiler_params=vmem_limit(16),
        name="put_rows",
    )(position, *pieces, decoded)


def shards(
    enc_rows,
    vis_index,
    owner_of,
    enc_gain,
    embed_weight,
    mask_token,
    attn_gain,
    qkv_weight,
    out_weight,
    mlp_gain,
    up_weight,
    down_weight,
):
    section = lax.axis_index("section")
    mp_size = lax.axis_size("mp")
    position = jnp.stack([section, lax.axis_index("mp"), lax.axis_index("seq")]).astype(I32)
    patch_total = owner_of.shape[0]
    own_rows = patch_total // lax.axis_size("seq")
    features = mask_token.shape[0]
    half = features // 2
    width = qkv_weight.shape[2]
    heads = width // HD
    slabs = patch_total // CUBE
    places = CUBE + slabs
    vmem = lambda shape, kind: jax.ShapeDtypeStruct(shape, kind)

    embed_other = shifted(embed_weight, "section", 1)
    qkv_mine = qkv_weight.reshape(half, 3 * width)
    qkv_other = shifted(qkv_mine, "section", 1)
    all_ids = gather_pieces(vis_index, "seq")
    embedded = pl.pallas_call(
        embed_kernel,
        in_specs=[SMEM] + [pl.BlockSpec(memory_space=pltpu.VMEM)] * 4,
        out_specs=pl.BlockSpec(memory_space=pltpu.VMEM),
        out_shape=vmem((enc_rows.shape[1], features), BF),
        compiler_params=vmem_limit(12),
        name="embed",
    )(position, enc_rows[0], enc_gain[None, :], embed_weight, embed_other)
    embedded, *all_ids = lax.optimization_barrier((embedded, *all_ids))
    all_rows = gather_pieces(embedded, "seq")
    id_row = jnp.concatenate([a.reshape(1, -1) for a in all_ids], axis=1)
    visible = id_row.shape[1]

    table = jnp.asarray(place_table(slabs, features))
    small = jnp.stack([attn_gain, mask_token, mlp_gain])
    groups = 3 * heads
    qkv_wide, proj, means, squares = pl.pallas_call(
        functools.partial(table_kernel, groups),
        in_specs=[SMEM] + [pl.BlockSpec(memory_space=pltpu.VMEM)] * 4,
        out_specs=[pl.BlockSpec(memory_space=pltpu.VMEM)] * 4,
        out_shape=[
            vmem((features, groups * LANES), BF),
            vmem((places, groups * LANES), F32),
            vmem((places, LANES), F32),
            vmem((places, LANES), F32),
        ],
        compiler_params=vmem_limit(16),
        name="tables",
    )(position, table, small, qkv_mine, qkv_other)

    blocks = 4 if slabs % 4 == 0 and patch_total % 64 == 0 else 1
    slab_rows = patch_total // blocks
    ins = [proj, means, squares, id_row]
    key_spec = pl.BlockSpec((heads, slab_rows, LANES), lambda i: (0, i, 0))
    km, vm, top = pl.pallas_call(
        functools.partial(masked_kernel, heads),
        grid=(blocks,),
        in_specs=[whole(a) for a in ins],
        out_specs=[key_spec, key_spec, pl.BlockSpec((24, LANES), lambda i: (0, 0))],
        out_shape=[vmem((heads, patch_total, LANES), BF)] * 2 + [vmem((24, LANES), F32)],
        scratch_shapes=[pltpu.VMEM((CUBE, LANES), BF)],
        compiler_params=vmem_limit(20),
        name="masked",
    )(*ins)

    group = HD
    own_ids = pl.pallas_call(
        owned_kernel,
        in_specs=[SMEM, pl.BlockSpec(memory_space=pltpu.VMEM)],
        out_specs=pl.BlockSpec(memory_space=pltpu.VMEM),
        out_shape=vmem((own_rows, 1), I32),
        compiler_params=vmem_limit(12),
        name="owned",
    )(position, owner_of.reshape(patch_total // group, group))

    row_block = 720 if own_rows % 720 == 0 else own_rows
    spaced = visible + (-visible % KEY_PAD)
    ins = [*all_rows, id_row, own_ids, table, small, qkv_wide, proj, means, squares, top]
    specs = [whole(a) for a in ins]
    specs[len(all_rows) + 1] = pl.BlockSpec((row_block, 1), lambda i: (jnp.maximum(i - 1, 0), 0))
    kv, vv, q_all = pl.pallas_call(
        functools.partial(queries_kernel, heads, len(all_rows)),
        grid=(1 + own_rows // row_block,),
        in_specs=specs,
        out_specs=[pl.BlockSpec((heads, spaced, LANES), lambda i: (0, 0, 0))] * 2
        + [pl.BlockSpec((heads, row_block, LANES), lambda i: (0, jnp.maximum(i - 1, 0), 0))],
        out_shape=[vmem((heads, spaced, LANES), BF)] * 2 + [vmem((heads, own_rows, LANES), BF)],
        scratch_shapes=[
            pltpu.VMEM((visible, heads * LANES), BF),
            pltpu.VMEM((8 * (-(-(heads + 2) // 8)), LANES), F32),
            pltpu.VMEM((2, places, (heads + 2) * LANES), BF),
        ],
        compiler_params=vmem_limit(22),
        name="queries",
    )(*ins)

    units = up_weight.shape[1]
    packed = jnp.concatenate(
        [up_weight[:, i : i + half] for i in range(0, units, half)] + [down_weight, out_weight], axis=0
    )
    packed, _unused = lax.optimization_barrier((packed, embedded))
    packed_other = shifted(packed, "section", 1)
    mine = shift_pieces(packed, "mp")

    big = 1472 if own_rows >= 2048 and mp_size > 1 else 0
    rest = own_rows - big

    q_all, packed_other = lax.optimization_barrier((q_all, packed_other))

    def pair_weights(after):
        pieces = mine
        if after is not None:
            *pieces, _unused = lax.optimization_barrier((*mine, after))
        others = [packed_other[None]]
        for i in range(1, len(pieces), 2):
            others.append(shifted(jnp.stack(pieces[i : i + 2]), "section", 1))
        return [p[None] for p in pieces], others

    def finish(weights, contexts, first_row, spread):
        return mlp(position, contexts, all_rows, own_ids, id_row, table, small, *weights, units, first_row, spread, own_rows)

    if not big:
        (context,) = attend(position, q_all, km, vm, kv, vv, 0, rest, 1)
        return finish(pair_weights(None), shift_pieces(context, "mp"), 0, False)[None]
    parts = attend(position, q_all, km, vm, kv, vv, 0, big, mp_size)
    weights = pair_weights(parts[0])
    exchanged = [part if step == 0 else shifted(part, "mp", step) for step, part in enumerate(parts)]
    (context,) = attend(position, q_all, km, vm, kv, vv, big, rest, 1)
    last = shift_pieces(context, "mp")
    *exchanged, _unused = lax.optimization_barrier((*exchanged, context))
    done = finish(weights, exchanged, 0, True)
    *last, done = lax.optimization_barrier((*last, done))
    pieces = shift_pieces(done, "mp")
    decoded = finish(weights, last, big, False)
    return put_rows(position, decoded, pieces, 0)[None]


def solution(mesh):
    in_specs = (
        P("section", "seq", None),
        P("section", "seq"),
        P(),
        P(),
        P("section", None),
        P(),
        P(),
        P("section", None, "mp"),
        P("mp", "section"),
        P(),
        P("section", "mp"),
        P("mp", "section"),
    )
    out_specs = P("section", "seq", None)
    return jax.shard_map(shards, mesh=mesh, in_specs=in_specs, out_specs=out_specs, check_vma=False)
```

```python
import functools
import math

import jax
import jax.numpy as jnp
import numpy as np
from jax import lax
from jax.experimental import pallas as pl
from jax.experimental.pallas import tpu as pltpu
from jax.sharding import PartitionSpec as P

GX = 6
HD = 64
LANES = 128
KEY_BLOCK = 2048
KEY_PAD = 256
OFF_BIAS = -1e30
HEADROOM = 88.0
WINDOW = 180.0
CUBE = GX * GX * GX
HIGH = lax.Precision.HIGHEST
BF = jnp.bfloat16
F32 = jnp.float32
I32 = jnp.int32
MIB = 1024 * 1024
LOG_SCALE = math.log2(math.e) * HD ** (-0.5)
NT = (((1,), (1,)), ((), ()))


def vmem_limit(mib):
    return pltpu.CompilerParams(vmem_limit_bytes=mib * MIB)


def layer_norm(values, scales):
    centred = values - jnp.mean(values, axis=-1, keepdims=True)
    spread = jnp.mean(centred * centred, axis=-1, keepdims=True)
    return centred * lax.rsqrt(spread + 1e-06) * scales


def dot32(a, b):
    return jnp.dot(a, b, preferred_element_type=F32)


def split3(values):
    high = values.astype(BF)
    rest = values - high.astype(F32)
    mid = rest.astype(BF)
    return high, mid, (rest - mid.astype(F32)).astype(BF)


def split2(values):
    high = values.astype(BF)
    return high, (values - high.astype(F32)).astype(BF)


def shifted(values, axis, step):
    size = lax.axis_size(axis)
    return lax.ppermute(values, axis, [(i, (i + step) % size) for i in range(size)])


def shift_pieces(values, axis):
    return [values] + [shifted(values, axis, step) for step in range(1, lax.axis_size(axis))]


def gather_pieces(values, axis):
    if lax.axis_size(axis) > 4:
        return [lax.all_gather(values, axis, axis=0, tiled=True)]
    return shift_pieces(values, axis)


def whole(array):
    return pl.BlockSpec(array.shape, lambda *_: (0,) * array.ndim)


SMEM = pl.BlockSpec(memory_space=pltpu.SMEM)


def place_table(slabs, features):
    quarter = features // 4
    frequency = (1.0 / 10000.0 ** (np.arange(quarter // 2, dtype=np.float32) / (quarter // 2))).astype(np.float32)
    angles = np.arange(max(slabs, GX), dtype=np.float32)[:, None] * frequency[None, :]
    codes = np.concatenate([np.sin(angles), np.cos(angles)], axis=1).astype(np.float32)
    place = np.arange(CUBE)
    cube = np.concatenate(
        [codes[place % GX], codes[place // GX % GX], codes[place // (GX * GX)], np.zeros((CUBE, quarter), np.float32)],
        axis=1,
    )
    slab = np.concatenate([np.zeros((slabs, 3 * quarter), np.float32), codes[:slabs]], axis=1)
    return np.concatenate([cube, slab], axis=0)


def embed_kernel(position, rows_ref, gain_ref, mine_ref, other_ref, out_ref):
    normed = layer_norm(rows_ref[...].astype(F32), gain_ref[...].astype(F32)).astype(BF)
    half = normed.shape[1] // 2
    low, high = normed[:, :half], normed[:, half:]
    first = position[0] == 0

    @pl.when(first)
    def _():
        out_ref[...] = (dot32(low, mine_ref[...]) + dot32(high, other_ref[...])).astype(BF)

    @pl.when(jnp.logical_not(first))
    def _():
        out_ref[...] = (dot32(low, other_ref[...]) + dot32(high, mine_ref[...])).astype(BF)


def table_kernel(
    groups, position, table_ref, small_ref, mine_ref, other_ref, weight_ref, proj_ref, sum_ref, square_ref
):
    features = table_ref.shape[1]
    places = table_ref.shape[0]
    first = position[0] == 0
    mine, other = mine_ref[...], other_ref[...]
    full = jnp.concatenate([jnp.where(first, mine, other), jnp.where(first, other, mine)], axis=0)
    gain = small_ref[0:1, :].astype(F32)
    mask = small_ref[1:2, :].astype(F32)
    mask = mask - jnp.mean(mask, axis=1, keepdims=True)
    table = table_ref[...]
    row = lax.broadcasted_iota(I32, table.shape, 0)
    lane = lax.broadcasted_iota(I32, table.shape, 1)
    rows = table + jnp.where(row < CUBE, mask, 0.0)
    gained = jnp.concatenate([rows * gain, jnp.broadcast_to(gain, (16, features))], axis=0)
    proj = sum(dot32(part, full) for part in split3(gained))
    last = lane >= features - features // 4
    squared = jnp.where(row < CUBE, jnp.where(last, 0.0, rows), jnp.where(last, rows + mask, 0.0))
    total = jnp.sum(rows, axis=1, keepdims=True)
    square = jnp.sum(squared * squared, axis=1, keepdims=True)
    column = lax.broadcasted_iota(I32, (1, groups * HD), 1)
    scale = jnp.where(column < groups * HD // 3, LOG_SCALE, 1.0)
    proj = (proj[:places, :] - (total / features) * proj[places : places + 1, :]) * scale
    for group in range(groups):
        span = slice(group * HD, (group + 1) * HD)
        wide = slice(group * LANES, (group + 1) * LANES)
        weight_ref[:, wide] = jnp.concatenate([full[:, span], jnp.zeros((features, HD), BF)], axis=1)
        proj_ref[:, wide] = jnp.concatenate([proj[:, span], jnp.zeros((places, HD), F32)], axis=1)
    sum_ref[...] = jnp.broadcast_to(total / features, sum_ref.shape)
    square_ref[...] = jnp.broadcast_to(square / features, square_ref.shape)


def top_rows(values):
    return jnp.max(values.reshape(values.shape[0] // 8, 8, LANES), axis=0)


def square_sums(values):
    return dot32((values * values).astype(BF), jnp.ones((LANES, LANES), BF))


def masked_kernel(heads, proj_ref, sum_ref, square_ref, ids_ref, km_ref, vm_ref, top_ref, shown):
    step = pl.program_id(0)
    parts = km_ref.shape[1] // CUBE
    lane = lax.broadcasted_iota(I32, (1, LANES), 1)

    @pl.when(step == 0)
    def _():
        ids = ids_ref[...]
        slab = slab_of(ids)
        inner = ids - slab * CUBE
        rows = lax.broadcasted_iota(I32, (CUBE, ids.shape[1]), 0)
        columns = lax.broadcasted_iota(I32, (LANES, ids.shape[1]), 0)
        by_place = jnp.where(rows == inner, 1.0, 0.0).astype(BF)
        by_slab = jnp.where(columns == slab, 1.0, 0.0).astype(BF)
        shown[...] = lax.dot_general(by_place, by_slab, NT, preferred_element_type=F32).astype(BF)
        largest = lambda x: jnp.max(jnp.max(x, axis=0, keepdims=True), axis=1, keepdims=True)
        norms = lambda x: jnp.sqrt(jnp.max(jnp.sum(x * x, axis=1, keepdims=True), axis=0, keepdims=True))
        key_top = jnp.zeros((1, 1), F32)
        value_top = jnp.zeros((1, 1), F32)
        for head in range(heads):
            wide = slice((heads + head) * LANES, (heads + head + 1) * LANES)
            inner, outer = proj_ref[:CUBE, wide], proj_ref[CUBE:, wide]
            middle = jnp.mean(outer, axis=0, keepdims=True)
            key_top = jnp.maximum(key_top, norms(inner + middle) + norms(outer - middle))
            wide = slice((2 * heads + head) * LANES, (2 * heads + head + 1) * LANES)
            value_top = jnp.maximum(value_top, largest(jnp.abs(proj_ref[:CUBE, wide])) + largest(jnp.abs(proj_ref[CUBE:, wide])))
        top_ref[0:8, :] = jnp.zeros((8, LANES), F32)
        top_ref[8:16, :] = jnp.broadcast_to(key_top, (8, LANES))
        top_ref[16:24, :] = jnp.broadcast_to(value_top, (8, LANES))

    value_extra = jnp.where(lane >= HD, 1.0, 0.0)
    scales = []
    extras = []
    slab_rows = []
    for part in range(parts):
        slab = step * parts + part
        row = CUBE + slab
        slab_rows.append(proj_ref[pl.ds(row, 1), :])
        mean = sum_ref[:CUBE, :] + sum_ref[pl.ds(row, 1), :]
        spread = square_ref[:CUBE, :] + square_ref[pl.ds(row, 1), :] - mean * mean
        scales.append(lax.rsqrt(spread + 1e-06))
        pick = (lax.broadcasted_iota(I32, (LANES, LANES), 0) == slab) & (
            lax.broadcasted_iota(I32, (LANES, LANES), 1) == HD
        )
        key_extra = dot32(shown[...], jnp.where(pick, OFF_BIAS, 0.0).astype(BF))
        extras.append(key_extra + jnp.where((lane > HD) & (lane < HD + 4), 1.0, 0.0))
    for scale in scales:
        top_ref[0:8, :] = jnp.maximum(top_ref[0:8, :], top_rows(scale))
    scale = jnp.concatenate(scales, axis=0)
    key_extra = jnp.concatenate(extras, axis=0)
    for head in range(heads):
        for first, extra, target in ((heads, key_extra, km_ref), (2 * heads, value_extra, vm_ref)):
            wide = slice((first + head) * LANES, (first + head + 1) * LANES)
            block = jnp.concatenate([proj_ref[:CUBE, wide] + row[:, wide] for row in slab_rows], axis=0)
            target[head] = (block * scale + extra).astype(BF)


def owned_kernel(seq_ref, owner_ref, ids_ref):
    groups, size = owner_ref.shape
    rows = ids_ref.shape[0]
    flags = jnp.where(owner_ref[...] == seq_ref[2], 1.0, 0.0).astype(BF)

    def upper(count):
        shape = (count, count)
        return jnp.where(lax.broadcasted_iota(I32, shape, 0) <= lax.broadcasted_iota(I32, shape, 1), 1.0, 0.0).astype(BF)

    local = dot32(flags, upper(size))
    totals = lax.dot_general(jnp.ones((8, size), BF), flags, NT, preferred_element_type=F32)
    ends = dot32(totals.astype(BF), upper(groups))
    begins = (ends - totals)[0:1, :]
    ends = ends[0:1, :]
    slot = lax.broadcasted_iota(I32, (rows, 1), 0).astype(F32)
    group = jnp.sum(jnp.where(ends <= slot, 1.0, 0.0), axis=1, keepdims=True)
    lane = lax.broadcasted_iota(I32, (rows, groups), 1).astype(F32)
    hot = jnp.where(lane == group, 1.0, 0.0)
    begin = jnp.sum(hot * begins, axis=1, keepdims=True)
    counts = dot32(hot.astype(BF), local.astype(BF))
    within = jnp.sum(jnp.where(counts <= slot - begin, 1.0, 0.0), axis=1, keepdims=True)
    ids_ref[...] = (group * size + within).astype(I32)


def slab_of(ids):
    return jnp.floor((ids.astype(F32) + 0.5) * (1.0 / CUBE)).astype(I32)


def place_hot(ids, places):
    lane = lax.broadcasted_iota(I32, (ids.shape[0], places), 1)
    slab = slab_of(ids)
    inner = ids - slab * CUBE
    return jnp.where((lane == inner) | (lane == slab + CUBE), 1.0, 0.0).astype(BF)


def queries_kernel(heads, pieces, *refs):
    queries_body(heads, refs[:pieces], *refs[pieces:])


def queries_body(
    heads, row_refs, idr_ref, own_ref, table_ref, small_ref, weight_ref, proj_ref, sum_ref, square_ref, top_ref,
    kv_ref, vv_ref, q_ref, seen_q, bounds, tables,
):
    step = pl.program_id(0)
    wide = heads * LANES

    @pl.when(step == 0)
    def _():
        count = idr_ref.shape[1]
        square = (count, count)
        here = lax.broadcasted_iota(I32, square, 0) == lax.broadcasted_iota(I32, square, 1)
        ids = jnp.sum(jnp.where(here, idr_ref[...].astype(F32), 0.0), axis=1, keepdims=True)
        rows = jnp.concatenate([ref[...].astype(F32) for ref in row_refs], axis=0)
        hot = place_hot(ids.astype(I32), table_ref.shape[0])
        place = sum(dot32(hot, part) for part in split2(table_ref[...]))
        seen = layer_norm(rows + place, small_ref[0:1, :].astype(F32)).astype(BF)
        seen_q[...] = (dot32(seen, weight_ref[:, :wide]) * LOG_SCALE).astype(BF)
        both = dot32(seen, weight_ref[:, wide:])
        lane = lax.broadcasted_iota(I32, (1, LANES), 1)
        extra = jnp.where((lane > HD) & (lane < HD + 4), 1.0, 0.0)
        ones = jnp.where(lane >= HD, 1.0, 0.0)
        scale = jnp.max(top_ref[0:8, :], axis=0, keepdims=True)
        scale = jnp.max(scale, axis=1, keepdims=True)
        masked_key = scale * top_ref[8:9, :]
        top = jnp.zeros((8, LANES), F32)
        high = scale * top_ref[16:24, :]
        spare = kv_ref.shape[1] - count
        for head in range(heads):
            keys = both[:, head * LANES : (head + 1) * LANES]
            top = jnp.maximum(top, top_rows(square_sums(keys)))
            middle = jnp.mean(keys, axis=0, keepdims=True)
            middle = jnp.sum(middle * middle, axis=1, keepdims=True)
            bounds[head : head + 1, :] = jnp.broadcast_to(jnp.sqrt(middle) * 1.03, (1, LANES))
            kv_ref[head, :count, :] = (keys + extra).astype(BF)
            values = both[:, (heads + head) * LANES : (heads + head + 1) * LANES]
            high = jnp.maximum(high, top_rows(jnp.abs(values)))
            vv_ref[head, :count, :] = (values + ones).astype(BF)
            if spare:
                off = lax.broadcasted_iota(I32, (spare, LANES), 1) == HD
                kv_ref[head, count:, :] = jnp.where(off, OFF_BIAS, 0.0).astype(BF)
                vv_ref[head, count:, :] = jnp.ones((spare, LANES), BF)
        seen_key = jnp.sqrt(jnp.max(top, axis=0, keepdims=True))
        bounds[heads : heads + 1, :] = jnp.maximum(seen_key, masked_key) * 1.03
        largest = jnp.max(jnp.max(high, axis=0, keepdims=True), axis=1, keepdims=True)
        bounds[heads + 1 : heads + 2, :] = jnp.broadcast_to(largest, (1, LANES))
        joined = jnp.concatenate([proj_ref[:, :wide], sum_ref[...], square_ref[...]], axis=1)
        for i, part in enumerate(split2(joined)):
            tables[i] = part

    @pl.when(step > 0)
    def _():
        ids = own_ref[...]
        count = ids.shape[0]
        hot = place_hot(ids, table_ref.shape[0])
        mixed = dot32(hot, tables[0]) + dot32(hot, tables[1])
        mean = mixed[:, wide : wide + LANES]
        scale = lax.rsqrt(mixed[:, wide + LANES :] - mean * mean + 1e-06)
        match = jnp.where(ids == idr_ref[...], 1.0, 0.0)
        shown = jnp.max(match, axis=1, keepdims=True) > 0.5
        picked = dot32(match.astype(BF), seen_q[...])
        lane = lax.broadcasted_iota(I32, (count, LANES), 1)
        limit = bounds[heads : heads + 1, :]
        fine = bounds[heads + 1 : heads + 2, :] < 2.0**25
        for head in range(heads):
            span = slice(head * LANES, (head + 1) * LANES)
            part = jnp.where(shown, picked[:, span], scale * mixed[:, span])
            norm = jnp.sqrt(square_sums(part))
            ceiling = norm * limit
            slack = jnp.where(fine, ceiling + norm * bounds[head : head + 1, :], 1e30)
            extra = jnp.where(lane == HD, 1.0, jnp.where(lane == HD + 1, HEADROOM - ceiling, 0.0))
            extra = jnp.where(lane == HD + 4, slack, extra)
            q_ref[head] = jnp.where(lane < HD, part, extra).astype(BF)


def attend_kernel(offset, rows, pieces, position, q_ref, km_ref, vm_ref, kv_ref, vv_ref, *refs):
    outs, (q_scr, acc, ctx, p_even, p_odd) = refs[:pieces], refs[pieces:]
    head = pl.program_id(0)
    q_scr[...] = q_ref[0, offset : offset + rows, :]
    block = p_even.shape[1]
    steps = km_ref.shape[1] // block
    rest = km_ref.shape[1] - steps * block
    tails = [(km_ref, vm_ref, steps * block, rest)] if rest else []
    visible = kv_ref.shape[1]
    tails += [(kv_ref, vv_ref, i, min(block, visible - i)) for i in range(0, visible, block)]

    def keys_of(i):
        if isinstance(i, int) and i >= steps:
            keys, _, start, size = tails[i - steps]
            return keys[0, start : start + size, :]
        return km_ref[0, pl.ds(i * block, block), :]

    def values_of(i):
        if isinstance(i, int) and i >= steps:
            _, values, start, size = tails[i - steps]
            return values[0, start : start + size, :]
        return vm_ref[0, pl.ds(i * block, block), :]

    def scores(i):
        return lax.dot_general(q_scr[...], keys_of(i), NT, preferred_element_type=F32)

    total = steps + len(tails)
    lane = lax.broadcasted_iota(I32, (rows, LANES), 1)
    slack = jnp.max(jnp.where(lane == HD + 4, q_scr[...].astype(F32), -1e30))

    @pl.when(jnp.logical_not(slack <= WINDOW))
    def _():
        q_scr[...] = jnp.where(lane > HD, 0.0, q_scr[...].astype(F32)).astype(BF)

        def look(i, best):
            return jnp.maximum(best, jnp.max(scores(i), axis=1, keepdims=True))

        peak = lax.fori_loop(0, steps, look, jnp.full((rows, 1), -3e38, F32))
        for i in range(steps, total):
            peak = look(i, peak)
        high, mid, low = split3(peak)
        new = jnp.where(lane == HD + 1, -high.astype(F32), q_scr[...].astype(F32))
        new = jnp.where(lane == HD + 2, -mid.astype(F32), new)
        new = jnp.where(lane == HD + 3, -low.astype(F32), new)
        q_scr[...] = new.astype(BF)

    def width_of(i):
        return tails[i - steps][3] if isinstance(i, int) and i >= steps else block

    def weigh(i, target):
        target[:, : width_of(i)] = jnp.exp2(scores(i)).astype(BF)

    def add(weights, i):
        acc[...] += dot32(weights[:, : width_of(i)], values_of(i))

    acc[...] = jnp.zeros_like(acc)
    slots = (p_even, p_odd)
    weigh(0, p_even)

    def body(j, carry):
        i = 2 * j + 1
        weigh(i, p_odd)
        add(p_even, i - 1)
        weigh(i + 1, p_even)
        add(p_odd, i)
        return carry

    pairs = (steps - 1) // 2
    lax.fori_loop(0, pairs, body, 0)
    for i in range(1 + 2 * pairs, total + 1):
        if i < total:
            weigh(i, slots[i % 2])
        add(slots[1 - i % 2], i - 1)
    totals = acc[...]
    ctx[head] = totals[:, :HD] / totals[:, HD:]

    @pl.when(head == pl.num_programs(0) - 1)
    def _():
        for step, out in enumerate(outs):
            target = lax.rem(position[1] + step, pieces)
            span = pl.ds(pl.multiple_of(target * (rows // pieces), 16), rows // pieces) if pieces > 1 else slice(None)
            out[...] = jnp.concatenate([ctx[i, span, :] for i in range(ctx.shape[0])], axis=1).astype(BF)


def attend(position, q_all, km, vm, kv, vv, offset, rows, pieces):
    heads, total, _ = q_all.shape
    masked, visible = km.shape[1], kv.shape[1]
    per_head = lambda size: pl.BlockSpec((1, size, LANES), lambda h: (h, 0, 0))
    shape = (rows // pieces, heads * HD)
    block = min(KEY_BLOCK, masked)
    return pl.pallas_call(
        functools.partial(attend_kernel, offset, rows, pieces),
        grid=(heads,),
        in_specs=[SMEM, per_head(total), per_head(masked), per_head(masked), per_head(visible), per_head(visible)],
        out_specs=[pl.BlockSpec(shape, lambda h: (0, 0))] * pieces,
        out_shape=[jax.ShapeDtypeStruct(shape, BF)] * pieces,
        scratch_shapes=[
            pltpu.VMEM((rows, LANES), BF),
            pltpu.VMEM((rows, LANES), F32),
            pltpu.VMEM((heads, rows, HD), F32),
            pltpu.VMEM((rows, block), BF),
            pltpu.VMEM((rows, block), BF),
        ],
        compiler_params=vmem_limit(32),
        cost_estimate=pl.CostEstimate(
            flops=8 * heads * rows * (masked + visible) * LANES,
            bytes_accessed=4 * heads * masked * LANES,
            transcendentals=heads * rows * masked,
        ),
        name="attend",
    )(position, q_all, km, vm, kv, vv)


def gelu(x):
    size = jnp.abs(x)
    base = 1.0 + 0.2316419 * size
    t = pl.reciprocal(base, approx=True)
    t = t * (2.0 - base * t)
    poly = 0.5307027145
    for c in (-0.7265760135, 0.7107068705, -0.142248368, 0.127414796):
        poly = poly * t + c
    tail = (size * t) * poly * jnp.exp2(size * size * (-0.5 * math.log2(math.e)))
    return jnp.maximum(x, 0.0) - tail


def mlp_kernel(pieces, row_pieces, layout, first_row, spread, position, *refs):
    ctx_refs, refs = refs[:pieces], refs[pieces:]
    row_refs, refs = refs[:row_pieces], refs[row_pieces:]
    own_ref, idr_ref, table_ref, small_ref = refs[:4]
    sources, (res_ref, ups, downs, outs, acc, mlp_in, sems) = refs[4:-7], refs[-7:]
    weights = [sources[k].at[j] for k, j in layout]
    step = pl.program_id(0)
    share = acc.shape[0]
    half = weights[0].shape[1]
    up = ups.shape[2]
    tail = up + downs.shape[1]
    swap = lambda a: jnp.where(position[0] == 0, a, jnp.concatenate([a[:, half:], a[:, :half]], axis=1))

    def out_copy(i):
        side = slice(i % 2 * half, (i % 2 + 1) * half)
        return pltpu.make_async_copy(weights[i].at[tail:], outs.at[i // 2, :, side], sems.at[i, 0])

    def copies(i):
        side = slice(i % 2 * half, (i % 2 + 1) * half)
        moves = [
            pltpu.make_async_copy(
                weights[i].at[k * half : (k + 1) * half],
                ups.at[i // 2, side, k * half : (k + 1) * half],
                sems.at[i, 1 + k],
            )
            for k in range(up // half)
        ]
        last = sems.at[i, 1 + up // half]
        return moves + [pltpu.make_async_copy(weights[i].at[up:tail], downs.at[i // 2, :, side], last)]

    @pl.when(step == 0)
    def _():
        for i in range(2 * pieces):
            out_copy(i).start()
        for i in range(2 * pieces):
            for copy in copies(i):
                copy.start()
        if share == own_ref.shape[0]:
            ids = own_ref[...]
        elif spread:
            ids = own_ref[pl.ds(pl.multiple_of(first_row + position[1] * share, 16), share), :]
        else:
            ids = own_ref[first_row : first_row + share, :]
        hot = place_hot(ids, table_ref.shape[0])
        place = sum(dot32(hot, part) for part in split2(table_ref[...]))
        match = jnp.where(ids == idr_ref[...], 1.0, 0.0)
        shown = jnp.max(match, axis=1, keepdims=True) > 0.5
        rows = jnp.concatenate([ref[...] for ref in row_refs], axis=0)
        stream = jnp.where(shown, dot32(match.astype(BF), rows), small_ref[1:2, :].astype(F32)) + place
        acc[...] = swap(stream)
        for i in range(pieces):
            out_copy(2 * i).wait()
            out_copy(2 * i + 1).wait()
            acc[...] += dot32(ctx_refs[i][...], outs[i])
        mlp_in[...] = layer_norm(acc[...], swap(small_ref[2:3, :].astype(F32))).astype(BF)

    for i in range(pieces):

        @pl.when(step == i)
        def _(i=i):
            for copy in copies(2 * i) + copies(2 * i + 1):
                copy.wait()

    wide = 256 if up % 256 == 0 else up
    blocks = [slice(k, k + wide) for k in range(0, up, wide)]
    pres = [dot32(mlp_in[...], ups[step, :, span]) for span in blocks]
    added = 0.0
    for pre, span in zip(pres, blocks):
        added += dot32(gelu(pre).astype(BF), downs[step, span, :])
    acc[...] += added

    @pl.when(step == pieces - 1)
    def _():
        if res_ref.shape[0] == share:
            res_ref[...] = swap(acc[...]).astype(res_ref.dtype)
        else:
            acc[...] = swap(acc[...])
            own = pltpu.make_async_copy(acc, res_ref.at[first_row : first_row + share], sems.at[2 * pieces, 0])
            own.start()
            own.wait()


def mlp(position, contexts, all_rows, own_ids, id_row, table, small, mine, others, units, first_row, spread, total):
    pieces = len(mine)
    weights = [*mine, *others]
    layout = [(k, j) for k, w in enumerate(weights) for j in range(w.shape[0])]
    layout = [layout[i // 2 + i % 2 * pieces] for i in range(2 * pieces)]
    share = contexts[0].shape[0]
    width = table.shape[1]
    ins = [*contexts, *all_rows, own_ids, id_row, table, small]
    out_rows = share if spread else total
    inside = out_rows == share
    return pl.pallas_call(
        functools.partial(mlp_kernel, pieces, len(all_rows), layout, first_row, spread),
        grid=(pieces,),
        in_specs=[SMEM] + [whole(a) for a in ins] + [pl.BlockSpec(memory_space=pl.ANY)] * len(weights),
        out_specs=pl.BlockSpec((share, width), lambda i: (0, 0)) if inside else pl.BlockSpec(memory_space=pl.ANY),
        out_shape=jax.ShapeDtypeStruct((out_rows, width), BF if spread else F32),
        scratch_shapes=[
            pltpu.VMEM((pieces, width, units), BF),
            pltpu.VMEM((pieces, units, width), BF),
            pltpu.VMEM((pieces, contexts[0].shape[1], width), BF),
            pltpu.VMEM((share, width), F32),
            pltpu.VMEM((share, width), BF),
            pltpu.SemaphoreType.DMA((2 * pieces + 1, 2 + units // (width // 2))),
        ],
        compiler_params=vmem_limit(24),
        cost_estimate=pl.CostEstimate(
            flops=30 * share * width * width, bytes_accessed=18 * width * width, transcendentals=4 * share * width
        ),
        name="mlp",
    )(position, *ins, *weights)


def place_kernel(pieces, first_row, position, *refs):
    sources, (_held, out_ref), (sems, *stages) = refs[:pieces], refs[pieces : pieces + 2], refs[pieces + 2 :]

    def move(k):
        count = sources[k].shape[0]
        source = lax.rem(position[1] + (pieces - k), pieces)
        place = pl.ds(pl.multiple_of(first_row + source * count, 16), count)
        return pltpu.make_async_copy(stages[k], out_ref.at[place], sems.at[k])

    for k in range(pieces):
        stages[k][...] = sources[k][...].astype(F32)
        move(k).start()
    for k in range(pieces):
        move(k).wait()


def put_rows(position, decoded, pieces, first_row):
    count = len(pieces)
    return pl.pallas_call(
        functools.partial(place_kernel, count, first_row),
        in_specs=[SMEM] + [pl.BlockSpec(memory_space=pltpu.VMEM)] * count + [pl.BlockSpec(memory_space=pl.ANY)],
        out_specs=pl.BlockSpec(memory_space=pl.ANY),
        out_shape=jax.ShapeDtypeStruct(decoded.shape, decoded.dtype),
        scratch_shapes=[pltpu.SemaphoreType.DMA((count,))] + [pltpu.VMEM(p.shape, F32) for p in pieces],
        input_output_aliases={count + 1: 0},
        compiler_params=vmem_limit(16),
        name="put_rows",
    )(position, *pieces, decoded)


def shards(
    enc_rows,
    vis_index,
    owner_of,
    enc_gain,
    embed_weight,
    mask_token,
    attn_gain,
    qkv_weight,
    out_weight,
    mlp_gain,
    up_weight,
    down_weight,
):
    section = lax.axis_index("section")
    mp_size = lax.axis_size("mp")
    position = jnp.stack([section, lax.axis_index("mp"), lax.axis_index("seq")]).astype(I32)
    patch_total = owner_of.shape[0]
    own_rows = patch_total // lax.axis_size("seq")
    features = mask_token.shape[0]
    half = features // 2
    width = qkv_weight.shape[2]
    heads = width // HD
    slabs = patch_total // CUBE
    places = CUBE + slabs
    vmem = lambda shape, kind: jax.ShapeDtypeStruct(shape, kind)

    embed_other = shifted(embed_weight, "section", 1)
    qkv_mine = qkv_weight.reshape(half, 3 * width)
    qkv_other = shifted(qkv_mine, "section", 1)
    all_ids = gather_pieces(vis_index, "seq")
    embedded = pl.pallas_call(
        embed_kernel,
        in_specs=[SMEM] + [pl.BlockSpec(memory_space=pltpu.VMEM)] * 4,
        out_specs=pl.BlockSpec(memory_space=pltpu.VMEM),
        out_shape=vmem((enc_rows.shape[1], features), BF),
        compiler_params=vmem_limit(12),
        name="embed",
    )(position, enc_rows[0], enc_gain[None, :], embed_weight, embed_other)
    embedded, *all_ids = lax.optimization_barrier((embedded, *all_ids))
    all_rows = gather_pieces(embedded, "seq")
    id_row = jnp.concatenate([a.reshape(1, -1) for a in all_ids], axis=1)
    visible = id_row.shape[1]

    table = jnp.asarray(place_table(slabs, features))
    small = jnp.stack([attn_gain, mask_token, mlp_gain])
    groups = 3 * heads
    qkv_wide, proj, means, squares = pl.pallas_call(
        functools.partial(table_kernel, groups),
        in_specs=[SMEM] + [pl.BlockSpec(memory_space=pltpu.VMEM)] * 4,
        out_specs=[pl.BlockSpec(memory_space=pltpu.VMEM)] * 4,
        out_shape=[
            vmem((features, groups * LANES), BF),
            vmem((places, groups * LANES), F32),
            vmem((places, LANES), F32),
            vmem((places, LANES), F32),
        ],
        compiler_params=vmem_limit(16),
        name="tables",
    )(position, table, small, qkv_mine, qkv_other)

    blocks = 4 if slabs % 4 == 0 and patch_total % 64 == 0 else 1
    slab_rows = patch_total // blocks
    ins = [proj, means, squares, id_row]
    key_spec = pl.BlockSpec((heads, slab_rows, LANES), lambda i: (0, i, 0))
    km, vm, top = pl.pallas_call(
        functools.partial(masked_kernel, heads),
        grid=(blocks,),
        in_specs=[whole(a) for a in ins],
        out_specs=[key_spec, key_spec, pl.BlockSpec((24, LANES), lambda i: (0, 0))],
        out_shape=[vmem((heads, patch_total, LANES), BF)] * 2 + [vmem((24, LANES), F32)],
        scratch_shapes=[pltpu.VMEM((CUBE, LANES), BF)],
        compiler_params=vmem_limit(18),
        name="masked",
    )(*ins)

    group = HD
    own_ids = pl.pallas_call(
        owned_kernel,
        in_specs=[SMEM, pl.BlockSpec(memory_space=pltpu.VMEM)],
        out_specs=pl.BlockSpec(memory_space=pltpu.VMEM),
        out_shape=vmem((own_rows, 1), I32),
        compiler_params=vmem_limit(12),
        name="owned",
    )(position, owner_of.reshape(patch_total // group, group))

    row_block = 720 if own_rows % 720 == 0 else own_rows
    spaced = visible + (-visible % KEY_PAD)
    ins = [*all_rows, id_row, own_ids, table, small, qkv_wide, proj, means, squares, top]
    specs = [whole(a) for a in ins]
    specs[len(all_rows) + 1] = pl.BlockSpec((row_block, 1), lambda i: (jnp.maximum(i - 1, 0), 0))
    kv, vv, q_all = pl.pallas_call(
        functools.partial(queries_kernel, heads, len(all_rows)),
        grid=(1 + own_rows // row_block,),
        in_specs=specs,
        out_specs=[pl.BlockSpec((heads, spaced, LANES), lambda i: (0, 0, 0))] * 2
        + [pl.BlockSpec((heads, row_block, LANES), lambda i: (0, jnp.maximum(i - 1, 0), 0))],
        out_shape=[vmem((heads, spaced, LANES), BF)] * 2 + [vmem((heads, own_rows, LANES), BF)],
        scratch_shapes=[
            pltpu.VMEM((visible, heads * LANES), BF),
            pltpu.VMEM((8 * (-(-(heads + 2) // 8)), LANES), F32),
            pltpu.VMEM((2, places, (heads + 2) * LANES), BF),
        ],
        compiler_params=vmem_limit(18),
        name="queries",
    )(*ins)

    units = up_weight.shape[1]
    packed = jnp.concatenate(
        [up_weight[:, i : i + half] for i in range(0, units, half)] + [down_weight, out_weight], axis=0
    )
    packed, _unused = lax.optimization_barrier((packed, embedded))
    packed_other = shifted(packed, "section", 1)
    mine = shift_pieces(packed, "mp")

    big = 1472 if own_rows >= 2048 and mp_size > 1 else 0
    rest = own_rows - big

    q_all, packed_other = lax.optimization_barrier((q_all, packed_other))

    def pair_weights(after):
        pieces = mine
        if after is not None:
            *pieces, _unused = lax.optimization_barrier((*mine, after))
        others = [packed_other[None]]
        for i in range(1, len(pieces), 2):
            others.append(shifted(jnp.stack(pieces[i : i + 2]), "section", 1))
        return [p[None] for p in pieces], others

    def finish(weights, contexts, first_row, spread):
        return mlp(position, contexts, all_rows, own_ids, id_row, table, small, *weights, units, first_row, spread, own_rows)

    if not big:
        (context,) = attend(position, q_all, km, vm, kv, vv, 0, rest, 1)
        return finish(pair_weights(None), shift_pieces(context, "mp"), 0, False)[None]
    parts = attend(position, q_all, km, vm, kv, vv, 0, big, mp_size)
    weights = pair_weights(parts[0])
    exchanged = [part if step == 0 else shifted(part, "mp", step) for step, part in enumerate(parts)]
    (context,) = attend(position, q_all, km, vm, kv, vv, big, rest, 1)
    last = shift_pieces(context, "mp")
    *exchanged, _unused = lax.optimization_barrier((*exchanged, context))
    done = finish(weights, exchanged, 0, True)
    *last, done = lax.optimization_barrier((*last, done))
    pieces = shift_pieces(done, "mp")
    decoded = finish(weights, last, big, False)
    return put_rows(position, decoded, pieces, 0)[None]


def solution(mesh):
    in_specs = (
        P("section", "seq", None),
        P("section", "seq"),
        P(),
        P(),
        P("section", None),
        P(),
        P(),
        P("section", None, "mp"),
        P("mp", "section"),
        P(),
        P("section", "mp"),
        P("mp", "section"),
    )
    out_specs = P("section", "seq", None)
    return jax.shard_map(shards, mesh=mesh, in_specs=in_specs, out_specs=out_specs, check_vma=False)
```
